32 devices in a mesh: ctx: 16 (over z, y, x), wt: 2 (over core).
Axes of the slice: x: 2, y: 2, z: 4, core: 2. Of those that a mesh axis runs over, the one named last changes fastest.
Arguments:
- tokens: bfloat16 [2, 4096, 1024], P('wt', 'ctx'), may hold values from -6 to 6
- block_table: int32 [16, 2], P('ctx'), may hold values from 0 to 31, as said below
- doc_flags: int32 [2, 4096], P('wt', 'ctx'), may hold values from 0 to 1, as said below
- w_query: float32 [1024, 1024], P(('ctx', 'wt')), may hold values from -0.1875 to 0.1875
- key_weight: float32 [1024, 512], P(('ctx', 'wt')), may hold values from -0.1875 to 0.1875
- value_weight: float32 [1024, 512], P(('ctx', 'wt')), may hold values from -0.1875 to 0.1875
- w_out: float32 [1024, 1024], P(('ctx', 'wt')), may hold values from -2 to 2
- w_gate: float32 [1024, 4608], P(('ctx', 'wt')), may hold values from -0.1875 to 0.1875
- w_up: float32 [1024, 4608], P(('ctx', 'wt')), may hold values from -0.1875 to 0.1875
- w_down: float32 [1024, 4608], P(('ctx', 'wt')), may hold values from -0.09375 to 0.09375
- gain_attn: float32 [1024], P(('ctx', 'wt')), may hold values from 0.25 to 1.75
- gain_mlp: float32 [1024], P(('ctx', 'wt')), may hold values from 0.25 to 1.75
- gain_q: float32 [64], replicated, may hold values from 0.25 to 1.75
- key_norm_gain: float32 [64], replicated, may hold values from 0.25 to 1.75
- cotangent: bfloat16 [2, 4096, 1024], P('wt', 'ctx'), may hold values from -6 to 6
Outputs:
- layer_out: bfloat16 [2, 4096, 1024], P('wt', 'ctx')
- grad_input: float32 [2, 4096, 1024], P('wt', 'ctx')
- grad_query: float32 [1024, 1024], P(('ctx', 'wt'))
- grad_key: float32 [1024, 512], P(('ctx', 'wt'))
- grad_value: float32 [1024, 512], P(('ctx', 'wt'))
- grad_wout: float32 [1024, 1024], P(('ctx', 'wt'))
- grad_gate: float32 [1024, 4608], P(('ctx', 'wt'))
- grad_up: float32 [1024, 4608], P(('ctx', 'wt'))
- grad_down: float32 [1024, 4608], P(('ctx', 'wt'))
- grad_gattn: float32 [1024], P(('ctx', 'wt'))
- grad_gmlp: float32 [1024], P(('ctx', 'wt'))
- grad_gq: float32 [64], replicated
- grad_gk: float32 [64], replicated
The draws below stay inside these ranges and needn't reach their ends.
Inputs may be any that keep to these rules, and one draw needn't show every extreme that they name: `block_table`: row c names the two blocks held at index c of ctx: a block p under 16, then 2 * 16 - 1 - p; every block of a sequence appears once; block b covers positions b * 128 to (b + 1) * 128 - 1. `doc_flags`: rows in the same order as tokens; the token at position 0 of each sequence always begins a document.
All inputs are finite; a program needn't handle non-finite values.
Results may differ from the reference program's by a relative error of at most 0.04.
Values may be sent and summed in bfloat16 or wider, within the bound.
No kernel may reach another device: no remote copies, remote signals or barrier semaphores. Data moves between devices by JAX's collectives and lax.ppermute only.
A program may use at most 320 MiB of HBM per device.

```python
import jax
import jax.numpy as jnp
from jax import lax

MODEL_WIDTH = 1024
QUERY_HEADS = 16
KEY_VALUE_HEADS = 8
HEAD_SIZE = 64
FF = 4608
TOK_DEV = 256
DOCMEAN = 2048
STREAMS = 2
PAIRS = 16
BLOCK = 128
SEQUENCE_TOKENS = 4096


def deal_layout(key):
    key = jax.random.fold_in(key, 11)
    key_start, key_rest, key_trio = jax.random.split(key, 3)
    start_pair = jax.random.randint(key_start, (), 0, PAIRS - 2)
    rest_pairs = jax.random.permutation(key_rest, PAIRS - 3)
    rest_pairs = jnp.where(rest_pairs >= start_pair, rest_pairs + 3, rest_pairs)
    trio_pairs = start_pair + jax.random.permutation(key_trio, 3)
    middle = PAIRS // 2
    lower_blocks = jnp.concatenate([trio_pairs[0:1], rest_pairs[:middle - 1], trio_pairs[1:2], rest_pairs[middle - 1:], trio_pairs[2:3]])
    pair_table = jnp.stack([lower_blocks, 2 * PAIRS - 1 - lower_blocks], axis=1).astype(jnp.int32)
    return (pair_table, start_pair)


def draw_block_table(key, part):
    pair_table, start_pair = deal_layout(key)
    return pair_table


def draw_doc_flags(key, part):
    pair_table, start_pair = deal_layout(key)
    key = jax.random.fold_in(key, 29)
    rolls = jax.random.randint(key, (STREAMS, SEQUENCE_TOKENS), 0, DOCMEAN)
    seq_pos = jnp.arange(SEQUENCE_TOKENS)
    inside = (seq_pos > start_pair * BLOCK) & (seq_pos < (start_pair + 3) * BLOCK)
    edges = (seq_pos == 0) | (seq_pos == start_pair * BLOCK) | (seq_pos == (start_pair + 3) * BLOCK)
    starts = jnp.where(edges[None, :], 1, jnp.where(inside[None, :], 0, (rolls == 0).astype(jnp.int32)))
    row_pos = (pair_table.reshape(-1)[:, None] * BLOCK + jnp.arange(BLOCK)[None, :]).reshape(-1)
    return starts[:, row_pos].astype(jnp.int32)


def block_scale(rng, dims, cuts, smallest, high):
    gain, own = 1.0, jax.random.fold_in(rng, 6)
    for dim, parts in cuts:
        draws = jnp.exp(jax.random.uniform(jax.random.fold_in(own, dim), (parts,), jnp.float32, smallest / len(cuts), high / len(cuts)))
        gain = gain * jnp.repeat(draws, dims[dim] // parts).reshape([-1 if axis == dim else 1 for axis in range(len(dims))])
    return gain


def gaussian(stream_key, extent, spread, bound, pieces=(), kind=jnp.bfloat16):
    loudness = block_scale(stream_key, extent, pieces, -0.22, 0.18) if pieces else 1.0
    entries = jax.random.normal(stream_key, extent, jnp.float32) * spread * loudness
    return jnp.minimum(jnp.maximum(entries, -bound), bound).astype(kind)


def setup_inputs(seed: int = 0) -> dict:
    keys = jax.random.split(jax.random.key(seed), 16)
    return {
        "tokens": gaussian(keys[0], (STREAMS, SEQUENCE_TOKENS, MODEL_WIDTH), 1.0, 6.0, ((0, 2), (1, 16))),
        "block_table": draw_block_table(jax.random.fold_in(keys[15], 71), 0),
        "doc_flags": draw_doc_flags(jax.random.fold_in(keys[15], 71), 0),
        "w_query": gaussian(keys[3], (MODEL_WIDTH, QUERY_HEADS * HEAD_SIZE), MODEL_WIDTH ** -0.5, 0.1875, ((0, 32),), jnp.float32),
        "key_weight": gaussian(keys[4], (MODEL_WIDTH, KEY_VALUE_HEADS * HEAD_SIZE), MODEL_WIDTH ** -0.5, 0.1875, ((0, 32),), jnp.float32),
        "value_weight": gaussian(keys[5], (MODEL_WIDTH, KEY_VALUE_HEADS * HEAD_SIZE), MODEL_WIDTH ** -0.5, 0.1875, ((0, 32),), jnp.float32),
        "w_out": gaussian(keys[6], (QUERY_HEADS * HEAD_SIZE, MODEL_WIDTH), (max(QUERY_HEADS * HEAD_SIZE // 128, 8)) ** -0.5, 2.0, ((0, 32),), jnp.float32),
        "w_gate": gaussian(keys[7], (MODEL_WIDTH, FF), MODEL_WIDTH ** -0.5, 0.1875, ((0, 32),), jnp.float32),
        "w_up": gaussian(keys[8], (MODEL_WIDTH, FF), MODEL_WIDTH ** -0.5, 0.1875, ((0, 32),), jnp.float32),
        "w_down": gaussian(keys[9], (MODEL_WIDTH, FF), FF ** -0.5, 0.09375, ((0, 32),), jnp.float32),
        "gain_attn": jnp.clip(1.0 + 0.15 * jax.random.normal(keys[10], (MODEL_WIDTH,), jnp.float32), 0.25, 1.75),
        "gain_mlp": jnp.clip(1.0 + 0.15 * jax.random.normal(keys[11], (MODEL_WIDTH,), jnp.float32), 0.25, 1.75),
        "gain_q": jnp.clip(1.0 + 0.15 * jax.random.normal(keys[12], (HEAD_SIZE,), jnp.float32), 0.25, 1.75),
        "key_norm_gain": jnp.clip(1.0 + 0.15 * jax.random.normal(keys[13], (HEAD_SIZE,), jnp.float32), 0.25, 1.75),
        "cotangent": gaussian(keys[14], (STREAMS, SEQUENCE_TOKENS, MODEL_WIDTH), 1.0, 6.0, ((0, 2), (1, 16))),
    }


@jax.custom_vjp
def lower_precision(v):
    return lax.optimization_barrier(v.astype(jnp.bfloat16)).astype(jnp.float32)

@jax.custom_vjp
def low_back(v):
    return v

def low_keep(v):
    return (lower_precision(v), None)

def low_pass(kept, grad):
    return (grad,)

def back_keep(v):
    return (v, None)

def back_low(kept, grad):
    return (lower_precision(grad),)
lower_precision.defvjp(low_keep, low_pass)
low_back.defvjp(back_keep, back_low)
epsilon = 1e-05

def matmul_hi(left, right):
    return jnp.dot(left, right, precision=lax.Precision.HIGHEST, preferred_element_type=jnp.float32)

def root_mean_norm(value_rows, gain_vec):
    return value_rows * lax.rsqrt(lax.optimization_barrier(jnp.mean(value_rows * value_rows, axis=-1, keepdims=True)) + epsilon) * gain_vec

def rope_tables(positions):
    half_width = HEAD_SIZE // 2
    inv_freq = jnp.power(jnp.float32(1000000.0), -(2.0 * jnp.arange(half_width, dtype=jnp.float32)) / HEAD_SIZE)
    angles = positions.astype(jnp.float32)[:, None] * inv_freq[None, :]
    cosine_table = jnp.concatenate([jnp.cos(angles), jnp.cos(angles)], axis=-1)[:, None, :]
    sine_table = jnp.concatenate([jnp.sin(angles), jnp.sin(angles)], axis=-1)[:, None, :]
    return (cosine_table, sine_table)

def apply_rotary(value_rows, cosine_table, sine_table):
    half_width = HEAD_SIZE // 2
    first_half = value_rows[..., :half_width]
    second_half = value_rows[..., half_width:]
    turned = jnp.concatenate([-second_half, first_half], axis=-1)
    return value_rows * cosine_table + turned * sine_table

def attend_block(query_block, pos_block, doc_block, key_rows, value_rows, positions, doc_ids):
    count_of_rows = query_block.shape[0]
    query_four_axes = query_block.reshape(count_of_rows, KEY_VALUE_HEADS, QUERY_HEADS // KEY_VALUE_HEADS, HEAD_SIZE)
    key_three_axes = key_rows.reshape(SEQUENCE_TOKENS, KEY_VALUE_HEADS, HEAD_SIZE)
    value_three_axes = value_rows.reshape(SEQUENCE_TOKENS, KEY_VALUE_HEADS, HEAD_SIZE)
    scores = jnp.einsum('tjgd,sjd->jgts', query_four_axes, key_three_axes, precision=lax.Precision.HIGHEST) * HEAD_SIZE ** (-0.5)
    scores = low_back(scores)
    allowed = (doc_block[:, None] == doc_ids[None, :]) & (positions[None, :] <= pos_block[:, None])
    masked = jnp.where(allowed[None, None], scores, -1e+30)
    peak = lax.optimization_barrier(jnp.max(masked, axis=-1, keepdims=True))
    expo = jnp.exp(masked - peak)
    probs = lower_precision(expo / lax.optimization_barrier(jnp.sum(expo, axis=-1, keepdims=True)))
    mixed = jnp.einsum('jgts,sjd->tjgd', probs, value_three_axes, precision=lax.Precision.HIGHEST)
    return mixed.reshape(count_of_rows, QUERY_HEADS * HEAD_SIZE)

def layer_seq(hidden, positions, doc_ids, params):
    wq_l, wk_l, wv_l, wo_l, wg_l, wu_l, wd_l, ga_l, gm_l, gain_q, key_norm_gain = params
    normed_a = lower_precision(root_mean_norm(hidden, ga_l))
    q_raw = low_back(matmul_hi(normed_a, wq_l))
    key_unnormed = low_back(matmul_hi(normed_a, wk_l))
    v_all = lower_precision(low_back(matmul_hi(normed_a, wv_l)))
    cosine_table, sine_table = rope_tables(positions)
    q_rot = apply_rotary(root_mean_norm(q_raw.reshape(SEQUENCE_TOKENS, QUERY_HEADS, HEAD_SIZE), gain_q), cosine_table, sine_table)
    key_rotated = apply_rotary(root_mean_norm(key_unnormed.reshape(SEQUENCE_TOKENS, KEY_VALUE_HEADS, HEAD_SIZE), key_norm_gain), cosine_table, sine_table)
    q_rot = lower_precision(q_rot.reshape(SEQUENCE_TOKENS, QUERY_HEADS * HEAD_SIZE))
    key_rotated = lower_precision(key_rotated.reshape(SEQUENCE_TOKENS, KEY_VALUE_HEADS * HEAD_SIZE))
    q_block_rows = min(512, SEQUENCE_TOKENS)
    block_count = SEQUENCE_TOKENS // q_block_rows
    block_fn = jax.checkpoint(attend_block)

    def one_block(inputs):
        query_block, pos_block, doc_block = inputs
        return block_fn(query_block, pos_block, doc_block, key_rotated, v_all, positions, doc_ids)
    attn = lax.map(one_block, (q_rot.reshape(block_count, q_block_rows, QUERY_HEADS * HEAD_SIZE), positions.reshape(block_count, q_block_rows), doc_ids.reshape(block_count, q_block_rows)))
    attn = lower_precision(low_back(attn.reshape(SEQUENCE_TOKENS, QUERY_HEADS * HEAD_SIZE)))
    branch = low_back(matmul_hi(attn, wo_l))
    residual = hidden + branch
    normed_m = lower_precision(root_mean_norm(residual, gm_l))
    gate_pre = low_back(matmul_hi(normed_m, wg_l))
    up_pre = low_back(matmul_hi(normed_m, wu_l))
    hidden_m = lower_precision(jax.nn.silu(gate_pre) * up_pre)
    return residual + matmul_hi(hidden_m, wd_l.T)

def reference(tokens, block_table, doc_flags, w_query, key_weight, value_weight, w_out, w_gate, w_up, w_down, gain_attn, gain_mlp, gain_q, key_norm_gain, cotangent):
    block_rows = TOK_DEV // 2
    offsets = jnp.arange(block_rows, dtype=jnp.int32)
    positions = (block_table.reshape(-1)[:, None].astype(jnp.int32) * block_rows + offsets[None, :]).reshape(-1).astype(jnp.int32)
    seq_flags = jnp.zeros((STREAMS, SEQUENCE_TOKENS), jnp.int32).at[:, positions].set(doc_flags)
    doc_seq = jnp.cumsum(seq_flags, axis=1).astype(jnp.int32) - 1
    doc_ids = doc_seq[:, positions].astype(jnp.int32)

    def forward(hidden, wq_f, wk_f, wv_f, wo_f, wg_f, wu_f, wd_f, ga_f, gm_f, gq_f, gk_f):
        params = (lower_precision(wq_f), lower_precision(wk_f), lower_precision(wv_f), lower_precision(wo_f), lower_precision(wg_f), lower_precision(wu_f), lower_precision(wd_f), lower_precision(ga_f), lower_precision(gm_f), gq_f, gk_f)
        outputs = [layer_seq(hidden[index_seq], positions, doc_ids[index_seq], params) for index_seq in range(STREAMS)]
        return jnp.stack(outputs)
    inputs = (tokens.astype(jnp.float32), w_query.astype(jnp.float32), key_weight.astype(jnp.float32), value_weight.astype(jnp.float32), w_out.astype(jnp.float32), w_gate.astype(jnp.float32), w_up.astype(jnp.float32), w_down.astype(jnp.float32), gain_attn.astype(jnp.float32), gain_mlp.astype(jnp.float32), gain_q.astype(jnp.float32), key_norm_gain.astype(jnp.float32))
    result, pullback = jax.vjp(forward, *inputs)
    grads = pullback(cotangent.astype(jnp.float32))
    return (result.astype(jnp.bfloat16), grads[0], grads[1], grads[2], grads[3], grads[4], grads[5], grads[6], grads[7], grads[8], grads[9], grads[10], grads[11])
```

```python
import functools

import jax
import jax.numpy as jnp
import numpy as np
from jax import lax
from jax.experimental import pallas as pl
from jax.experimental.pallas import tpu as pltpu
from jax.sharding import PartitionSpec as P

HEADS = 16
KV_HEADS = 8
HEAD = 64
LANES = 2 * HEAD
BLOCK = 128
EPS = 1e-05
SCALE = HEAD**-0.5
BF = jnp.bfloat16
F32 = jnp.float32
I32 = jnp.int32
QT = 512
KT = 512
VMEM_BYTES = 56 * 1024 * 1024

NN = (((1,), (0,)), ((), ()))
NT = (((1,), (1,)), ((), ()))
TN = (((0,), (0,)), ((), ()))


def dot(a, b, dims=NN):
    return lax.dot_general(a, b, dims, preferred_element_type=F32)


def params(**kw):
    return pltpu.CompilerParams(vmem_limit_bytes=VMEM_BYTES, **kw)


def in_vmem():
    return pl.BlockSpec(memory_space=pltpu.VMEM)


def in_smem():
    return pl.BlockSpec(memory_space=pltpu.SMEM)


def low_lanes(shape):
    return lax.broadcasted_iota(I32, shape, 1) < HEAD


def half_sums(value, low):
    total = jnp.sum(value, axis=-1, keepdims=True)
    first = jnp.sum(jnp.where(low, value, 0.0), axis=-1, keepdims=True)
    return jnp.where(low, first, total - first)


def half_turn(value):
    lane = lax.broadcasted_iota(I32, value.shape, 1)
    first = (lane % HEAD) < HEAD // 2
    return jnp.where(
        first,
        pltpu.roll(value, LANES - HEAD // 2, 1),
        pltpu.roll(value, HEAD // 2, 1),
    )


def project_kernel(core_ref, n_ref, w_ref, gain_ref, cos_ref, sin_ref, raw_ref, out_ref):
    rows = cos_ref.shape[0]
    is_value = core_ref[0] == 1
    raw_all = dot(n_ref[...], w_ref[...])
    raw_ref[0] = raw_all
    for s in range(2):
        raw = raw_all[s * rows : (s + 1) * rows]
        low = low_lanes(raw.shape)
        inverse = lax.rsqrt(half_sums(raw * raw, low) * (1.0 / HEAD) + EPS)
        normed = raw * inverse * gain_ref[...]
        turned = normed * cos_ref[...] + half_turn(normed) * sin_ref[...]
        kept = jnp.where(jnp.logical_or(low, jnp.logical_not(is_value)), turned, raw)
        out_ref[0, s] = kept.astype(BF)


def project(core, normed, weight, gain, cosine, sine):
    rows = cosine.shape[0]
    return pl.pallas_call(
        project_kernel,
        grid=(KV_HEADS,),
        in_specs=[
            in_smem(),
            pl.BlockSpec(normed.shape, lambda g: (0, 0)),
            pl.BlockSpec((weight.shape[0], LANES), lambda g: (0, g)),
            pl.BlockSpec((1, LANES), lambda g: (0, 0)),
            pl.BlockSpec((rows, LANES), lambda g: (0, 0)),
            pl.BlockSpec((rows, LANES), lambda g: (0, 0)),
        ],
        out_specs=[
            pl.BlockSpec((1, 2 * rows, LANES), lambda g: (g, 0, 0)),
            pl.BlockSpec((1, 2, rows, LANES), lambda g: (g, 0, 0, 0)),
        ],
        out_shape=[
            jax.ShapeDtypeStruct((KV_HEADS, 2 * rows, LANES), F32),
            jax.ShapeDtypeStruct((KV_HEADS, 2, rows, LANES), BF),
        ],
        compiler_params=params(),
        cost_estimate=pl.CostEstimate(
            flops=2 * normed.shape[0] * normed.shape[1] * weight.shape[1],
            bytes_accessed=8 << 20,
            transcendentals=0,
        ),
    )(core, normed, weight, gain, cosine, sine)


def unproject_kernel(core_ref, grad_ref, raw_ref, gain_ref, cos_ref, sin_ref, out_ref, gain_out_ref):
    rows = cos_ref.shape[0]
    is_value = core_ref[0] == 1
    for s in range(2):
        raw = raw_ref[0, s * rows : (s + 1) * rows]
        grad = grad_ref[0, s].astype(F32)
        low = low_lanes(raw.shape)
        inverse = lax.rsqrt(half_sums(raw * raw, low) * (1.0 / HEAD) + EPS)
        back = grad * cos_ref[...] + half_turn(grad * sin_ref[...])
        is_q_or_k = jnp.logical_or(low, jnp.logical_not(is_value))
        gain_rows = jnp.sum(back * raw * inverse, axis=0, keepdims=True)
        scaled = back * gain_ref[...]
        mean = half_sums(scaled * raw, low) * (1.0 / HEAD)
        moved = inverse * scaled - raw * (inverse * inverse * inverse) * mean
        out_ref[s * rows : (s + 1) * rows, :] = jnp.where(is_q_or_k, moved, grad).astype(BF)
        gain_rows = jnp.where(is_q_or_k[:1], gain_rows, 0.0)
        if s == 0:
            total = gain_rows
        else:
            total = total + gain_rows
    gain_out_ref[0] = jnp.broadcast_to(total, (8, LANES))


def unproject(core, grads, raw, gain, cosine, sine):
    rows = cosine.shape[0]
    return pl.pallas_call(
        unproject_kernel,
        grid=(KV_HEADS,),
        in_specs=[
            in_smem(),
            pl.BlockSpec((1, 2, rows, LANES), lambda g: (g, 0, 0, 0)),
            pl.BlockSpec((1, 2 * rows, LANES), lambda g: (g, 0, 0)),
            pl.BlockSpec((1, LANES), lambda g: (0, 0)),
            pl.BlockSpec((rows, LANES), lambda g: (0, 0)),
            pl.BlockSpec((rows, LANES), lambda g: (0, 0)),
        ],
        out_specs=[
            pl.BlockSpec((2 * rows, LANES), lambda g: (0, g)),
            pl.BlockSpec((1, 8, LANES), lambda g: (g, 0, 0)),
        ],
        out_shape=[
            jax.ShapeDtypeStruct((2 * rows, KV_HEADS * LANES), BF),
            jax.ShapeDtypeStruct((KV_HEADS, 8, LANES), F32),
        ],
        compiler_params=params(),
        cost_estimate=pl.CostEstimate(flops=1 << 24, bytes_accessed=8 << 20, transcendentals=0),
    )(core, grads, raw, gain, cosine, sine)


def block_rows(ref, slot):
    return ref[pl.ds(pl.multiple_of(slot * BLOCK, BLOCK), BLOCK), :]


def sum_of_parts(value):
    first = value.astype(BF)
    rest = value - first.astype(F32)
    second = rest.astype(BF)
    third = (rest - second.astype(F32)).astype(BF)
    return first, second, third


def allowed_pairs(j, pos_row, start_row):
    key_pos = j * KT + lax.broadcasted_iota(I32, (KT, 1), 0)
    return jnp.logical_and(key_pos <= pos_row, key_pos >= start_row)


def walk_keys(lims_ref, i, step, carry):
    lo, full_lo, full_hi, hi = (lims_ref[e, i] for e in range(4))
    carry = lax.fori_loop(lo, full_lo, functools.partial(step, True), carry)
    carry = lax.fori_loop(full_lo, full_hi, functools.partial(step, False), carry)
    return lax.fori_loop(full_hi, hi, functools.partial(step, True), carry)


def attend_kernel(
    core_ref, kslot_ref, qslot_ref, lims_ref, q_ref, own_ref, other_ref, pos_ref, start_ref,
    out_ref, keep_ref, lse_ref, keys, values_t, placed,
):
    q_tiles = q_ref.shape[0] // QT
    k_tiles = own_ref.shape[0] // KT
    per = KT // BLOCK
    is_first = core_ref[0] == 0
    values_t[HEAD:, :] = jnp.ones((values_t.shape[0] - HEAD, values_t.shape[1]), BF)

    def load(t, carry):
        for b in range(per):
            slot = kslot_ref[t * per + b]
            own = block_rows(own_ref, slot)[:, HEAD:]
            other = block_rows(other_ref, slot)[:, HEAD:]
            at = pl.ds(pl.multiple_of((t * per + b) * BLOCK, BLOCK), BLOCK)
            keys[at, :] = jnp.where(is_first, own, other)
            value = jnp.where(is_first, other, own).astype(F32)
            values_t[:HEAD, at] = value.T.astype(BF)
        return carry

    lax.fori_loop(0, k_tiles, load, 0)

    def tile(i, carry):
        cols = pl.ds(pl.multiple_of(i * QT, QT), QT)
        parts = [block_rows(q_ref, qslot_ref[i * (QT // BLOCK) + b])[:, :HEAD] for b in range(QT // BLOCK)]
        query_t = (jnp.concatenate(parts, axis=0).astype(F32) * SCALE).T.astype(BF)
        pos_row = pos_ref[:, cols]
        start_row = start_ref[:, cols]

        def step(masked, j, acc):
            at = pl.ds(pl.multiple_of(j * KT, KT), KT)
            p = jnp.exp(dot(keys[at, :], query_t))
            if masked:
                p = jnp.where(allowed_pairs(j, pos_row, start_row), p, 0.0)
            return acc + dot(values_t[:, at], p.astype(BF))

        acc = walk_keys(lims_ref, i, step, jnp.zeros((values_t.shape[0], QT), F32))
        total = acc[HEAD : HEAD + 1]
        mixed = acc[:HEAD] / total
        keep_ref[:, cols] = mixed
        lse_ref[:, cols] = jnp.log(total)
        rows = mixed.T
        for b in range(QT // BLOCK):
            slot = qslot_ref[i * (QT // BLOCK) + b]
            placed[pl.ds(pl.multiple_of(slot * BLOCK, BLOCK), BLOCK), :] = rows[b * BLOCK : (b + 1) * BLOCK]
        return carry

    lax.fori_loop(0, q_tiles, tile, 0)

    def pack(c, carry):
        first = placed[pl.ds(pl.multiple_of(c * 2 * BLOCK, BLOCK), BLOCK), :]
        second = placed[pl.ds(pl.multiple_of((c * 2 + 1) * BLOCK, BLOCK), BLOCK), :]
        out_ref[pl.ds(pl.multiple_of(c * BLOCK, BLOCK), BLOCK), :] = jnp.concatenate([first, second], axis=1).astype(BF)
        return carry

    lax.fori_loop(0, q_ref.shape[0] // (2 * BLOCK), pack, 0)


def attend(core, tables, queries, own, other):
    kslot, qslot, lims, pos, start = tables
    n_q, n_k = queries.shape[0], own.shape[0]
    return pl.pallas_call(
        attend_kernel,
        in_specs=[in_smem()] * 4 + [in_vmem()] * 5,
        out_specs=[in_vmem()] * 3,
        out_shape=[
            jax.ShapeDtypeStruct((n_q // 2, LANES), BF),
            jax.ShapeDtypeStruct((HEAD, n_q), F32),
            jax.ShapeDtypeStruct((1, n_q), F32),
        ],
        scratch_shapes=[
            pltpu.VMEM((n_k, HEAD), BF),
            pltpu.VMEM((HEAD + 16, n_k), BF),
            pltpu.VMEM((n_q, HEAD), F32),
        ],
        compiler_params=params(),
        cost_estimate=pl.CostEstimate(flops=8 * n_q * n_k * HEAD, bytes_accessed=8 << 20, transcendentals=n_q * n_k),
    )(core, kslot, qslot, lims, queries, own, other, pos, start)


def attend_back_kernel(
    core_ref, kslot_ref, qslot_ref, lims_ref, q_ref, own_ref, other_ref, pos_ref, start_ref,
    grad_ref, mixed_ref, lse_ref,
    dq_ref, keep_ref, send_ref,
    keys, values, keys_t, grad_keys, grad_values, grad_placed,
):
    q_tiles = q_ref.shape[0] // QT
    k_tiles = own_ref.shape[0] // KT
    per = KT // BLOCK
    is_first = core_ref[0] == 0
    ones = jnp.ones((BLOCK, HEAD), BF)

    def load(t, carry):
        for b in range(per):
            slot = kslot_ref[t * per + b]
            own = block_rows(own_ref, slot)[:, HEAD:]
            other = block_rows(other_ref, slot)[:, HEAD:]
            at = pl.ds(pl.multiple_of((t * per + b) * BLOCK, BLOCK), BLOCK)
            key = jnp.where(is_first, own, other)
            value = jnp.where(is_first, other, own)
            keys[at, :] = jnp.concatenate([key, ones], axis=1)
            values[at, :] = jnp.concatenate([value, ones], axis=1)
            keys_t[:, at] = key.astype(F32).T.astype(BF)
            grad_keys[at, :] = jnp.zeros((BLOCK, HEAD), F32)
            grad_values[at, :] = jnp.zeros((BLOCK, HEAD), F32)
        return carry

    lax.fori_loop(0, k_tiles, load, 0)

    def unpack(c, carry):
        pair = grad_ref[pl.ds(pl.multiple_of(c * BLOCK, BLOCK), BLOCK), :]
        grad_placed[pl.ds(pl.multiple_of(c * 2 * BLOCK, BLOCK), BLOCK), :] = pair[:, :HEAD]
        grad_placed[pl.ds(pl.multiple_of((c * 2 + 1) * BLOCK, BLOCK), BLOCK), :] = pair[:, HEAD:]
        return carry

    lax.fori_loop(0, q_ref.shape[0] // (2 * BLOCK), unpack, 0)

    def tile(i, carry):
        cols = pl.ds(pl.multiple_of(i * QT, QT), QT)
        slots = [qslot_ref[i * (QT // BLOCK) + b] for b in range(QT // BLOCK)]
        query_f = jnp.concatenate([block_rows(q_ref, s)[:, :HEAD] for s in slots], axis=0).astype(F32) * SCALE
        grad = jnp.concatenate([block_rows(grad_placed, s) for s in slots], axis=0)
        query = query_f.astype(BF)
        grad_t = grad.astype(F32).T
        delta = jnp.sum(grad_t * mixed_ref[:, cols], axis=0, keepdims=True)
        pad = jnp.zeros((HEAD - 3, QT), F32)
        query_t = jnp.concatenate(
            [query_f.T] + [e.astype(F32) for e in sum_of_parts(-lse_ref[:, cols])] + [pad], axis=0
        ).astype(BF)
        grad_t = jnp.concatenate([grad_t] + [e.astype(F32) for e in sum_of_parts(-delta)] + [pad], axis=0).astype(BF)
        pos_row = pos_ref[:, cols]
        start_row = start_ref[:, cols]

        def step(masked, j, acc):
            at = pl.ds(pl.multiple_of(j * KT, KT), KT)
            p = jnp.exp(dot(keys[at, :], query_t))
            if masked:
                p = jnp.where(allowed_pairs(j, pos_row, start_row), p, 0.0)
            grad_s = (p * dot(values[at, :], grad_t)).astype(BF)
            grad_values[at, :] += dot(p.astype(BF), grad)
            grad_keys[at, :] += dot(grad_s, query)
            return acc + dot(keys_t[:, at], grad_s)

        acc = walk_keys(lims_ref, i, step, jnp.zeros((HEAD, QT), F32))
        rows = (acc * SCALE).T
        rows = jnp.concatenate([rows, jnp.zeros((QT, HEAD), F32)], axis=1)
        for b in range(QT // BLOCK):
            dq_ref[pl.ds(pl.multiple_of(slots[b] * BLOCK, BLOCK), BLOCK), :] = rows[b * BLOCK : (b + 1) * BLOCK]
        return carry

    lax.fori_loop(0, q_tiles, tile, 0)

    def place(t, carry):
        zeros = jnp.zeros((BLOCK, HEAD), F32)
        for b in range(per):
            slot = kslot_ref[t * per + b]
            at = pl.ds(pl.multiple_of((t * per + b) * BLOCK, BLOCK), BLOCK)
            to = pl.ds(pl.multiple_of(slot * BLOCK, BLOCK), BLOCK)
            key, value = grad_keys[at, :], grad_values[at, :]
            mine = jnp.where(is_first, key, value)
            theirs = jnp.where(is_first, value, key)
            keep_ref[to, :] = jnp.concatenate([zeros, mine], axis=1)
            send_ref[to, :] = jnp.concatenate([zeros, theirs], axis=1).astype(BF)
        return carry

    lax.fori_loop(0, k_tiles, place, 0)


def attend_back(core, tables, queries, own, other, grads, mixed, lse):
    kslot, qslot, lims, pos, start = tables
    n_q, n_k = queries.shape[0], own.shape[0]
    return pl.pallas_call(
        attend_back_kernel,
        in_specs=[in_smem()] * 4 + [in_vmem()] * 8,
        out_specs=[in_vmem()] * 3,
        out_shape=[
            jax.ShapeDtypeStruct((n_q, LANES), F32),
            jax.ShapeDtypeStruct((n_k, LANES), F32),
            jax.ShapeDtypeStruct((n_k, LANES), BF),
        ],
        scratch_shapes=[
            pltpu.VMEM((n_k, LANES), BF),
            pltpu.VMEM((n_k, LANES), BF),
            pltpu.VMEM((HEAD, n_k), BF),
            pltpu.VMEM((n_k, HEAD), F32),
            pltpu.VMEM((n_k, HEAD), F32),
            pltpu.VMEM((n_q, HEAD), BF),
        ],
        compiler_params=params(),
        cost_estimate=pl.CostEstimate(flops=16 * n_q * n_k * HEAD, bytes_accessed=8 << 20, transcendentals=n_q * n_k),
    )(core, kslot, qslot, lims, queries, own, other, pos, start, grads, mixed, lse)


def rms(value, gain):
    inverse = lax.rsqrt(jnp.mean(value * value, axis=-1, keepdims=True) + EPS)
    return value * inverse * gain, inverse


def rms_back(value, inverse, gain, grad):
    scaled = grad * gain
    mean = jnp.mean(scaled * value, axis=-1, keepdims=True)
    moved = inverse * scaled - value * (inverse * inverse * inverse) * mean
    return moved, jnp.sum(grad * value * inverse, axis=0)


def rope_tables(positions):
    inv_freq = jnp.power(F32(1000000.0), -(2.0 * jnp.arange(HEAD // 2, dtype=F32)) / HEAD)
    angles = positions.astype(F32)[:, None] * inv_freq[None, :]
    cosine, sine = jnp.cos(angles), jnp.sin(angles)
    return (
        jnp.concatenate([cosine] * 4, axis=1),
        jnp.concatenate([-sine, sine, -sine, sine], axis=1),
    )


def make_shards(n):
    bits = n.bit_length() - 1
    order = [4, 8, 1, 2] if n == 16 else [1 << b for b in range(bits)]
    groups = n // 16
    a2a_groups = None if groups == 1 else [[t * 16 + d for d in range(16)] for t in range(groups)]
    kv_groups = None if groups == 1 else [[t * 16 + d for t in range(groups)] for d in range(16)]

    def ctx_swap(value, mask):
        return lax.ppermute(value, "ctx", [(i, i ^ mask) for i in range(n)])

    def core_swap(value):
        return lax.ppermute(value, "wt", [(0, 1), (1, 0)])

    def gather_rows(piece):
        for mask in order:
            piece = jnp.concatenate([piece, ctx_swap(piece, mask)], axis=0)
        return piece

    def scatter_rows(value):
        for level, mask in enumerate(reversed(order)):
            half = value.shape[0] // 2
            arrived = ctx_swap(value[half:], mask)
            value = value[:half].astype(F32) + arrived.astype(F32)
            if level < len(order) - 1:
                value = value.astype(BF)
        return value

    def swap_heads(value):
        return lax.all_to_all(value, "ctx", 0, 0, axis_index_groups=a2a_groups, tiled=True)

    def shards(
        tokens, block_table, doc_flags, w_query, key_weight, value_weight, w_out, w_gate, w_up, w_down,
        gain_attn, gain_mlp, gain_q, key_norm_gain, cotangent,
    ):
        width = tokens.shape[-1]
        rows = tokens.shape[1]
        owned = w_query.shape[0]
        chip_rows = 2 * owned
        me = lax.axis_index("ctx")
        core = lax.axis_index("wt")
        first = core == 0
        core_arr = core.astype(I32).reshape(1)
        slots_n = 2 * n

        def by_core(a, b, axis=0):
            return jnp.where(first, jnp.concatenate([a, b], axis=axis), jnp.concatenate([b, a], axis=axis))

        def pick(a, b):
            return jnp.where(first, a, b)

        rel = np.arange(n)
        offset = sum(((rel >> level) & 1) * mask for level, mask in enumerate(order))
        chip_of = jnp.bitwise_xor(me.astype(I32), jnp.asarray(offset, I32))
        canon = (chip_of[:, None] * chip_rows + jnp.arange(chip_rows, dtype=I32)[None, :]).reshape(-1)
        perm = (jnp.arange(width, dtype=I32)[:, None] == canon[None, :]).astype(BF)

        def chip_piece(zero, one):
            mine = pick(zero, one).astype(BF)
            theirs = pick(one, zero).astype(BF)
            return by_core(mine, core_swap(theirs))

        def halves(weight):
            half = weight.shape[1] // 2
            return chip_piece(weight[:, :half], weight[:, half:])

        q_pairs = w_query.reshape(owned, KV_HEADS, 2, HEAD)
        qk = jnp.concatenate([q_pairs[:, :, 0], key_weight.reshape(owned, KV_HEADS, HEAD)], axis=-1).reshape(owned, width)
        qv = jnp.concatenate([q_pairs[:, :, 1], value_weight.reshape(owned, KV_HEADS, HEAD)], axis=-1).reshape(owned, width)
        flag_cols = rows // owned
        own_blocks = block_table[0]
        table_col = jnp.concatenate([own_blocks.astype(F32), jnp.zeros((owned - 2,), F32)])
        extra = jnp.concatenate(
            [
                gain_attn[:, None],
                gain_mlp[:, None],
                table_col[:, None],
                doc_flags[0].reshape(owned, flag_cols).astype(F32),
                jnp.zeros((owned, LANES - 3 - flag_cols), F32),
            ],
            axis=1,
        )
        first_piece = chip_piece(jnp.concatenate([qk, extra], axis=1), jnp.concatenate([qv, extra], axis=1))
        first_full = gather_rows(first_piece)
        w_qkv = first_full[:, :width]
        extras = first_full[:, width:].astype(F32)

        x_own, c_own = tokens[0], cotangent[0]
        x_two = dot(by_core(x_own, core_swap(x_own)), perm).astype(BF)
        c_two = dot(by_core(c_own, core_swap(c_own)), perm).astype(BF)
        hidden = x_two.astype(F32)

        wo_half = gather_rows(halves(w_out))
        w_g = gather_rows(halves(w_gate))
        w_u = gather_rows(halves(w_up))
        w_d = gather_rows(halves(w_down))

        gain_a, gain_m = extras[:, 0][None, :], extras[:, 1][None, :]
        per_chip = extras.reshape(n, 2, owned, LANES)
        block_of = per_chip[:, 0, :2, 2].reshape(-1).astype(I32)
        seq = me % 2
        flags = jnp.where(seq == 0, per_chip[:, 0], per_chip[:, 1])[:, :, 3 : 3 + flag_cols].reshape(slots_n, BLOCK)
        slot_of = (chip_of[:, None] * 2 + jnp.arange(2, dtype=I32)[None, :]).reshape(-1)
        ids = jnp.arange(slots_n, dtype=I32)
        hit = ids[:, None] == block_of[None, :]
        flags_pos = dot(hit.astype(BF), flags.astype(BF))
        kslot = jnp.sum(jnp.where(hit, slot_of[None, :], 0), axis=1)
        pos = jnp.arange(slots_n * BLOCK, dtype=I32).reshape(slots_n, BLOCK)
        begins = jnp.where(flags_pos > 0.5, pos, -1)
        lane = jnp.arange(BLOCK, dtype=I32)
        inside = jnp.max(jnp.where(lane[None, None, :] <= lane[None, :, None], begins[:, None, :], -1), axis=2)
        carried = jnp.max(jnp.where(ids[None, :] < ids[:, None], jnp.max(begins, axis=1)[None, :], -1), axis=1)
        doc_start = jnp.maximum(inside, carried[:, None])
        here = (slot_of // 32) == (me // 16)
        rank = jnp.sum((here[None, :] & (block_of[None, :] < block_of[:, None])).astype(I32), axis=1)
        hit_q = here[None, :] & (rank[None, :] == jnp.arange(32, dtype=I32)[:, None])
        q_block = jnp.sum(jnp.where(hit_q, block_of[None, :], 0), axis=1)
        qslot = jnp.sum(jnp.where(hit_q, slot_of[None, :] - (me // 16) * 32, 0), axis=1)
        q_pos = q_block[:, None] * BLOCK + lane[None, :]
        q_start = jnp.sum(jnp.where((q_block[:, None] == ids[None, :])[:, :, None], doc_start[None], 0), axis=1)
        n_q = 32 * BLOCK
        tile_start = q_start.reshape(n_q // QT, QT)
        tile_pos = q_pos.reshape(n_q // QT, QT)
        low, high = jnp.min(tile_start, axis=1) // KT, jnp.max(tile_pos, axis=1) // KT + 1
        full_low = jnp.minimum((jnp.max(tile_start, axis=1) + KT - 1) // KT, high)
        full_high = jnp.maximum(jnp.minimum((jnp.min(tile_pos, axis=1) + 1) // KT, high), full_low)
        lims = jnp.stack([low, full_low, full_high, high])
        tables = (kslot, qslot, lims, q_pos.reshape(1, n_q), q_start.reshape(1, n_q))

        own_pos = (own_blocks[:, None] * BLOCK + lane[None, :]).reshape(-1)
        cosine, sine = rope_tables(own_pos)
        gain_qk = jnp.concatenate([gain_q, key_norm_gain])[None, :]

        normed_a, inv_a = rms(hidden, gain_a)
        normed_ab = normed_a.astype(BF)
        raw, packed = project(core_arr, normed_ab, w_qkv, gain_qk, cosine, sine)
        queries = swap_heads(packed.reshape(16, rows, LANES)).reshape(n_q, LANES)
        own_kv = queries
        if groups > 1:
            own_kv = lax.all_gather(queries, "ctx", axis=0, tiled=True, axis_index_groups=kv_groups)
        other_kv = core_swap(own_kv)
        mixed_packed, mixed, lse = attend(core_arr, tables, queries, own_kv, other_kv)

        def heads_to_rows(value):
            value = value.reshape(KV_HEADS, 2, BLOCK, 2, HEAD)
            return jnp.transpose(value, (1, 3, 2, 0, 4)).reshape(2 * rows, KV_HEADS * HEAD)

        def rows_to_heads(value):
            value = value.reshape(2, 2, BLOCK, KV_HEADS, HEAD)
            return jnp.transpose(value, (3, 0, 2, 1, 4)).reshape(16, BLOCK, LANES)

        wo_other = core_swap(wo_half)
        wo_full = by_core(wo_half, wo_other, axis=1)
        head_ids = jnp.arange(width, dtype=I32)
        place = (head_ids // 512).astype(I32)
        head_row = (((head_ids % 512) // HEAD) * 2 + jnp.bitwise_xor(core.astype(I32), place)) * HEAD + head_ids % HEAD
        select = (head_row[:, None] == canon[None, :]).astype(BF)
        wo_sel = dot(select, dot(wo_full, perm).astype(BF)).astype(BF)

        attn_own = heads_to_rows(swap_heads(mixed_packed.reshape(16, BLOCK, LANES)))
        attn = jnp.concatenate([attn_own, core_swap(attn_own)], axis=1)
        residual = hidden + dot(attn, wo_sel)
        normed_m, inv_m = rms(residual, gain_m)
        normed_mb = normed_m.astype(BF)

        gate = dot(normed_mb, w_g)
        up = dot(normed_mb, w_u)
        sig = jax.nn.sigmoid(gate)
        silu = gate * sig
        mid = (silu * up).astype(BF)
        grad_mid = dot(c_two, w_d)
        grad_gate_in = (grad_mid * up * (sig * (1.0 + gate * (1.0 - sig)))).astype(BF)
        grad_up_in = (grad_mid * silu).astype(BF)
        grad_n2_part = (dot(grad_gate_in, w_g, NT) + dot(grad_up_in, w_u, NT)).astype(BF)
        grad_n2 = grad_n2_part.astype(F32) + core_swap(grad_n2_part).astype(F32)
        moved_m, grad_gm = rms_back(residual, inv_m, gain_m, grad_n2)
        grad_h = c_two.astype(F32) + moved_m
        grad_hb = grad_h.astype(BF)
        grad_attn = dot(grad_hb, wo_sel[: KV_HEADS * HEAD], NT).astype(BF)
        grads_in = swap_heads(rows_to_heads(grad_attn)).reshape(n_q // 2, LANES)

        mlp_part = dot(mid, w_d, NT)
        mlp_other = core_swap(pick(mlp_part[rows:], mlp_part[:rows]))
        layer_rel = pick(residual[:rows], residual[rows:]) + (pick(mlp_part[:rows], mlp_part[rows:]) + mlp_other)
        layer_out = dot(layer_rel.astype(BF), perm, NT).astype(BF)[None]

        part_down = scatter_rows(dot(c_two, mid, TN).astype(BF))
        part_gate = scatter_rows(dot(normed_mb, grad_gate_in, TN).astype(BF))
        part_up = scatter_rows(dot(normed_mb, grad_up_in, TN).astype(BF))
        attn_rel = dot(attn, select).astype(BF)
        grad_hc = dot(grad_hb, pick(perm[: width // 2], perm[width // 2 :]), NT).astype(BF)
        part_out = scatter_rows(dot(attn_rel, grad_hc, TN).astype(BF))

        dq, keep, send = attend_back(core_arr, tables, queries, own_kv, other_kv, grads_in, mixed, lse)
        grad_kv = keep + core_swap(send).astype(F32)
        if groups > 1:
            grad_kv = lax.psum_scatter(grad_kv, "ctx", scatter_dimension=0, tiled=True, axis_index_groups=kv_groups)
        back = swap_heads((dq + grad_kv).astype(BF).reshape(16, rows, LANES))
        grad_qkv_in, gain_parts = unproject(core_arr, back.reshape(KV_HEADS, 2, rows, LANES), raw, gain_qk, cosine, sine)
        part_qkv = scatter_rows(dot(normed_ab, grad_qkv_in, TN).astype(BF))
        n1_part = dot(grad_qkv_in, w_qkv, NT)
        n1_other = core_swap(pick(n1_part[rows:], n1_part[:rows]))
        grad_n1 = pick(n1_part[:rows], n1_part[rows:]) + n1_other

        def mine(value):
            return pick(value[:rows], value[rows:])

        moved_a, grad_ga = rms_back(mine(hidden), mine(inv_a), gain_a, grad_n1)
        grad_in_rel = mine(grad_h) + moved_a
        in_hi = grad_in_rel.astype(BF)
        in_lo = (grad_in_rel - in_hi.astype(F32)).astype(BF)
        grad_input = (dot(in_hi, perm, NT) + dot(in_lo, perm, NT))[None]

        vectors = jnp.stack([grad_ga, jnp.where(first, grad_gm, 0.0)])
        vectors = lax.dot_general(
            vectors, perm.astype(F32), NT, precision=lax.Precision.HIGHEST, preferred_element_type=F32
        )
        heads_gain = jnp.sum(gain_parts[:, 0], axis=0)
        small = jnp.concatenate([vectors.reshape(-1, LANES), heads_gain[None], jnp.zeros((7, LANES), F32)])
        for mask in order:
            small = small + ctx_swap(small, mask)
        small = small + core_swap(small)
        my_row = (me * 2 + core) * owned
        gains = small[: 2 * width // LANES].reshape(2, width)
        gains = lax.dynamic_slice_in_dim(gains, my_row, owned, axis=1)

        def finish(part):
            kept = pick(part[:owned], part[owned:])
            arrived = core_swap(pick(part[owned:], part[:owned]))
            return kept, arrived

        def finish_halves(part):
            return by_core(*finish(part), axis=1)

        kept, arrived = finish(part_qkv)
        zero = pick(kept, arrived).reshape(owned, KV_HEADS, LANES)
        one = pick(arrived, kept).reshape(owned, KV_HEADS, LANES)
        grad_query = jnp.stack([zero[..., :HEAD], one[..., :HEAD]], axis=2).reshape(owned, width)
        grad_key = zero[..., HEAD:].reshape(owned, KV_HEADS * HEAD)
        grad_value = one[..., HEAD:].reshape(owned, KV_HEADS * HEAD)
        return (
            layer_out,
            grad_input,
            grad_query,
            grad_key,
            grad_value,
            finish_halves(part_out),
            finish_halves(part_gate),
            finish_halves(part_up),
            finish_halves(part_down),
            gains[0],
            gains[1],
            small[2 * width // LANES, :HEAD],
            small[2 * width // LANES, HEAD:],
        )

    return shards


def solution(mesh):
    seq = P("wt", "ctx", None)
    weight = P(("ctx", "wt"), None)
    vector = P(("ctx", "wt"))
    return jax.shard_map(
        make_shards(mesh.shape["ctx"]),
        mesh=mesh,
        in_specs=(seq, P("ctx", None), P("wt", "ctx")) + (weight,) * 7 + (vector, vector, P(), P(), seq),
        out_specs=(seq, seq) + (weight,) * 7 + (vector, vector, P(), P()),
        check_vma=False,
    )
```

```python
import functools

import jax
import jax.numpy as jnp
import numpy as np
from jax import lax
from jax.experimental import pallas as pl
from jax.experimental.pallas import tpu as pltpu
from jax.sharding import PartitionSpec as P

HEADS = 16
KV_HEADS = 8
HEAD = 64
LANES = 2 * HEAD
BLOCK = 128
EPS = 1e-05
SCALE = HEAD**-0.5
BF = jnp.bfloat16
F32 = jnp.float32
I32 = jnp.int32
QT = 512
KT = 512
TILES = 9
VMEM_BYTES = 56 * 1024 * 1024

NN = (((1,), (0,)), ((), ()))
NT = (((1,), (1,)), ((), ()))
TN = (((0,), (0,)), ((), ()))


def dot(a, b, dims=NN):
    return lax.dot_general(a, b, dims, preferred_element_type=F32)


def params(**kw):
    return pltpu.CompilerParams(vmem_limit_bytes=VMEM_BYTES, **kw)


def in_vmem():
    return pl.BlockSpec(memory_space=pltpu.VMEM)


def in_smem():
    return pl.BlockSpec(memory_space=pltpu.SMEM)


def low_lanes(shape):
    return lax.broadcasted_iota(I32, shape, 1) < HEAD


def half_sums(value, low):
    total = jnp.sum(value, axis=-1, keepdims=True)
    first = jnp.sum(jnp.where(low, value, 0.0), axis=-1, keepdims=True)
    return jnp.where(low, first, total - first)


def half_turn(value):
    lane = lax.broadcasted_iota(I32, value.shape, 1)
    first = (lane % HEAD) < HEAD // 2
    return jnp.where(
        first,
        pltpu.roll(value, LANES - HEAD // 2, 1),
        pltpu.roll(value, HEAD // 2, 1),
    )


def project_kernel(n_parts, swaps, core_ref, x_ref, norm_gain_ref, gain_ref, cos_ref, sin_ref, *refs):
    weights, (n_ref, raw_ref, out_ref) = refs[: 2 * n_parts], refs[2 * n_parts :]
    rows = cos_ref.shape[0]
    is_value = core_ref[0] == 1
    x = x_ref[...].astype(F32)
    inverse = lax.rsqrt(jnp.mean(x * x, axis=-1, keepdims=True) + EPS)
    n_ref[...] = (x * inverse * norm_gain_ref[...]).astype(BF)
    groups = KV_HEADS // 2
    for half in range(2):
        total, at = None, 0
        for part in weights[half * n_parts : (half + 1) * n_parts]:
            length = part.shape[0]
            pieces = [n_ref[:, e : e + swaps[2]] for e in swaps[half][at // swaps[2] : (at + length) // swaps[2]]]
            left = pieces[0] if len(pieces) == 1 else jnp.concatenate(pieces, axis=1)
            term = dot(left, part[:, : groups * LANES])
            total = term if total is None else total + term
            at += length
        raw_ref[:, half * groups * LANES : (half + 1) * groups * LANES] = total
    low = low_lanes((rows, LANES))
    turns = jnp.logical_or(low, jnp.logical_not(is_value))
    for g in range(KV_HEADS):
        for s in range(2):
            raw = raw_ref[s * rows : (s + 1) * rows, g * LANES : (g + 1) * LANES]
            inverse = lax.rsqrt(half_sums(raw * raw, low) * (1.0 / HEAD) + EPS)
            normed = raw * inverse * gain_ref[...]
            turned = normed * cos_ref[...] + half_turn(normed) * sin_ref[...]
            out_ref[g, s] = jnp.where(turns, turned, raw).astype(BF)


def project(core, x, norm_gain, gain, cosine, sine, parts, chunk, chunk_orders):
    rows = cosine.shape[0]
    n_parts = len(parts[0])
    swaps = ([c * chunk for c in chunk_orders[0]], [c * chunk for c in chunk_orders[1]], chunk)
    return pl.pallas_call(
        functools.partial(project_kernel, n_parts, swaps),
        in_specs=[in_smem()] + [in_vmem()] * (5 + 2 * n_parts),
        out_specs=[in_vmem()] * 3,
        out_shape=[
            jax.ShapeDtypeStruct(x.shape, BF),
            jax.ShapeDtypeStruct((2 * rows, KV_HEADS * LANES), F32),
            jax.ShapeDtypeStruct((KV_HEADS, 2, rows, LANES), BF),
        ],
        compiler_params=params(),
        cost_estimate=pl.CostEstimate(flops=2 * x.shape[0] * x.shape[1] * KV_HEADS * LANES, bytes_accessed=8 << 20, transcendentals=0),
    )(core, x, norm_gain, gain, cosine, sine, *parts[0], *parts[1])


def unproject_kernel(core_ref, grad_ref, raw_ref, gain_ref, cos_ref, sin_ref, out_ref, gain_out_ref):
    rows = cos_ref.shape[0]
    is_value = core_ref[0] == 1
    for s in range(2):
        raw = raw_ref[s * rows : (s + 1) * rows]
        grad = grad_ref[0, s].astype(F32)
        low = low_lanes(raw.shape)
        inverse = lax.rsqrt(half_sums(raw * raw, low) * (1.0 / HEAD) + EPS)
        back = grad * cos_ref[...] + half_turn(grad * sin_ref[...])
        is_q_or_k = jnp.logical_or(low, jnp.logical_not(is_value))
        gain_rows = jnp.sum(back * raw * inverse, axis=0, keepdims=True)
        scaled = back * gain_ref[...]
        mean = half_sums(scaled * raw, low) * (1.0 / HEAD)
        moved = inverse * scaled - raw * (inverse * inverse * inverse) * mean
        out_ref[s * rows : (s + 1) * rows, :] = jnp.where(is_q_or_k, moved, grad).astype(BF)
        gain_rows = jnp.where(is_q_or_k[:1], gain_rows, 0.0)
        if s == 0:
            total = gain_rows
        else:
            total = total + gain_rows
    gain_out_ref[0] = jnp.broadcast_to(total, (8, LANES))


def unproject(core, grads, raw, gain, cosine, sine):
    rows = cosine.shape[0]
    return pl.pallas_call(
        unproject_kernel,
        grid=(KV_HEADS,),
        in_specs=[
            in_smem(),
            pl.BlockSpec((1, 2, rows, LANES), lambda g: (g, 0, 0, 0)),
            pl.BlockSpec((2 * rows, LANES), lambda g: (0, g)),
            pl.BlockSpec((1, LANES), lambda g: (0, 0)),
            pl.BlockSpec((rows, LANES), lambda g: (0, 0)),
            pl.BlockSpec((rows, LANES), lambda g: (0, 0)),
        ],
        out_specs=[
            pl.BlockSpec((2 * rows, LANES), lambda g: (0, g)),
            pl.BlockSpec((1, 8, LANES), lambda g: (g, 0, 0)),
        ],
        out_shape=[
            jax.ShapeDtypeStruct((2 * rows, KV_HEADS * LANES), BF),
            jax.ShapeDtypeStruct((KV_HEADS, 8, LANES), F32),
        ],
        compiler_params=params(),
        cost_estimate=pl.CostEstimate(flops=1 << 24, bytes_accessed=8 << 20, transcendentals=0),
    )(core, grads, raw, gain, cosine, sine)


def block_rows(ref, slot):
    return ref[pl.ds(pl.multiple_of(slot * BLOCK, BLOCK), BLOCK), :]


def sum_of_parts(value):
    first = value.astype(BF)
    rest = value - first.astype(F32)
    second = rest.astype(BF)
    third = (rest - second.astype(F32)).astype(BF)
    return first, second, third


def allowed_pairs(j, pos_row, start_row):
    key_pos = j * KT + lax.broadcasted_iota(I32, (KT, 1), 0)
    return jnp.logical_and(key_pos <= pos_row, key_pos >= start_row)


def walk_keys(lims_ref, i, step, carry):
    lo, full_lo, full_hi, hi = (lims_ref[e, i] for e in range(4))
    carry = lax.fori_loop(lo, full_lo, functools.partial(step, True), carry)
    carry = lax.fori_loop(full_lo, full_hi, functools.partial(step, False), carry)
    return lax.fori_loop(full_hi, hi, functools.partial(step, True), carry)


def attend_kernel(
    core_ref, kslot_ref, qslot_ref, lims_ref, q_ref, own_ref, other_ref, pos_ref, start_ref,
    out_ref, keep_ref, lse_ref, keys, values_t, placed,
):
    q_tiles = q_ref.shape[0] // QT
    k_tiles = own_ref.shape[0] // KT
    per = KT // BLOCK
    is_first = core_ref[0] == 0
    values_t[HEAD:, :] = jnp.ones((values_t.shape[0] - HEAD, values_t.shape[1]), BF)

    def load(t, carry):
        for b in range(per):
            slot = kslot_ref[t * per + b]
            own = block_rows(own_ref, slot)[:, HEAD:]
            other = block_rows(other_ref, slot)[:, HEAD:]
            at = pl.ds(pl.multiple_of((t * per + b) * BLOCK, BLOCK), BLOCK)
            keys[at, :] = jnp.where(is_first, own, other)
            value = jnp.where(is_first, other, own).astype(F32)
            values_t[:HEAD, at] = value.T.astype(BF)
        return carry

    lax.fori_loop(0, k_tiles, load, 0)

    def tile(i, carry):
        cols = pl.ds(pl.multiple_of(i * QT, QT), QT)
        parts = [block_rows(q_ref, qslot_ref[i * (QT // BLOCK) + b])[:, :HEAD] for b in range(QT // BLOCK)]
        query_t = (jnp.concatenate(parts, axis=0).astype(F32) * SCALE).T.astype(BF)
        pos_row = pos_ref[:, cols]
        start_row = start_ref[:, cols]

        def step(masked, j, acc):
            at = pl.ds(pl.multiple_of(j * KT, KT), KT)
            p = jnp.exp(dot(keys[at, :], query_t))
            if masked:
                p = jnp.where(allowed_pairs(j, pos_row, start_row), p, 0.0)
            return acc + dot(values_t[:, at], p.astype(BF))

        acc = walk_keys(lims_ref, i, step, jnp.zeros((values_t.shape[0], QT), F32))
        total = acc[HEAD : HEAD + 1]
        mixed = acc[:HEAD] / total
        keep_ref[:, cols] = mixed
        lse_ref[:, cols] = jnp.log(total)
        rows = mixed.T
        for b in range(QT // BLOCK):
            slot = qslot_ref[i * (QT // BLOCK) + b]
            placed[pl.ds(pl.multiple_of(slot * BLOCK, BLOCK), BLOCK), :] = rows[b * BLOCK : (b + 1) * BLOCK]
        return carry

    lax.fori_loop(0, q_tiles, tile, 0)

    def pack(c, carry):
        first = placed[pl.ds(pl.multiple_of(c * 2 * BLOCK, BLOCK), BLOCK), :]
        second = placed[pl.ds(pl.multiple_of((c * 2 + 1) * BLOCK, BLOCK), BLOCK), :]
        out_ref[pl.ds(pl.multiple_of(c * BLOCK, BLOCK), BLOCK), :] = jnp.concatenate([first, second], axis=1).astype(BF)
        return carry

    lax.fori_loop(0, q_ref.shape[0] // (2 * BLOCK), pack, 0)


def attend(core, tables, queries, own, other):
    kslot, qslot, lims, pos, start = tables
    n_q, n_k = queries.shape[0], own.shape[0]
    return pl.pallas_call(
        attend_kernel,
        in_specs=[in_smem()] * 4 + [in_vmem()] * 5,
        out_specs=[in_vmem()] * 3,
        out_shape=[
            jax.ShapeDtypeStruct((n_q // 2, LANES), BF),
            jax.ShapeDtypeStruct((HEAD, n_q), F32),
            jax.ShapeDtypeStruct((1, n_q), F32),
        ],
        scratch_shapes=[
            pltpu.VMEM((n_k, HEAD), BF),
            pltpu.VMEM((HEAD + 16, n_k), BF),
            pltpu.VMEM((n_q, HEAD), F32),
        ],
        compiler_params=params(),
        cost_estimate=pl.CostEstimate(flops=8 * n_q * n_k * HEAD, bytes_accessed=8 << 20, transcendentals=n_q * n_k),
    )(core, kslot, qslot, lims, queries, own, other, pos, start)


def attend_back_kernel(
    core_ref, kslot_ref, qslot_ref, lims_ref, q_ref, own_ref, other_ref, pos_ref, start_ref,
    grad_ref, mixed_ref, lse_ref,
    dq_ref, keep_ref, send_ref,
    keys, values, keys_t, grad_keys, grad_values, grad_placed,
):
    q_tiles = q_ref.shape[0] // QT
    k_tiles = own_ref.shape[0] // KT
    per = KT // BLOCK
    is_first = core_ref[0] == 0
    ones = jnp.ones((BLOCK, HEAD), BF)

    def load(t, carry):
        for b in range(per):
            slot = kslot_ref[t * per + b]
            own = block_rows(own_ref, slot)[:, HEAD:]
            other = block_rows(other_ref, slot)[:, HEAD:]
            at = pl.ds(pl.multiple_of((t * per + b) * BLOCK, BLOCK), BLOCK)
            key = jnp.where(is_first, own, other)
            value = jnp.where(is_first, other, own)
            keys[at, :] = jnp.concatenate([key, ones], axis=1)
            values[at, :] = jnp.concatenate([value, ones], axis=1)
            keys_t[:, at] = key.astype(F32).T.astype(BF)
            grad_keys[at, :] = jnp.zeros((BLOCK, HEAD), F32)
            grad_values[at, :] = jnp.zeros((BLOCK, HEAD), F32)
        return carry

    lax.fori_loop(0, k_tiles, load, 0)

    def unpack(c, carry):
        pair = grad_ref[pl.ds(pl.multiple_of(c * BLOCK, BLOCK), BLOCK), :]
        grad_placed[pl.ds(pl.multiple_of(c * 2 * BLOCK, BLOCK), BLOCK), :] = pair[:, :HEAD]
        grad_placed[pl.ds(pl.multiple_of((c * 2 + 1) * BLOCK, BLOCK), BLOCK), :] = pair[:, HEAD:]
        return carry

    lax.fori_loop(0, q_ref.shape[0] // (2 * BLOCK), unpack, 0)

    def tile(i, carry):
        cols = pl.ds(pl.multiple_of(i * QT, QT), QT)
        slots = [qslot_ref[i * (QT // BLOCK) + b] for b in range(QT // BLOCK)]
        query_f = jnp.concatenate([block_rows(q_ref, s)[:, :HEAD] for s in slots], axis=0).astype(F32) * SCALE
        grad = jnp.concatenate([block_rows(grad_placed, s) for s in slots], axis=0)
        query = query_f.astype(BF)
        grad_t = grad.astype(F32).T
        delta = jnp.sum(grad_t * mixed_ref[:, cols], axis=0, keepdims=True)
        pad = jnp.zeros((HEAD - 3, QT), F32)
        query_t = jnp.concatenate(
            [query_f.T] + [e.astype(F32) for e in sum_of_parts(-lse_ref[:, cols])] + [pad], axis=0
        ).astype(BF)
        grad_t = jnp.concatenate([grad_t] + [e.astype(F32) for e in sum_of_parts(-delta)] + [pad], axis=0).astype(BF)
        pos_row = pos_ref[:, cols]
        start_row = start_ref[:, cols]

        def step(masked, j, acc):
            at = pl.ds(pl.multiple_of(j * KT, KT), KT)
            p = jnp.exp(dot(keys[at, :], query_t))
            if masked:
                p = jnp.where(allowed_pairs(j, pos_row, start_row), p, 0.0)
            grad_s = (p * dot(values[at, :], grad_t)).astype(BF)
            grad_values[at, :] += dot(p.astype(BF), grad)
            grad_keys[at, :] += dot(grad_s, query)
            return acc + dot(keys_t[:, at], grad_s)

        acc = walk_keys(lims_ref, i, step, jnp.zeros((HEAD, QT), F32))
        rows = (acc * SCALE).T
        rows = jnp.concatenate([rows, jnp.zeros((QT, HEAD), F32)], axis=1)
        for b in range(QT // BLOCK):
            dq_ref[pl.ds(pl.multiple_of(slots[b] * BLOCK, BLOCK), BLOCK), :] = rows[b * BLOCK : (b + 1) * BLOCK]
        return carry

    lax.fori_loop(0, q_tiles, tile, 0)

    def place(t, carry):
        zeros = jnp.zeros((BLOCK, HEAD), F32)
        for b in range(per):
            slot = kslot_ref[t * per + b]
            at = pl.ds(pl.multiple_of((t * per + b) * BLOCK, BLOCK), BLOCK)
            to = pl.ds(pl.multiple_of(slot * BLOCK, BLOCK), BLOCK)
            key, value = grad_keys[at, :], grad_values[at, :]
            mine = jnp.where(is_first, key, value)
            theirs = jnp.where(is_first, value, key)
            keep_ref[to, :] = jnp.concatenate([zeros, mine], axis=1)
            send_ref[to, :] = jnp.concatenate([zeros, theirs], axis=1).astype(BF)
        return carry

    lax.fori_loop(0, k_tiles, place, 0)


def attend_back(core, tables, queries, own, other, grads, mixed, lse):
    kslot, qslot, lims, pos, start = tables
    n_q, n_k = queries.shape[0], own.shape[0]
    return pl.pallas_call(
        attend_back_kernel,
        in_specs=[in_smem()] * 4 + [in_vmem()] * 8,
        out_specs=[in_vmem()] * 3,
        out_shape=[
            jax.ShapeDtypeStruct((n_q, LANES), F32),
            jax.ShapeDtypeStruct((n_k, LANES), F32),
            jax.ShapeDtypeStruct((n_k, LANES), BF),
        ],
        scratch_shapes=[
            pltpu.VMEM((n_k, LANES), BF),
            pltpu.VMEM((n_k, LANES), BF),
            pltpu.VMEM((HEAD, n_k), BF),
            pltpu.VMEM((n_k, HEAD), F32),
            pltpu.VMEM((n_k, HEAD), F32),
            pltpu.VMEM((n_q, HEAD), BF),
        ],
        compiler_params=params(),
        cost_estimate=pl.CostEstimate(flops=16 * n_q * n_k * HEAD, bytes_accessed=8 << 20, transcendentals=n_q * n_k),
    )(core, kslot, qslot, lims, queries, own, other, pos, start, grads, mixed, lse)


def feed_kernel(n_parts, chunk, chunks, blocks, has_acc, final, n_ref, nt_ref, c_ref, ct_ref, *refs):
    parts, refs = refs[:n_parts], refs[n_parts:]
    if has_acc:
        (out_in_ref, back_in_ref), refs = refs[:2], refs[2:]
    keep_ref, send_ref, out_ref, final_ref = refs[:4]
    back_ref = refs[4] if final else final_ref
    width = n_ref.shape[1]
    tile = parts[0].shape[1] // 3
    length = parts[0].shape[0]
    places = []
    for p in range(n_parts):
        for at in range(0, length, chunk):
            places.append((p, at, chunks[(p * length + at) // chunk] * chunk))

    @pl.when(pl.program_id(0) == 0)
    def _():
        if has_acc:
            out_ref[...] = out_in_ref[...]
            back_ref[...] = back_in_ref[...]
        else:
            out_ref[...] = jnp.zeros_like(out_ref)
            back_ref[...] = jnp.zeros_like(back_ref)

    both = down = None
    for p in range(n_parts):
        tos = [to for q, _, to in places if q == p]
        left_n = jnp.concatenate([n_ref[:, to : to + chunk] for to in tos], axis=1)
        left_c = jnp.concatenate([c_ref[:, to : to + chunk] for to in tos], axis=1)
        term = dot(left_n, parts[p][:, : 2 * tile])
        other = dot(left_c, parts[p][:, 2 * tile :])
        both = term if both is None else both + term
        down = other if down is None else down + other
    gate, up = both[:, :tile], both[:, tile:]
    sig = 1.0 / (1.0 + jnp.exp(-gate))
    silu = gate * sig
    mid = (silu * up).astype(BF)
    grad_gate = (down * up * (sig * (1.0 + gate * (1.0 - sig)))).astype(BF)
    grad_up = (down * silu).astype(BF)
    grads = jnp.concatenate([grad_gate, grad_up], axis=1)
    for p in range(n_parts):
        out = dot(mid, parts[p][:, 2 * tile :], NT)
        back = dot(grads, parts[p][:, : 2 * tile], NT)
        for q, at, to in places:
            if q == p:
                out_ref[:, to : to + chunk] += out[:, at : at + chunk]
                back_ref[:, to : to + chunk] += back[:, at : at + chunk]
    if final:

        @pl.when(pl.program_id(0) == pl.num_programs(0) - 1)
        def _():
            final_ref[...] = back_ref[...].astype(BF)

    unit = width // len(blocks)
    per = 256 // unit
    half = len(blocks) // 2
    for k in range(0, len(blocks), per):
        left_n = jnp.concatenate([nt_ref[b * unit : (b + 1) * unit, :] for b in blocks[k : k + per]], axis=0)
        left_c = jnp.concatenate([ct_ref[b * unit : (b + 1) * unit, :] for b in blocks[k : k + per]], axis=0)
        ref, row = (keep_ref, k) if k < half else (send_ref, k - half)
        ref[row * unit : row * unit + 256, : 2 * tile] = dot(left_n, grads).astype(BF)
        ref[row * unit : row * unit + 256, 2 * tile :] = dot(left_c, mid).astype(BF)


def feed(n, n_t, c, c_t, parts, chunk, chunks, blocks, acc, tile, final):
    rows, width = n.shape
    cols = parts[0].shape[1]
    whole = lambda shape: pl.BlockSpec(shape, lambda i: (0, 0))
    cut = lambda height: pl.BlockSpec((height, 3 * tile), lambda i: (0, i))
    acc = [] if acc is None else list(acc)
    return pl.pallas_call(
        functools.partial(feed_kernel, len(parts), chunk, chunks, blocks, bool(acc), final),
        grid=(cols // (3 * tile),),
        in_specs=[whole((rows, width)), whole((width, rows))] * 2
        + [cut(p.shape[0]) for p in parts]
        + [whole((rows, width))] * len(acc),
        out_specs=[cut(width // 2)] * 2 + [whole((rows, width))] * 2,
        out_shape=[jax.ShapeDtypeStruct((width // 2, cols), BF)] * 2 + [jax.ShapeDtypeStruct((rows, width), F32), jax.ShapeDtypeStruct((rows, width), BF if final else F32)],
        scratch_shapes=[pltpu.VMEM((rows, width), F32)] if final else [],
        compiler_params=params(),
        cost_estimate=pl.CostEstimate(flops=18 * rows * width * cols // 3, bytes_accessed=16 << 20, transcendentals=0),
    )(n, n_t, c, c_t, *parts, *acc)


def prepare_kernel(
    core_ref, table_ref, q_ref, k_ref, v_ref, o_ref, g_ref, u_ref, d_ref, ga_ref, gm_ref, flags_ref,
    mine_q_ref, theirs_q_ref, mine_f_ref, theirs_f_ref,
):
    first = core_ref[0] == 0
    owned, width = q_ref.shape

    def put(mine_ref, theirs_ref, at, zero, one):
        size = zero.shape[1]
        mine_ref[:, at : at + size] = jnp.where(first, zero, one).astype(BF)
        theirs_ref[:, at : at + size] = jnp.where(first, one, zero).astype(BF)

    for g in range(KV_HEADS):
        at = g * LANES
        kv = slice(g * HEAD, (g + 1) * HEAD)
        zero = jnp.concatenate([q_ref[:, at : at + HEAD], k_ref[:, kv]], axis=1)
        one = jnp.concatenate([q_ref[:, at + HEAD : at + LANES], v_ref[:, kv]], axis=1)
        put(mine_q_ref, theirs_q_ref, at, zero, one)
    shape = (owned, owned)
    diagonal = lax.broadcasted_iota(I32, shape, 0) == lax.broadcasted_iota(I32, shape, 1)
    gain_a = jnp.sum(jnp.where(diagonal, ga_ref[...], 0.0), axis=1, keepdims=True)
    gain_m = jnp.sum(jnp.where(diagonal, gm_ref[...], 0.0), axis=1, keepdims=True)
    count = flags_ref.shape[1]
    cols = count // owned
    row = lax.broadcasted_iota(I32, (owned, count), 0)
    col = lax.broadcasted_iota(I32, (owned, count), 1)
    spread = jnp.where(col // cols == row, flags_ref[...].astype(F32), 0.0).astype(BF)
    row = lax.broadcasted_iota(I32, (count, LANES), 0)
    col = lax.broadcasted_iota(I32, (count, LANES), 1)
    extra = dot(spread, jnp.where(row % cols == col - 3, 1.0, 0.0).astype(BF))
    row = lax.broadcasted_iota(I32, (owned, LANES), 0)
    col = lax.broadcasted_iota(I32, (owned, LANES), 1)
    blocks = jnp.where(row == 0, table_ref[0, 0], jnp.where(row == 1, table_ref[0, 1], 0)).astype(F32)
    extra = jnp.where(col == 0, gain_a, jnp.where(col == 1, gain_m, jnp.where(col == 2, blocks, extra)))
    put(mine_q_ref, theirs_q_ref, width, extra, extra)
    half = g_ref.shape[1] // 2
    tile = half // TILES
    for t in range(TILES):
        for e, ref in enumerate((g_ref, u_ref, d_ref)):
            at = t * tile
            put(mine_f_ref, theirs_f_ref, (t * 3 + e) * tile, ref[:, at : at + tile], ref[:, half + at : half + at + tile])
    put(mine_q_ref, theirs_q_ref, width + LANES, o_ref[:, : width // 2], o_ref[:, width // 2 :])


def prepare(core, table, *arrays):
    owned, width = arrays[0].shape
    cols = 3 * arrays[4].shape[1] // 2
    return pl.pallas_call(
        prepare_kernel,
        in_specs=[in_smem()] * 2 + [in_vmem()] * len(arrays),
        out_specs=[in_vmem()] * 4,
        out_shape=[jax.ShapeDtypeStruct((owned, width + LANES + width // 2), BF)] * 2 + [jax.ShapeDtypeStruct((owned, cols), BF)] * 2,
        compiler_params=params(),
    )(core, table, *arrays)


def deliver_kernel(core_ref, a_ref, b_ref, c_ref, other_ref, gate_ref, up_ref, down_ref):
    first = core_ref[0] == 0
    owned, half = gate_ref.shape[0], gate_ref.shape[1] // 2
    tile = half // TILES
    per = TILES // 3
    for t in range(TILES):
        part = (a_ref, b_ref, c_ref)[t // per]
        for e, out in enumerate((gate_ref, up_ref, down_ref)):
            at = ((t % per) * 3 + e) * tile
            kept = jnp.where(first, part[:owned, at : at + tile], part[owned:, at : at + tile])
            arrived = other_ref[:, (t * 3 + e) * tile : (t * 3 + e + 1) * tile]
            out[:, t * tile : (t + 1) * tile] = jnp.where(first, kept, arrived)
            out[:, half + t * tile : half + (t + 1) * tile] = jnp.where(first, arrived, kept)


def deliver(core, parts, other):
    owned, cols = other.shape
    return pl.pallas_call(
        deliver_kernel,
        in_specs=[in_smem()] + [in_vmem()] * 4,
        out_specs=[in_vmem()] * 3,
        out_shape=[jax.ShapeDtypeStruct((owned, 2 * cols // 3), F32)] * 3,
        compiler_params=params(),
    )(core, *parts, other)


def deliver_heads_kernel(core_ref, qkv_ref, out_ref, other_ref, wo_ref, q_ref, k_ref, v_ref):
    first = core_ref[0] == 0
    owned, width = q_ref.shape
    half = width // 2

    def sides(ref, at, size, shift):
        kept = jnp.where(first, ref[:owned, at : at + size], ref[owned:, at : at + size])
        arrived = other_ref[:, shift + at : shift + at + size]
        return jnp.where(first, kept, arrived), jnp.where(first, arrived, kept)

    wo_ref[:, :half], wo_ref[:, half:] = sides(out_ref, 0, half, width)
    for g in range(0, KV_HEADS, 2):
        zero, one = sides(qkv_ref, g * LANES, LANES, 0)
        zero_next, one_next = sides(qkv_ref, (g + 1) * LANES, LANES, 0)
        q_ref[:, g * LANES : (g + 1) * LANES] = jnp.concatenate([zero[:, :HEAD], one[:, :HEAD]], axis=1)
        q_ref[:, (g + 1) * LANES : (g + 2) * LANES] = jnp.concatenate([zero_next[:, :HEAD], one_next[:, :HEAD]], axis=1)
        k_ref[:, g * HEAD : (g + 2) * HEAD] = jnp.concatenate([zero[:, HEAD:], zero_next[:, HEAD:]], axis=1)
        v_ref[:, g * HEAD : (g + 2) * HEAD] = jnp.concatenate([one[:, HEAD:], one_next[:, HEAD:]], axis=1)


def deliver_heads(core, qkv, out, other):
    owned, width = other.shape[0], qkv.shape[1]
    shapes = [(owned, width), (owned, width), (owned, width // 2), (owned, width // 2)]
    return pl.pallas_call(
        deliver_heads_kernel,
        in_specs=[in_smem()] + [in_vmem()] * 3,
        out_specs=[in_vmem()] * 4,
        out_shape=[jax.ShapeDtypeStruct(e, F32) for e in shapes],
        compiler_params=params(),
    )(core, qkv, out, other)


def leave_kernel(own_ref, other_ref, x_ref, wo_ref, gain_ref, res_ref, n_ref, nt_ref, attn_ref):
    half = KV_HEADS * HEAD
    for which, ref in enumerate((own_ref, other_ref)):
        for g in range(0, KV_HEADS, 2):
            for s in range(2):
                for j in range(2):
                    lanes = slice(j * HEAD, (j + 1) * HEAD)
                    a = ref[(g * 2 + s) * BLOCK : (g * 2 + s + 1) * BLOCK, lanes]
                    b = ref[((g + 1) * 2 + s) * BLOCK : ((g + 1) * 2 + s + 1) * BLOCK, lanes]
                    row, col = (s * 2 + j) * BLOCK, which * half + g * HEAD
                    attn_ref[row : row + BLOCK, col : col + LANES] = jnp.concatenate([a, b], axis=1)
    value = x_ref[...].astype(F32) + dot(attn_ref[...], wo_ref[...])
    res_ref[...] = value
    inverse = lax.rsqrt(jnp.mean(value * value, axis=-1, keepdims=True) + EPS)
    normed = (value * inverse * gain_ref[...]).astype(BF)
    n_ref[...] = normed
    nt_ref[...] = normed.T


def leave(own, other, x, wo, gain):
    rows, width = x.shape
    return pl.pallas_call(
        leave_kernel,
        in_specs=[in_vmem()] * 5,
        out_specs=[in_vmem()] * 4,
        out_shape=[
            jax.ShapeDtypeStruct((rows, width), F32),
            jax.ShapeDtypeStruct((rows, width), BF),
            jax.ShapeDtypeStruct((width, rows), BF),
            jax.ShapeDtypeStruct((rows, width), BF),
        ],
        compiler_params=params(),
        cost_estimate=pl.CostEstimate(flops=2 * rows * width * width, bytes_accessed=10 << 20, transcendentals=0),
    )(own, other, x, wo, gain)


def enter_kernel(back_ref, other_ref, res_ref, c_ref, gain_ref, wo_ref, grad_ref, grad_b_ref, gain_out_ref, out_ref):
    value = res_ref[...]
    inverse = lax.rsqrt(jnp.mean(value * value, axis=-1, keepdims=True) + EPS)
    grad = back_ref[...].astype(F32) + other_ref[...].astype(F32)
    gain_out_ref[...] = jnp.sum(grad * value * inverse, axis=0, keepdims=True)
    scaled = grad * gain_ref[...]
    mean = jnp.mean(scaled * value, axis=-1, keepdims=True)
    total = c_ref[...].astype(F32) + (inverse * scaled - value * (inverse * inverse * inverse) * mean)
    grad_ref[...] = total
    grad_b_ref[...] = total.astype(BF)
    heads = dot(grad_b_ref[...], wo_ref[: KV_HEADS * HEAD, :], NT).astype(BF)
    for g in range(KV_HEADS):
        for s in range(2):
            row = s * 2 * BLOCK
            lanes = slice(g * HEAD, (g + 1) * HEAD)
            out_ref[(g * 2 + s) * BLOCK : (g * 2 + s + 1) * BLOCK, :] = jnp.concatenate(
                [heads[row : row + BLOCK, lanes], heads[row + BLOCK : row + 2 * BLOCK, lanes]], axis=1
            )


def enter(back, other, residual, c, gain, wo):
    rows, width = residual.shape
    return pl.pallas_call(
        enter_kernel,
        in_specs=[in_vmem()] * 6,
        out_specs=[in_vmem()] * 4,
        out_shape=[
            jax.ShapeDtypeStruct((rows, width), F32),
            jax.ShapeDtypeStruct((rows, width), BF),
            jax.ShapeDtypeStruct((1, width), F32),
            jax.ShapeDtypeStruct((2 * KV_HEADS * BLOCK, LANES), BF),
        ],
        compiler_params=params(),
        cost_estimate=pl.CostEstimate(flops=rows * width * width, bytes_accessed=10 << 20, transcendentals=0),
    )(back, other, residual, c, gain, wo)


def rms(value, gain):
    inverse = lax.rsqrt(jnp.mean(value * value, axis=-1, keepdims=True) + EPS)
    return value * inverse * gain, inverse


def rms_back(value, inverse, gain, grad):
    scaled = grad * gain
    mean = jnp.mean(scaled * value, axis=-1, keepdims=True)
    moved = inverse * scaled - value * (inverse * inverse * inverse) * mean
    return moved, jnp.sum(grad * value * inverse, axis=0)


def rope_tables(positions):
    inv_freq = jnp.power(F32(1000000.0), -(2.0 * jnp.arange(HEAD // 2, dtype=F32)) / HEAD)
    angles = positions.astype(F32)[:, None] * inv_freq[None, :]
    cosine, sine = jnp.cos(angles), jnp.sin(angles)
    return (
        jnp.concatenate([cosine] * 4, axis=1),
        jnp.concatenate([-sine, sine, -sine, sine], axis=1),
    )


class Dim:
    def __init__(self, stride, size):
        self.stride, self.size = stride, size


def make_shards(n):
    if n == 16:
        dims = {"x": Dim(1, 2), "y": Dim(2, 2), "p": Dim(4, 2), "q": Dim(8, 2)}
        order_a, order_b, order_c = "qpxy", "qpyx", "qxyp"
    else:
        names = "abcdefghijkl"[: n.bit_length() - 1]
        dims = {name: Dim(1 << b, 2) for b, name in enumerate(names)}
        order_a = order_b = order_c = names
    groups = n // 16
    a2a_groups = None if groups == 1 else [[t * 16 + d for d in range(16)] for t in range(groups)]
    kv_groups = None if groups == 1 else [[t * 16 + d for t in range(groups)] for d in range(16)]

    def digits(order):
        places = []
        for r in range(n):
            place = {}
            for name in order:
                place[name] = r % dims[name].size
                r //= dims[name].size
            places.append(place)
        return places

    def place_in(order):
        found = {tuple(sorted(p.items())): r for r, p in enumerate(digits(order))}
        return [found[tuple(sorted(p.items()))] for p in digits(order_a)]

    def chips(me, order):
        out = []
        for place in digits(order):
            chip = me
            for name, digit in place.items():
                d = dims[name]
                at = (me // d.stride) % d.size
                to = jnp.bitwise_xor(at, digit)
                chip = chip + (to - at) * d.stride
            out.append(chip)
        return jnp.stack(out).astype(I32)

    def ctx_send(value, pairs):
        return lax.ppermute(value, "ctx", pairs)

    def ctx_swap(value, stride):
        return ctx_send(value, [(i, i ^ stride) for i in range(n)])

    def core_swap(value):
        return lax.ppermute(value, "wt", [(0, 1), (1, 0)])

    def gather_dim(value, name):
        return [value, ctx_swap(value, dims[name].stride)]

    def join(parts):
        return parts[0] if len(parts) == 1 else jnp.concatenate(parts, axis=0)

    def gather_rows(parts, names):
        for name in names:
            parts = gather_dim(join(parts), name)
        return parts

    def hold(parts, *others):
        return parts[:-1] + [after(parts[-1], *others)]

    def scatter_begin(keep, send, name):
        return keep, ctx_swap(send.astype(BF), dims[name].stride)

    def scatter_next(state, name):
        keep, arrived = state
        half = keep.shape[0] // 2
        send = (keep[half:].astype(F32) + arrived[half:].astype(F32)).astype(BF)
        return keep[:half].astype(F32) + arrived[:half].astype(F32), ctx_swap(send, dims[name].stride)

    def scatter_end(state):
        keep, arrived = state
        return keep.astype(F32) + arrived.astype(F32)

    def scatter_rows(keep, send, names):
        state = scatter_begin(keep, send, names[-1])
        for name in reversed(names[:-1]):
            state = scatter_next(state, name)
        return scatter_end(state)

    def scatter_whole(value, names):
        half = value.shape[0] // 2
        return scatter_rows(value[:half], value[half:], names)

    def runs(places):
        out = []
        for p in places:
            if out and out[-1][1] == p:
                out[-1][1] = p + 1
            else:
                out.append([p, p + 1])
        return out

    def assemble(parts, order):
        total = sum(p.shape[0] for p in parts)
        unit, each = total // n, parts[0].shape[0] // (total // n)
        out = []
        for lo, hi in runs(place_in(order)):
            while lo < hi:
                part, at = lo // each, lo % each
                stop = min(hi, (part + 1) * each)
                out.append(parts[part][at * unit : (at + stop - lo) * unit])
                lo = stop
        return join(out)

    def columns_in(value, order):
        unit = value.shape[1] // n
        inverse = np.argsort(place_in(order)).tolist()
        pieces = [value[:, lo * unit : hi * unit] for lo, hi in runs(inverse)]
        return pieces[0] if len(pieces) == 1 else jnp.concatenate(pieces, axis=1)

    def after(value, *others):
        return lax.optimization_barrier((value,) + others)[0]

    def swap_heads(value):
        return lax.all_to_all(value, "ctx", 0, 0, axis_index_groups=a2a_groups, tiled=True)

    def shards(
        tokens, block_table, doc_flags, w_query, key_weight, value_weight, w_out, w_gate, w_up, w_down,
        gain_attn, gain_mlp, gain_q, key_norm_gain, cotangent,
    ):
        width = tokens.shape[-1]
        rows = tokens.shape[1]
        owned = w_query.shape[0]
        chip_rows = 2 * owned
        me = lax.axis_index("ctx")
        core = lax.axis_index("wt")
        first = core == 0
        core_arr = core.astype(I32).reshape(1)
        slots_n = 2 * n

        def by_core(a, b, axis=0):
            return jnp.where(first, jnp.concatenate([a, b], axis=axis), jnp.concatenate([b, a], axis=axis))

        def pick(a, b):
            return jnp.where(first, a, b)

        chip_of = chips(me, order_a)

        def features(order):
            return (chips(me, order)[:, None] * chip_rows + jnp.arange(chip_rows, dtype=I32)[None, :]).reshape(-1)

        def spread(order):
            return (jnp.arange(width, dtype=I32)[:, None] == features(order)[None, :]).astype(BF)

        canon = features(order_a)
        perm = spread(order_a)

        flag_cols = rows // owned
        own_blocks = block_table[0]
        mine_q, theirs_q, mine_f, theirs_f = prepare(
            core_arr, block_table, w_query, key_weight, value_weight, w_out, w_gate, w_up, w_down,
            gain_attn[None, :], gain_mlp[None, :], doc_flags,
        )
        first_piece = by_core(mine_q, core_swap(theirs_q))
        acts = jnp.stack([tokens[0], cotangent[0]])
        acts_other = core_swap(acts)
        other_f = core_swap(theirs_f)
        x_two = dot(by_core(acts[0], acts_other[0]), perm).astype(BF)
        c_two = dot(by_core(acts[1], acts_other[1]), perm).astype(BF)
        head_cols = width // 2
        out_cols = width // 4
        out_at = width + LANES

        def cut(value):
            first_cols = [value[:, :head_cols], value[:, width:out_at], value[:, out_at : out_at + out_cols]]
            second_cols = [value[:, head_cols:width], value[:, out_at + out_cols :]]
            return [jnp.concatenate(first_cols, axis=1)], [jnp.concatenate(second_cols, axis=1)]

        if n == 16:
            shared = cut(join(gather_rows([first_piece], "qp")))
            qkv_parts = [gather_rows(shared[0], "x"), gather_rows(shared[1], "y")]
            first_swap = qkv_parts[0][-1]
            qkv_parts = [gather_rows(hold(qkv_parts[0], x_two), "y"), gather_rows(qkv_parts[1], "x")]
        else:
            shared = cut(first_piece)
            qkv_parts = [gather_rows(shared[0], order_a), gather_rows(shared[1], order_b)]
            first_swap = first_piece
        chunk = LANES
        per = chunk // chip_rows
        chunk_orders = [[e // per for e in np.argsort(place_in(o)).tolist()[::per]] for o in (order_a, order_b, order_c)]
        extras = assemble([p[:, head_cols : head_cols + LANES] for p in qkv_parts[0]], order_a).astype(F32)
        wo_half = jnp.concatenate(
            [
                assemble([p[:, head_cols + LANES :] for p in qkv_parts[0]], order_a),
                assemble([p[:, head_cols:] for p in qkv_parts[1]], order_b),
            ],
            axis=1,
        )

        hidden = x_two.astype(F32)

        ff_half = w_gate.shape[1] // 2
        tile = ff_half // TILES
        piece_cols = ff_half
        orders = (order_a, order_b, order_c)
        other_f = after(other_f, first_swap)

        def feed_piece(lo, hi):
            return by_core(mine_f[:, lo:hi], other_f[:, lo:hi])

        feed_parts = [
            gather_rows([feed_piece(e * piece_cols, (e + 1) * piece_cols)], orders[e][:1]) for e in range(3)
        ]

        gain_a, gain_m = extras[:, 0][None, :], extras[:, 1][None, :]
        per_chip = extras.reshape(n, 2, owned, LANES)
        block_of = per_chip[:, 0, :2, 2].reshape(-1).astype(I32)
        seq = me % 2
        flags = jnp.where(seq == 0, per_chip[:, 0], per_chip[:, 1])[:, :, 3 : 3 + flag_cols].reshape(slots_n, BLOCK)
        slot_of = (chip_of[:, None] * 2 + jnp.arange(2, dtype=I32)[None, :]).reshape(-1)
        ids = jnp.arange(slots_n, dtype=I32)
        hit = ids[:, None] == block_of[None, :]
        flags_pos = dot(hit.astype(BF), flags.astype(BF))
        kslot = jnp.sum(jnp.where(hit, slot_of[None, :], 0), axis=1)
        pos = jnp.arange(slots_n * BLOCK, dtype=I32).reshape(slots_n, BLOCK)
        begins = jnp.where(flags_pos > 0.5, pos, -1)
        lane = jnp.arange(BLOCK, dtype=I32)
        inside = jnp.max(jnp.where(lane[None, None, :] <= lane[None, :, None], begins[:, None, :], -1), axis=2)
        carried = jnp.max(jnp.where(ids[None, :] < ids[:, None], jnp.max(begins, axis=1)[None, :], -1), axis=1)
        doc_start = jnp.maximum(inside, carried[:, None])
        here = (slot_of // 32) == (me // 16)
        rank = jnp.sum((here[None, :] & (block_of[None, :] < block_of[:, None])).astype(I32), axis=1)
        hit_q = here[None, :] & (rank[None, :] == jnp.arange(32, dtype=I32)[:, None])
        q_block = jnp.sum(jnp.where(hit_q, block_of[None, :], 0), axis=1)
        qslot = jnp.sum(jnp.where(hit_q, slot_of[None, :] - (me // 16) * 32, 0), axis=1)
        q_pos = q_block[:, None] * BLOCK + lane[None, :]
        q_start = jnp.sum(jnp.where((q_block[:, None] == ids[None, :])[:, :, None], doc_start[None], 0), axis=1)
        n_q = 32 * BLOCK
        tile_start = q_start.reshape(n_q // QT, QT)
        tile_pos = q_pos.reshape(n_q // QT, QT)
        low, high = jnp.min(tile_start, axis=1) // KT, jnp.max(tile_pos, axis=1) // KT + 1
        full_low = jnp.minimum((jnp.max(tile_start, axis=1) + KT - 1) // KT, high)
        full_high = jnp.maximum(jnp.minimum((jnp.min(tile_pos, axis=1) + 1) // KT, high), full_low)
        lims = jnp.stack([low, full_low, full_high, high])
        tables = (kslot, qslot, lims, q_pos.reshape(1, n_q), q_start.reshape(1, n_q))

        own_pos = (own_blocks[:, None] * BLOCK + lane[None, :]).reshape(-1)
        cosine, sine = rope_tables(own_pos)
        gain_qk = jnp.concatenate([gain_q, key_norm_gain])[None, :]

        normed_ab, raw, packed = project(
            core_arr, x_two, gain_a, gain_qk, cosine, sine, qkv_parts, chunk, chunk_orders
        )
        feed_parts = [gather_rows(hold(feed_parts[e], packed), orders[e][1:]) for e in range(3)]
        queries = swap_heads(packed.reshape(16, rows, LANES)).reshape(n_q, LANES)
        own_kv = queries
        if groups > 1:
            own_kv = lax.all_gather(queries, "ctx", axis=0, tiled=True, axis_index_groups=kv_groups)
        other_kv = core_swap(own_kv)
        wo_other = core_swap(wo_half)
        wo_full = by_core(wo_half, wo_other, axis=1)
        head_ids = jnp.arange(width, dtype=I32)
        place = (head_ids // 512).astype(I32)
        head_row = (((head_ids % 512) // HEAD) * 2 + jnp.bitwise_xor(core.astype(I32), place)) * HEAD + head_ids % HEAD
        select = (head_row[:, None] == canon[None, :]).astype(BF)
        wo_sel = dot(select, dot(wo_full, perm).astype(BF)).astype(BF)

        other_kv = after(other_kv, wo_sel)
        mixed_packed, mixed, lse = attend(core_arr, tables, queries, own_kv, other_kv)

        attn_own = swap_heads(mixed_packed.reshape(16, BLOCK, LANES)).reshape(16 * BLOCK, LANES)
        residual, normed_mb, n_t, attn = leave(attn_own, core_swap(attn_own), x_two, wo_sel, gain_m)

        c_t = c_two.T
        acc, feed_sums = None, []
        for e in range(3):
            blocks = np.argsort(place_in(orders[e])).tolist()
            keep, send, *acc = feed(
                normed_mb, n_t, c_two, c_t, feed_parts[e], chunk, chunk_orders[e], blocks, acc, tile, e == 2
            )
            feed_sums.append(scatter_begin(keep, send, orders[e][-1]))
        mlp_part, grad_n2_part = acc
        grad_h, grad_hb, grad_gm, do_packed = enter(
            grad_n2_part, core_swap(grad_n2_part), residual, c_two, gain_m, wo_sel
        )
        grads_in = swap_heads(do_packed.reshape(16, BLOCK, LANES)).reshape(n_q // 2, LANES)
        attn = after(attn, do_packed)

        mlp_other = core_swap(pick(mlp_part[rows:], mlp_part[:rows]))
        layer_rel = pick(residual[:rows], residual[rows:]) + (pick(mlp_part[:rows], mlp_part[rows:]) + mlp_other)
        layer_out = dot(layer_rel.astype(BF), perm, NT).astype(BF)[None]

        attn_rel = dot(attn, select).astype(BF)
        grad_hc = dot(grad_hb, pick(perm[: width // 2], perm[width // 2 :]), NT).astype(BF)
        out_first = dot(attn_rel, grad_hc[:, :out_cols], TN).astype(BF)
        out_second = dot(columns_in(attn_rel, order_b), grad_hc[:, out_cols:], TN).astype(BF)

        dq, keep, send = attend_back(core_arr, tables, queries, own_kv, other_kv, grads_in, mixed, lse)
        feed_sums = [scatter_next(hold(list(feed_sums[e]), send), orders[e][-2]) for e in range(3)]
        grad_kv = keep + core_swap(send).astype(F32)
        if groups > 1:
            grad_kv = lax.psum_scatter(grad_kv, "ctx", scatter_dimension=0, tiled=True, axis_index_groups=kv_groups)
        back = swap_heads((dq + grad_kv).astype(BF).reshape(16, rows, LANES))
        grad_qkv_in, gain_parts = unproject(core_arr, back.reshape(KV_HEADS, 2, rows, LANES), raw, gain_qk, cosine, sine)
        g_first, g_second = grad_qkv_in[:, : width // 2], grad_qkv_in[:, width // 2 :]

        def halves(value):
            half = value.shape[0] // 2
            return value[:half], value[half:]

        sum_first = jnp.concatenate([dot(normed_ab, g_first, TN).astype(BF), out_first], axis=1)
        sum_second = jnp.concatenate([dot(columns_in(normed_ab, order_b), g_second, TN).astype(BF), out_second], axis=1)
        level_holds = {}
        if n == 16:
            sum_first = scatter_begin(*halves(sum_first), "y")
            sum_second = scatter_begin(*halves(sum_second), "x")
            level_holds[3] = sum_first[1], sum_second[1]
            sum_first = scatter_next(sum_first, "x")
            sum_second = scatter_next(sum_second, "y")
            level_holds[4] = sum_first[1], sum_second[1]
            sums = jnp.concatenate([scatter_end(sum_first), scatter_end(sum_second)], axis=1)
            sums = scatter_whole(sums, "qp")
        else:
            sums = jnp.concatenate([scatter_whole(sum_first, order_a), scatter_whole(sum_second, order_b)], axis=1)
        cut_cols = head_cols + out_cols
        part_qkv = jnp.concatenate([sums[:, :head_cols], sums[:, cut_cols : cut_cols + head_cols]], axis=1)
        part_out = jnp.concatenate([sums[:, head_cols:cut_cols], sums[:, cut_cols + head_cols :]], axis=1)
        w_first = assemble([p[:, : width // 2] for p in qkv_parts[0]], order_a)
        w_second = assemble([p[:, : width // 2] for p in qkv_parts[1]], order_b)
        n1_part = dot(g_first, w_first, NT) + dot(g_second, w_second, NT)
        n1_other = core_swap(pick(n1_part[rows:], n1_part[:rows]))
        grad_n1 = pick(n1_part[:rows], n1_part[rows:]) + n1_other

        def mine(value):
            return pick(value[:rows], value[rows:])

        x_mine = mine(hidden)
        _, inv_a = rms(x_mine, gain_a)
        moved_a, grad_ga = rms_back(x_mine, inv_a, gain_a, grad_n1)
        grad_in_rel = mine(grad_h) + moved_a
        in_hi = grad_in_rel.astype(BF)
        in_lo = (grad_in_rel - in_hi.astype(F32)).astype(BF)
        grad_input = (dot(in_hi, perm, NT) + dot(in_lo, perm, NT))[None]

        vectors = jnp.stack([grad_ga, jnp.where(first, grad_gm[0], 0.0)])
        vectors = lax.dot_general(
            vectors, perm.astype(F32), NT, precision=lax.Precision.HIGHEST, preferred_element_type=F32
        )
        for level in range(3, len(order_a) + 1):
            if level == 3:
                feed_sums = [hold(list(v), *level_holds.get(3, (grad_qkv_in,))) for v in feed_sums]
            if level == 4:
                feed_sums = [hold(list(v), vectors, *level_holds.get(4, ())) for v in feed_sums]
            feed_sums = [scatter_next(feed_sums[e], orders[e][-level]) for e in range(3)]
        feed_sums = [scatter_end(v) for v in feed_sums]
        heads_gain = jnp.sum(gain_parts[:, 0], axis=0)
        small = jnp.concatenate([vectors.reshape(-1, LANES), heads_gain[None], jnp.zeros((7, LANES), F32)])
        for bit in range(n.bit_length() - 1):
            small = small + ctx_swap(small, 1 << bit)
        small = small + core_swap(small)
        my_row = (me * 2 + core) * owned
        gains = small[: 2 * width // LANES].reshape(2, width)
        gains = lax.dynamic_slice_in_dim(gains, my_row, owned, axis=1)

        def theirs(parts):
            return jnp.concatenate([pick(p[owned:], p[:owned]) for p in parts], axis=1)

        grad_gate, grad_up, grad_down = deliver(core_arr, feed_sums, core_swap(theirs(feed_sums)))
        grad_wout, grad_query, grad_key, grad_value = deliver_heads(
            core_arr, part_qkv, part_out, core_swap(theirs([part_qkv, part_out]))
        )
        return (
            layer_out,
            grad_input,
            grad_query,
            grad_key,
            grad_value,
            grad_wout,
            grad_gate,
            grad_up,
            grad_down,
            gains[0],
            gains[1],
            small[2 * width // LANES, :HEAD],
            small[2 * width // LANES, HEAD:],
        )

    return shards


def solution(mesh):
    seq = P("wt", "ctx", None)
    weight = P(("ctx", "wt"), None)
    vector = P(("ctx", "wt"))
    return jax.shard_map(
        make_shards(mesh.shape["ctx"]),
        mesh=mesh,
        in_specs=(seq, P("ctx", None), P("wt", "ctx")) + (weight,) * 7 + (vector, vector, P(), P(), seq),
        out_specs=(seq, seq) + (weight,) * 7 + (vector, vector, P(), P()),
        check_vma=False,
    )
```

```python
import functools

import jax
import jax.numpy as jnp
import numpy as np
from jax import lax
from jax.experimental import pallas as pl
from jax.experimental.pallas import tpu as pltpu
from jax.sharding import PartitionSpec as P

HEADS = 16
KV_HEADS = 8
HEAD = 64
LANES = 2 * HEAD
BLOCK = 128
EPS = 1e-05
SCALE = HEAD**-0.5
BF = jnp.bfloat16
F32 = jnp.float32
I32 = jnp.int32
QT = 512
KT = 512
VMEM_BYTES = 56 * 1024 * 1024

NN = (((1,), (0,)), ((), ()))
NT = (((1,), (1,)), ((), ()))
TN = (((0,), (0,)), ((), ()))


def dot(a, b, dims=NN):
    return lax.dot_general(a, b, dims, preferred_element_type=F32)


def params(**kw):
    return pltpu.CompilerParams(vmem_limit_bytes=VMEM_BYTES, **kw)


def in_vmem():
    return pl.BlockSpec(memory_space=pltpu.VMEM)


def in_smem():
    return pl.BlockSpec(memory_space=pltpu.SMEM)


def low_lanes(shape):
    return lax.broadcasted_iota(I32, shape, 1) < HEAD


def half_sums(value, low):
    total = jnp.sum(value, axis=-1, keepdims=True)
    first = jnp.sum(jnp.where(low, value, 0.0), axis=-1, keepdims=True)
    return jnp.where(low, first, total - first)


def half_turn(value):
    lane = lax.broadcasted_iota(I32, value.shape, 1)
    first = (lane % HEAD) < HEAD // 2
    return jnp.where(
        first,
        pltpu.roll(value, LANES - HEAD // 2, 1),
        pltpu.roll(value, HEAD // 2, 1),
    )


def project_kernel(n_parts, swaps, core_ref, x_ref, norm_gain_ref, gain_ref, cos_ref, sin_ref, *refs):
    weights, (n_ref, raw_ref, out_ref) = refs[: 2 * n_parts], refs[2 * n_parts :]
    rows = cos_ref.shape[0]
    is_value = core_ref[0] == 1
    x = x_ref[...].astype(F32)
    inverse = lax.rsqrt(jnp.mean(x * x, axis=-1, keepdims=True) + EPS)
    n_ref[...] = (x * inverse * norm_gain_ref[...]).astype(BF)
    groups = KV_HEADS // 2
    for half in range(2):
        total, at = None, 0
        for part in weights[half * n_parts : (half + 1) * n_parts]:
            length = part.shape[0]
            pieces = [n_ref[:, e : e + swaps[2]] for e in swaps[half][at // swaps[2] : (at + length) // swaps[2]]]
            left = pieces[0] if len(pieces) == 1 else jnp.concatenate(pieces, axis=1)
            term = dot(left, part[:, : groups * LANES])
            total = term if total is None else total + term
            at += length
        raw_ref[:, half * groups * LANES : (half + 1) * groups * LANES] = total
    low = low_lanes((rows, LANES))
    turns = jnp.logical_or(low, jnp.logical_not(is_value))
    for g in range(KV_HEADS):
        for s in range(2):
            raw = raw_ref[s * rows : (s + 1) * rows, g * LANES : (g + 1) * LANES]
            inverse = lax.rsqrt(half_sums(raw * raw, low) * (1.0 / HEAD) + EPS)
            normed = raw * inverse * gain_ref[...]
            turned = normed * cos_ref[...] + half_turn(normed) * sin_ref[...]
            out_ref[g, s] = jnp.where(turns, turned, raw).astype(BF)


def project(core, x, norm_gain, gain, cosine, sine, parts, chunk, chunk_orders):
    rows = cosine.shape[0]
    n_parts = len(parts[0])
    swaps = ([c * chunk for c in chunk_orders[0]], [c * chunk for c in chunk_orders[1]], chunk)
    return pl.pallas_call(
        functools.partial(project_kernel, n_parts, swaps),
        in_specs=[in_smem()] + [in_vmem()] * (5 + 2 * n_parts),
        out_specs=[in_vmem()] * 3,
        out_shape=[
            jax.ShapeDtypeStruct(x.shape, BF),
            jax.ShapeDtypeStruct((2 * rows, KV_HEADS * LANES), F32),
            jax.ShapeDtypeStruct((KV_HEADS, 2, rows, LANES), BF),
        ],
        compiler_params=params(),
        cost_estimate=pl.CostEstimate(flops=2 * x.shape[0] * x.shape[1] * KV_HEADS * LANES, bytes_accessed=8 << 20, transcendentals=0),
    )(core, x, norm_gain, gain, cosine, sine, *parts[0], *parts[1])


def unproject_kernel(core_ref, grad_ref, raw_ref, gain_ref, cos_ref, sin_ref, out_ref, gain_out_ref):
    rows = cos_ref.shape[0]
    is_value = core_ref[0] == 1
    for s in range(2):
        raw = raw_ref[s * rows : (s + 1) * rows]
        grad = grad_ref[0, s].astype(F32)
        low = low_lanes(raw.shape)
        inverse = lax.rsqrt(half_sums(raw * raw, low) * (1.0 / HEAD) + EPS)
        back = grad * cos_ref[...] + half_turn(grad * sin_ref[...])
        is_q_or_k = jnp.logical_or(low, jnp.logical_not(is_value))
        gain_rows = jnp.sum(back * raw * inverse, axis=0, keepdims=True)
        scaled = back * gain_ref[...]
        mean = half_sums(scaled * raw, low) * (1.0 / HEAD)
        moved = inverse * scaled - raw * (inverse * inverse * inverse) * mean
        out_ref[s * rows : (s + 1) * rows, :] = jnp.where(is_q_or_k, moved, grad).astype(BF)
        gain_rows = jnp.where(is_q_or_k[:1], gain_rows, 0.0)
        if s == 0:
            total = gain_rows
        else:
            total = total + gain_rows
    gain_out_ref[0] = jnp.broadcast_to(total, (8, LANES))


def unproject(core, grads, raw, gain, cosine, sine):
    rows = cosine.shape[0]
    return pl.pallas_call(
        unproject_kernel,
        grid=(KV_HEADS,),
        in_specs=[
            in_smem(),
            pl.BlockSpec((1, 2, rows, LANES), lambda g: (g, 0, 0, 0)),
            pl.BlockSpec((2 * rows, LANES), lambda g: (0, g)),
            pl.BlockSpec((1, LANES), lambda g: (0, 0)),
            pl.BlockSpec((rows, LANES), lambda g: (0, 0)),
            pl.BlockSpec((rows, LANES), lambda g: (0, 0)),
        ],
        out_specs=[
            pl.BlockSpec((2 * rows, LANES), lambda g: (0, g)),
            pl.BlockSpec((1, 8, LANES), lambda g: (g, 0, 0)),
        ],
        out_shape=[
            jax.ShapeDtypeStruct((2 * rows, KV_HEADS * LANES), BF),
            jax.ShapeDtypeStruct((KV_HEADS, 8, LANES), F32),
        ],
        compiler_params=params(),
        cost_estimate=pl.CostEstimate(flops=1 << 24, bytes_accessed=8 << 20, transcendentals=0),
    )(core, grads, raw, gain, cosine, sine)


def block_rows(ref, slot):
    return ref[pl.ds(pl.multiple_of(slot * BLOCK, BLOCK), BLOCK), :]


def sum_of_parts(value):
    first = value.astype(BF)
    rest = value - first.astype(F32)
    second = rest.astype(BF)
    third = (rest - second.astype(F32)).astype(BF)
    return first, second, third


def allowed_pairs(j, pos_row, start_row):
    key_pos = j * KT + lax.broadcasted_iota(I32, (KT, 1), 0)
    return jnp.logical_and(key_pos <= pos_row, key_pos >= start_row)


def walk_keys(lims_ref, i, step, carry):
    lo, full_lo, full_hi, hi = (lims_ref[e, i] for e in range(4))
    carry = lax.fori_loop(lo, full_lo, functools.partial(step, True), carry)
    carry = lax.fori_loop(full_lo, full_hi, functools.partial(step, False), carry)
    return lax.fori_loop(full_hi, hi, functools.partial(step, True), carry)


def attend_kernel(
    core_ref, kslot_ref, qslot_ref, lims_ref, q_ref, own_ref, other_ref, pos_ref, start_ref,
    out_ref, keep_ref, lse_ref, keys, values_t, placed,
):
    q_tiles = q_ref.shape[0] // QT
    k_tiles = own_ref.shape[0] // KT
    per = KT // BLOCK
    is_first = core_ref[0] == 0
    values_t[HEAD:, :] = jnp.ones((values_t.shape[0] - HEAD, values_t.shape[1]), BF)

    def load(t, carry):
        for b in range(per):
            slot = kslot_ref[t * per + b]
            own = block_rows(own_ref, slot)[:, HEAD:]
            other = block_rows(other_ref, slot)[:, HEAD:]
            at = pl.ds(pl.multiple_of((t * per + b) * BLOCK, BLOCK), BLOCK)
            keys[at, :] = jnp.where(is_first, own, other)
            value = jnp.where(is_first, other, own).astype(F32)
            values_t[:HEAD, at] = value.T.astype(BF)
        return carry

    lax.fori_loop(0, k_tiles, load, 0)

    def tile(i, carry):
        cols = pl.ds(pl.multiple_of(i * QT, QT), QT)
        parts = [block_rows(q_ref, qslot_ref[i * (QT // BLOCK) + b])[:, :HEAD] for b in range(QT // BLOCK)]
        query_t = (jnp.concatenate(parts, axis=0).astype(F32) * SCALE).T.astype(BF)
        pos_row = pos_ref[:, cols]
        start_row = start_ref[:, cols]

        def step(masked, j, acc):
            at = pl.ds(pl.multiple_of(j * KT, KT), KT)
            p = jnp.exp(dot(keys[at, :], query_t))
            if masked:
                p = jnp.where(allowed_pairs(j, pos_row, start_row), p, 0.0)
            return acc + dot(values_t[:, at], p.astype(BF))

        acc = walk_keys(lims_ref, i, step, jnp.zeros((values_t.shape[0], QT), F32))
        total = acc[HEAD : HEAD + 1]
        mixed = acc[:HEAD] / total
        keep_ref[:, cols] = mixed
        lse_ref[:, cols] = jnp.log(total)
        rows = mixed.T
        for b in range(QT // BLOCK):
            slot = qslot_ref[i * (QT // BLOCK) + b]
            placed[pl.ds(pl.multiple_of(slot * BLOCK, BLOCK), BLOCK), :] = rows[b * BLOCK : (b + 1) * BLOCK]
        return carry

    lax.fori_loop(0, q_tiles, tile, 0)

    def pack(c, carry):
        first = placed[pl.ds(pl.multiple_of(c * 2 * BLOCK, BLOCK), BLOCK), :]
        second = placed[pl.ds(pl.multiple_of((c * 2 + 1) * BLOCK, BLOCK), BLOCK), :]
        out_ref[pl.ds(pl.multiple_of(c * BLOCK, BLOCK), BLOCK), :] = jnp.concatenate([first, second], axis=1).astype(BF)
        return carry

    lax.fori_loop(0, q_ref.shape[0] // (2 * BLOCK), pack, 0)


def attend(core, tables, queries, own, other):
    kslot, qslot, lims, pos, start = tables
    n_q, n_k = queries.shape[0], own.shape[0]
    return pl.pallas_call(
        attend_kernel,
        in_specs=[in_smem()] * 4 + [in_vmem()] * 5,
        out_specs=[in_vmem()] * 3,
        out_shape=[
            jax.ShapeDtypeStruct((n_q // 2, LANES), BF),
            jax.ShapeDtypeStruct((HEAD, n_q), F32),
            jax.ShapeDtypeStruct((1, n_q), F32),
        ],
        scratch_shapes=[
            pltpu.VMEM((n_k, HEAD), BF),
            pltpu.VMEM((HEAD + 16, n_k), BF),
            pltpu.VMEM((n_q, HEAD), F32),
        ],
        compiler_params=params(),
        cost_estimate=pl.CostEstimate(flops=8 * n_q * n_k * HEAD, bytes_accessed=8 << 20, transcendentals=n_q * n_k),
    )(core, kslot, qslot, lims, queries, own, other, pos, start)


def attend_back_kernel(
    core_ref, kslot_ref, qslot_ref, lims_ref, q_ref, own_ref, other_ref, pos_ref, start_ref,
    grad_ref, mixed_ref, lse_ref,
    dq_ref, keep_ref, send_ref,
    keys, values, keys_t, grad_keys, grad_values, grad_placed,
):
    q_tiles = q_ref.shape[0] // QT
    k_tiles = own_ref.shape[0] // KT
    per = KT // BLOCK
    is_first = core_ref[0] == 0
    ones = jnp.ones((BLOCK, HEAD), BF)

    def load(t, carry):
        for b in range(per):
            slot = kslot_ref[t * per + b]
            own = block_rows(own_ref, slot)[:, HEAD:]
            other = block_rows(other_ref, slot)[:, HEAD:]
            at = pl.ds(pl.multiple_of((t * per + b) * BLOCK, BLOCK), BLOCK)
            key = jnp.where(is_first, own, other)
            value = jnp.where(is_first, other, own)
            keys[at, :] = jnp.concatenate([key, ones], axis=1)
            values[at, :] = jnp.concatenate([value, ones], axis=1)
            keys_t[:, at] = key.astype(F32).T.astype(BF)
            grad_keys[at, :] = jnp.zeros((BLOCK, HEAD), F32)
            grad_values[at, :] = jnp.zeros((BLOCK, HEAD), F32)
        return carry

    lax.fori_loop(0, k_tiles, load, 0)

    def unpack(c, carry):
        pair = grad_ref[pl.ds(pl.multiple_of(c * BLOCK, BLOCK), BLOCK), :]
        grad_placed[pl.ds(pl.multiple_of(c * 2 * BLOCK, BLOCK), BLOCK), :] = pair[:, :HEAD]
        grad_placed[pl.ds(pl.multiple_of((c * 2 + 1) * BLOCK, BLOCK), BLOCK), :] = pair[:, HEAD:]
        return carry

    lax.fori_loop(0, q_ref.shape[0] // (2 * BLOCK), unpack, 0)

    def tile(i, carry):
        cols = pl.ds(pl.multiple_of(i * QT, QT), QT)
        slots = [qslot_ref[i * (QT // BLOCK) + b] for b in range(QT // BLOCK)]
        query_f = jnp.concatenate([block_rows(q_ref, s)[:, :HEAD] for s in slots], axis=0).astype(F32) * SCALE
        grad = jnp.concatenate([block_rows(grad_placed, s) for s in slots], axis=0)
        query = query_f.astype(BF)
        grad_t = grad.astype(F32).T
        delta = jnp.sum(grad_t * mixed_ref[:, cols], axis=0, keepdims=True)
        pad = jnp.zeros((HEAD - 3, QT), F32)
        query_t = jnp.concatenate(
            [query_f.T] + [e.astype(F32) for e in sum_of_parts(-lse_ref[:, cols])] + [pad], axis=0
        ).astype(BF)
        grad_t = jnp.concatenate([grad_t] + [e.astype(F32) for e in sum_of_parts(-delta)] + [pad], axis=0).astype(BF)
        pos_row = pos_ref[:, cols]
        start_row = start_ref[:, cols]

        def step(masked, j, acc):
            at = pl.ds(pl.multiple_of(j * KT, KT), KT)
            p = jnp.exp(dot(keys[at, :], query_t))
            if masked:
                p = jnp.where(allowed_pairs(j, pos_row, start_row), p, 0.0)
            grad_s = (p * dot(values[at, :], grad_t)).astype(BF)
            grad_values[at, :] += dot(p.astype(BF), grad)
            grad_keys[at, :] += dot(grad_s, query)
            return acc + dot(keys_t[:, at], grad_s)

        acc = walk_keys(lims_ref, i, step, jnp.zeros((HEAD, QT), F32))
        rows = (acc * SCALE).T
        rows = jnp.concatenate([rows, jnp.zeros((QT, HEAD), F32)], axis=1)
        for b in range(QT // BLOCK):
            dq_ref[pl.ds(pl.multiple_of(slots[b] * BLOCK, BLOCK), BLOCK), :] = rows[b * BLOCK : (b + 1) * BLOCK]
        return carry

    lax.fori_loop(0, q_tiles, tile, 0)

    def place(t, carry):
        zeros = jnp.zeros((BLOCK, HEAD), F32)
        for b in range(per):
            slot = kslot_ref[t * per + b]
            at = pl.ds(pl.multiple_of((t * per + b) * BLOCK, BLOCK), BLOCK)
            to = pl.ds(pl.multiple_of(slot * BLOCK, BLOCK), BLOCK)
            key, value = grad_keys[at, :], grad_values[at, :]
            mine = jnp.where(is_first, key, value)
            theirs = jnp.where(is_first, value, key)
            keep_ref[to, :] = jnp.concatenate([zeros, mine], axis=1)
            send_ref[to, :] = jnp.concatenate([zeros, theirs], axis=1).astype(BF)
        return carry

    lax.fori_loop(0, k_tiles, place, 0)


def attend_back(core, tables, queries, own, other, grads, mixed, lse):
    kslot, qslot, lims, pos, start = tables
    n_q, n_k = queries.shape[0], own.shape[0]
    return pl.pallas_call(
        attend_back_kernel,
        in_specs=[in_smem()] * 4 + [in_vmem()] * 8,
        out_specs=[in_vmem()] * 3,
        out_shape=[
            jax.ShapeDtypeStruct((n_q, LANES), F32),
            jax.ShapeDtypeStruct((n_k, LANES), F32),
            jax.ShapeDtypeStruct((n_k, LANES), BF),
        ],
        scratch_shapes=[
            pltpu.VMEM((n_k, LANES), BF),
            pltpu.VMEM((n_k, LANES), BF),
            pltpu.VMEM((HEAD, n_k), BF),
            pltpu.VMEM((n_k, HEAD), F32),
            pltpu.VMEM((n_k, HEAD), F32),
            pltpu.VMEM((n_q, HEAD), BF),
        ],
        compiler_params=params(),
        cost_estimate=pl.CostEstimate(flops=16 * n_q * n_k * HEAD, bytes_accessed=8 << 20, transcendentals=n_q * n_k),
    )(core, kslot, qslot, lims, queries, own, other, pos, start, grads, mixed, lse)


def columns_of(value, chunk, order, part, parts):
    count = len(order) // parts
    pieces = [value[:, e * chunk : (e + 1) * chunk] for e in order[part * count : (part + 1) * count]]
    return jnp.concatenate(pieces, axis=1)


def in_order(values, chunk, order):
    joined = jnp.concatenate(values, axis=1)
    places = sorted(range(len(order)), key=lambda e: order[e])
    return jnp.concatenate([joined[:, e * chunk : (e + 1) * chunk] for e in places], axis=1)


def feed_kernel(n_parts, chunk, orders, n_ref, c_ref, *refs):
    first, second = refs[:n_parts], refs[n_parts : 2 * n_parts]
    mid_ref, gate_ref, up_ref, out_ref, back_ref = refs[2 * n_parts :]
    quarter = mid_ref.shape[1]
    split = first[0].shape[1] - quarter
    normed, upstream = n_ref[...], c_ref[...]

    def over_parts(value, order, parts, lo, hi):
        total = None
        for p, part in enumerate(parts):
            term = dot(columns_of(value, chunk, order, p, n_parts), part[:, lo:hi])
            total = term if total is None else total + term
        return total

    gate = over_parts(normed, orders[0], first, 0, quarter)
    up = over_parts(normed, orders[1], second, 0, quarter)
    down = jnp.concatenate(
        [
            over_parts(upstream, orders[0], first, quarter, quarter + split),
            over_parts(upstream, orders[1], second, quarter, 2 * quarter - split),
        ],
        axis=1,
    )
    sig = 1.0 / (1.0 + jnp.exp(-gate))
    silu = gate * sig
    mid_ref[...] = (silu * up).astype(BF)
    gate_ref[...] = (down * up * (sig * (1.0 + gate * (1.0 - sig)))).astype(BF)
    up_ref[...] = (down * silu).astype(BF)
    out_ref[...] = in_order(
        [dot(mid_ref[:, :split], part[:, quarter:], NT) for part in first], chunk, orders[0]
    ) + in_order([dot(mid_ref[:, split:], part[:, quarter:], NT) for part in second], chunk, orders[1])
    back = in_order([dot(gate_ref[...], part[:, :quarter], NT) for part in first], chunk, orders[0]) + in_order(
        [dot(up_ref[...], part[:, :quarter], NT) for part in second], chunk, orders[1]
    )
    back_ref[...] = back.astype(BF)


def feed(n, c, parts, chunk, orders, quarter):
    rows, width = n.shape
    step = rows // 2
    tall = lambda cols: pl.BlockSpec((step, cols), lambda i: (i, 0))
    whole = [p for piece in parts for p in piece]
    return pl.pallas_call(
        functools.partial(feed_kernel, len(parts[0]), chunk, orders),
        grid=(2,),
        in_specs=[tall(width)] * 2 + [pl.BlockSpec(p.shape, lambda i: (0, 0)) for p in whole],
        out_specs=[tall(quarter)] * 3 + [tall(width)] * 2,
        out_shape=[jax.ShapeDtypeStruct((rows, quarter), BF)] * 3
        + [jax.ShapeDtypeStruct((rows, width), F32), jax.ShapeDtypeStruct((rows, width), BF)],
        compiler_params=params(),
        cost_estimate=pl.CostEstimate(flops=12 * rows * width * quarter, bytes_accessed=16 << 20, transcendentals=0),
    )(n, c, *whole)


def feed_back_kernel(chunk, orders, *refs):
    (nt_a, ct_a, nt_b, ct_b, mid_a, gate_a, up_a, mid_b, gate_b, up_b), outs = refs[:10], refs[10:]
    quarter = mid_a.shape[1]
    split = outs[0].shape[1] - quarter
    height = outs[0].shape[0]
    per = height // chunk

    def rows_of(ref, order, place):
        return jnp.concatenate([ref[e * chunk : (e + 1) * chunk, :] for e in order[place * per : (place + 1) * per]], axis=0)

    def total(order, place, left_a, right_a, left_b, right_b):
        return (dot(rows_of(left_a, order, place), right_a) + dot(rows_of(left_b, order, place), right_b)).astype(BF)

    for i in range(2):

        @pl.when(pl.program_id(0) == i)
        def _():
            for side in range(2):
                place = side * 2 + i
                one, two = outs[side], outs[2 + side]
                one[:, :quarter] = total(orders[0], place, nt_a, gate_a[...], nt_b, gate_b[...])
                one[:, quarter:] = total(orders[0], place, ct_a, mid_a[:, :split], ct_b, mid_b[:, :split])
                two[:, :quarter] = total(orders[1], place, nt_a, up_a[...], nt_b, up_b[...])
                two[:, quarter:] = total(orders[1], place, ct_a, mid_a[:, split:], ct_b, mid_b[:, split:])


def feed_back(transposed, acts, chunk, orders, cols):
    width, rows = transposed[0].shape
    quarter = acts[0].shape[1]
    whole = lambda v: pl.BlockSpec(v.shape, lambda i: (0, 0))
    out = lambda c: pl.BlockSpec((width // 4, c), lambda i: (i, 0))
    return pl.pallas_call(
        functools.partial(feed_back_kernel, chunk, orders),
        grid=(2,),
        in_specs=[whole(v) for v in transposed] + [whole(v) for v in acts],
        out_specs=[out(cols[0])] * 2 + [out(cols[1])] * 2,
        out_shape=[jax.ShapeDtypeStruct((width // 2, c), BF) for c in (cols[0], cols[0], cols[1], cols[1])],
        compiler_params=params(),
        cost_estimate=pl.CostEstimate(flops=12 * rows * width * quarter, bytes_accessed=16 << 20, transcendentals=0),
    )(*transposed, *acts)


def down_split(quarter):
    return (quarter // 2 + LANES // 2) // LANES * LANES


def prepare_kernel(
    core_ref, table_ref, q_ref, k_ref, v_ref, o_ref, g_ref, u_ref, d_ref, ga_ref, gm_ref, flags_ref,
    mine_q_ref, theirs_q_ref, mine_f_ref, theirs_f_ref,
):
    first = core_ref[0] == 0
    owned, width = q_ref.shape

    def put(mine_ref, theirs_ref, at, zero, one):
        size = zero.shape[1]
        mine_ref[:, at : at + size] = jnp.where(first, zero, one).astype(BF)
        theirs_ref[:, at : at + size] = jnp.where(first, one, zero).astype(BF)

    for g in range(KV_HEADS):
        at = g * LANES
        kv = slice(g * HEAD, (g + 1) * HEAD)
        zero = jnp.concatenate([q_ref[:, at : at + HEAD], k_ref[:, kv]], axis=1)
        one = jnp.concatenate([q_ref[:, at + HEAD : at + LANES], v_ref[:, kv]], axis=1)
        put(mine_q_ref, theirs_q_ref, at, zero, one)
    shape = (owned, owned)
    diagonal = lax.broadcasted_iota(I32, shape, 0) == lax.broadcasted_iota(I32, shape, 1)
    gain_a = jnp.sum(jnp.where(diagonal, ga_ref[...], 0.0), axis=1, keepdims=True)
    gain_m = jnp.sum(jnp.where(diagonal, gm_ref[...], 0.0), axis=1, keepdims=True)
    count = flags_ref.shape[1]
    cols = count // owned
    row = lax.broadcasted_iota(I32, (owned, count), 0)
    col = lax.broadcasted_iota(I32, (owned, count), 1)
    spread = jnp.where(col // cols == row, flags_ref[...].astype(F32), 0.0).astype(BF)
    row = lax.broadcasted_iota(I32, (count, LANES), 0)
    col = lax.broadcasted_iota(I32, (count, LANES), 1)
    extra = dot(spread, jnp.where(row % cols == col - 3, 1.0, 0.0).astype(BF))
    row = lax.broadcasted_iota(I32, (owned, LANES), 0)
    col = lax.broadcasted_iota(I32, (owned, LANES), 1)
    blocks = jnp.where(row == 0, table_ref[0, 0], jnp.where(row == 1, table_ref[0, 1], 0)).astype(F32)
    extra = jnp.where(col == 0, gain_a, jnp.where(col == 1, gain_m, jnp.where(col == 2, blocks, extra)))
    put(mine_q_ref, theirs_q_ref, width, extra, extra)
    half = g_ref.shape[1] // 2
    quarter = half // 2
    split = down_split(quarter)
    for x in range(2):
        at = 2 * x * quarter * 3 // 2
        for ref, lo, hi in ((g_ref, 0, quarter), (d_ref, 0, split), (u_ref, 0, quarter), (d_ref, split, quarter)):
            zero = ref[:, x * quarter + lo : x * quarter + hi]
            one = ref[:, half + x * quarter + lo : half + x * quarter + hi]
            put(mine_f_ref, theirs_f_ref, at, zero, one)
            at += hi - lo
    put(mine_q_ref, theirs_q_ref, width + LANES, o_ref[:, : width // 2], o_ref[:, width // 2 :])


def prepare(core, table, *arrays):
    owned, width = arrays[0].shape
    cols = 3 * arrays[4].shape[1] // 2
    return pl.pallas_call(
        prepare_kernel,
        in_specs=[in_smem()] * 2 + [in_vmem()] * len(arrays),
        out_specs=[in_vmem()] * 4,
        out_shape=[jax.ShapeDtypeStruct((owned, width + LANES + width // 2), BF)] * 2 + [jax.ShapeDtypeStruct((owned, cols), BF)] * 2,
        compiler_params=params(),
    )(core, table, *arrays)


def deliver_kernel(core_ref, zero_ref, one_ref, other_ref, gate_ref, up_ref, down_ref):
    first = core_ref[0] == 0
    owned, half = gate_ref.shape[0], gate_ref.shape[1] // 2
    quarter = half // 2
    split = down_split(quarter)
    for x, ref in enumerate((zero_ref, one_ref)):
        at = 0
        for out, lo, hi in ((gate_ref, 0, quarter), (down_ref, 0, split), (up_ref, 0, quarter), (down_ref, split, quarter)):
            size = hi - lo
            kept = jnp.where(first, ref[:owned, at : at + size], ref[owned:, at : at + size])
            arrived = other_ref[:, x * 3 * quarter + at : x * 3 * quarter + at + size]
            out[:, x * quarter + lo : x * quarter + hi] = jnp.where(first, kept, arrived)
            out[:, half + x * quarter + lo : half + x * quarter + hi] = jnp.where(first, arrived, kept)
            at += size


def deliver(core, zero, one, other):
    owned, cols = other.shape
    return pl.pallas_call(
        deliver_kernel,
        in_specs=[in_smem()] + [in_vmem()] * 3,
        out_specs=[in_vmem()] * 3,
        out_shape=[jax.ShapeDtypeStruct((owned, 2 * cols // 3), F32)] * 3,
        compiler_params=params(),
    )(core, zero, one, other)


def deliver_heads_kernel(core_ref, qkv_ref, out_ref, other_ref, wo_ref, q_ref, k_ref, v_ref):
    first = core_ref[0] == 0
    owned, width = q_ref.shape
    half = width // 2

    def sides(ref, at, size, shift):
        kept = jnp.where(first, ref[:owned, at : at + size], ref[owned:, at : at + size])
        arrived = other_ref[:, shift + at : shift + at + size]
        return jnp.where(first, kept, arrived), jnp.where(first, arrived, kept)

    wo_ref[:, :half], wo_ref[:, half:] = sides(out_ref, 0, half, width)
    for g in range(0, KV_HEADS, 2):
        zero, one = sides(qkv_ref, g * LANES, LANES, 0)
        zero_next, one_next = sides(qkv_ref, (g + 1) * LANES, LANES, 0)
        q_ref[:, g * LANES : (g + 1) * LANES] = jnp.concatenate([zero[:, :HEAD], one[:, :HEAD]], axis=1)
        q_ref[:, (g + 1) * LANES : (g + 2) * LANES] = jnp.concatenate([zero_next[:, :HEAD], one_next[:, :HEAD]], axis=1)
        k_ref[:, g * HEAD : (g + 2) * HEAD] = jnp.concatenate([zero[:, HEAD:], zero_next[:, HEAD:]], axis=1)
        v_ref[:, g * HEAD : (g + 2) * HEAD] = jnp.concatenate([one[:, HEAD:], one_next[:, HEAD:]], axis=1)


def deliver_heads(core, qkv, out, other):
    owned, width = other.shape[0], qkv.shape[1]
    shapes = [(owned, width), (owned, width), (owned, width // 2), (owned, width // 2)]
    return pl.pallas_call(
        deliver_heads_kernel,
        in_specs=[in_smem()] + [in_vmem()] * 3,
        out_specs=[in_vmem()] * 4,
        out_shape=[jax.ShapeDtypeStruct(e, F32) for e in shapes],
        compiler_params=params(),
    )(core, qkv, out, other)


def leave_kernel(core_ref, own_ref, other_ref, x_ref, wo_ref, gain_ref, res_ref, n_ref, nt_ref, attn_ref, half_ref):
    half = KV_HEADS * HEAD
    for which, ref in enumerate((own_ref, other_ref)):
        for g in range(0, KV_HEADS, 2):
            for s in range(2):
                for j in range(2):
                    lanes = slice(j * HEAD, (j + 1) * HEAD)
                    a = ref[(g * 2 + s) * BLOCK : (g * 2 + s + 1) * BLOCK, lanes]
                    b = ref[((g + 1) * 2 + s) * BLOCK : ((g + 1) * 2 + s + 1) * BLOCK, lanes]
                    row, col = (s * 2 + j) * BLOCK, which * half + g * HEAD
                    attn_ref[row : row + BLOCK, col : col + LANES] = jnp.concatenate([a, b], axis=1)
    value = x_ref[...].astype(F32) + dot(attn_ref[...], wo_ref[...])
    res_ref[...] = value
    inverse = lax.rsqrt(jnp.mean(value * value, axis=-1, keepdims=True) + EPS)
    normed = (value * inverse * gain_ref[...]).astype(BF)
    n_ref[...] = normed
    nt_ref[...] = normed.T
    rows = half_ref.shape[0]
    half_ref[...] = jnp.where(core_ref[0] == 0, normed[:rows], normed[rows:])


def leave(core, own, other, x, wo, gain):
    rows, width = x.shape
    return pl.pallas_call(
        leave_kernel,
        in_specs=[in_smem()] + [in_vmem()] * 5,
        out_specs=[in_vmem()] * 5,
        out_shape=[
            jax.ShapeDtypeStruct((rows, width), F32),
            jax.ShapeDtypeStruct((rows, width), BF),
            jax.ShapeDtypeStruct((width, rows), BF),
            jax.ShapeDtypeStruct((rows, width), BF),
            jax.ShapeDtypeStruct((rows // 2, width), BF),
        ],
        compiler_params=params(),
        cost_estimate=pl.CostEstimate(flops=2 * rows * width * width, bytes_accessed=10 << 20, transcendentals=0),
    )(core, own, other, x, wo, gain)


def enter_kernel(
    core_ref, back_ref, other_ref, far_ref, far_other_ref, res_ref, c_ref, gain_ref, wo_ref,
    grad_ref, grad_b_ref, gain_out_ref, out_ref,
):
    value = res_ref[...]
    inverse = lax.rsqrt(jnp.mean(value * value, axis=-1, keepdims=True) + EPS)
    first = core_ref[0] == 0
    far, far_other = far_ref[...].astype(F32), far_other_ref[...].astype(F32)
    far_all = jnp.concatenate([jnp.where(first, far, far_other), jnp.where(first, far_other, far)], axis=0)
    grad = back_ref[...].astype(F32) + other_ref[...].astype(F32) + far_all
    gain_out_ref[...] = jnp.sum(grad * value * inverse, axis=0, keepdims=True)
    scaled = grad * gain_ref[...]
    mean = jnp.mean(scaled * value, axis=-1, keepdims=True)
    total = c_ref[...].astype(F32) + (inverse * scaled - value * (inverse * inverse * inverse) * mean)
    grad_ref[...] = total
    grad_b_ref[...] = total.astype(BF)
    heads = dot(grad_b_ref[...], wo_ref[: KV_HEADS * HEAD, :], NT).astype(BF)
    for g in range(KV_HEADS):
        for s in range(2):
            row = s * 2 * BLOCK
            lanes = slice(g * HEAD, (g + 1) * HEAD)
            out_ref[(g * 2 + s) * BLOCK : (g * 2 + s + 1) * BLOCK, :] = jnp.concatenate(
                [heads[row : row + BLOCK, lanes], heads[row + BLOCK : row + 2 * BLOCK, lanes]], axis=1
            )


def enter(core, back, other, far, far_other, residual, c, gain, wo):
    rows, width = residual.shape
    return pl.pallas_call(
        enter_kernel,
        in_specs=[in_smem()] + [in_vmem()] * 8,
        out_specs=[in_vmem()] * 4,
        out_shape=[
            jax.ShapeDtypeStruct((rows, width), F32),
            jax.ShapeDtypeStruct((rows, width), BF),
            jax.ShapeDtypeStruct((1, width), F32),
            jax.ShapeDtypeStruct((2 * KV_HEADS * BLOCK, LANES), BF),
        ],
        compiler_params=params(),
        cost_estimate=pl.CostEstimate(flops=rows * width * width, bytes_accessed=10 << 20, transcendentals=0),
    )(core, back, other, far, far_other, residual, c, gain, wo)


def rms(value, gain):
    inverse = lax.rsqrt(jnp.mean(value * value, axis=-1, keepdims=True) + EPS)
    return value * inverse * gain, inverse


def rms_back(value, inverse, gain, grad):
    scaled = grad * gain
    mean = jnp.mean(scaled * value, axis=-1, keepdims=True)
    moved = inverse * scaled - value * (inverse * inverse * inverse) * mean
    return moved, jnp.sum(grad * value * inverse, axis=0)


def rope_tables(positions):
    inv_freq = jnp.power(F32(1000000.0), -(2.0 * jnp.arange(HEAD // 2, dtype=F32)) / HEAD)
    angles = positions.astype(F32)[:, None] * inv_freq[None, :]
    cosine, sine = jnp.cos(angles), jnp.sin(angles)
    return (
        jnp.concatenate([cosine] * 4, axis=1),
        jnp.concatenate([-sine, sine, -sine, sine], axis=1),
    )


class Dim:
    def __init__(self, stride, size):
        self.stride, self.size = stride, size


def make_shards(n):
    if n == 16:
        dims = {"x": Dim(1, 2), "y": Dim(2, 2), "p": Dim(4, 2), "q": Dim(8, 2)}
        order_a, order_b, order_m, order_w = "qpxy", "qpyx", "xqpy", "xqyp"
    else:
        names = "abcdefghijkl"[: n.bit_length() - 1]
        dims = {name: Dim(1 << b, 2) for b, name in enumerate(names)}
        order_a = order_b = order_m = order_w = names
    groups = n // 16
    a2a_groups = None if groups == 1 else [[t * 16 + d for d in range(16)] for t in range(groups)]
    kv_groups = None if groups == 1 else [[t * 16 + d for t in range(groups)] for d in range(16)]

    def digits(order):
        places = []
        for r in range(n):
            place = {}
            for name in order:
                place[name] = r % dims[name].size
                r //= dims[name].size
            places.append(place)
        return places

    def place_in(order, base=order_a):
        found = {tuple(sorted(p.items())): r for r, p in enumerate(digits(order))}
        return [found[tuple(sorted(p.items()))] for p in digits(base)]

    def chips(me, order, absolute=None):
        out = []
        for place in digits(order):
            chip = me
            for name, digit in place.items():
                d = dims[name]
                at = (me // d.stride) % d.size
                to = digit if name == absolute else jnp.bitwise_xor(at, digit)
                chip = chip + (to - at) * d.stride
            out.append(chip)
        return jnp.stack(out).astype(I32)

    def ctx_send(value, pairs):
        return lax.ppermute(value, "ctx", pairs)

    def ctx_swap(value, stride):
        return ctx_send(value, [(i, i ^ stride) for i in range(n)])

    def core_swap(value):
        return lax.ppermute(value, "wt", [(0, 1), (1, 0)])

    def gather_dim(value, name):
        return [value, ctx_swap(value, dims[name].stride)]

    def join(parts):
        return parts[0] if len(parts) == 1 else jnp.concatenate(parts, axis=0)

    def gather_rows(parts, names):
        for name in names:
            parts = gather_dim(join(parts), name)
        return parts

    def hold(parts, *others):
        return parts[:-1] + [after(parts[-1], *others)]

    def scatter_begin(keep, send, name):
        return keep, ctx_swap(send.astype(BF), dims[name].stride)

    def scatter_next(state, name):
        keep, arrived = state
        half = keep.shape[0] // 2
        send = (keep[half:].astype(F32) + arrived[half:].astype(F32)).astype(BF)
        return keep[:half].astype(F32) + arrived[:half].astype(F32), ctx_swap(send, dims[name].stride)

    def scatter_end(state):
        keep, arrived = state
        return keep.astype(F32) + arrived.astype(F32)

    def scatter_rows(keep, send, names):
        state = scatter_begin(keep, send, names[-1])
        for name in reversed(names[:-1]):
            state = scatter_next(state, name)
        return scatter_end(state)

    def scatter_whole(value, names):
        half = value.shape[0] // 2
        return scatter_rows(value[:half], value[half:], names)

    def runs(places):
        out = []
        for p in places:
            if out and out[-1][1] == p:
                out[-1][1] = p + 1
            else:
                out.append([p, p + 1])
        return out

    def assemble(parts, order):
        total = sum(p.shape[0] for p in parts)
        unit, each = total // n, parts[0].shape[0] // (total // n)
        out = []
        for lo, hi in runs(place_in(order)):
            while lo < hi:
                part, at = lo // each, lo % each
                stop = min(hi, (part + 1) * each)
                out.append(parts[part][at * unit : (at + stop - lo) * unit])
                lo = stop
        return join(out)

    def columns_in(value, order):
        unit = value.shape[1] // n
        inverse = np.argsort(place_in(order)).tolist()
        pieces = [value[:, lo * unit : hi * unit] for lo, hi in runs(inverse)]
        return pieces[0] if len(pieces) == 1 else jnp.concatenate(pieces, axis=1)

    def after(value, *others):
        return lax.optimization_barrier((value,) + others)[0]

    def swap_heads(value):
        return lax.all_to_all(value, "ctx", 0, 0, axis_index_groups=a2a_groups, tiled=True)

    def shards(
        tokens, block_table, doc_flags, w_query, key_weight, value_weight, w_out, w_gate, w_up, w_down,
        gain_attn, gain_mlp, gain_q, key_norm_gain, cotangent,
    ):
        width = tokens.shape[-1]
        rows = tokens.shape[1]
        owned = w_query.shape[0]
        chip_rows = 2 * owned
        me = lax.axis_index("ctx")
        core = lax.axis_index("wt")
        first = core == 0
        core_arr = core.astype(I32).reshape(1)
        slots_n = 2 * n

        def by_core(a, b, axis=0):
            return jnp.where(first, jnp.concatenate([a, b], axis=axis), jnp.concatenate([b, a], axis=axis))

        def pick(a, b):
            return jnp.where(first, a, b)

        chip_of = chips(me, order_a)

        def features(order, absolute=None):
            chip = chips(me, order, absolute)
            return (chip[:, None] * chip_rows + jnp.arange(chip_rows, dtype=I32)[None, :]).reshape(-1)

        def spread(order, absolute=None):
            return (jnp.arange(width, dtype=I32)[:, None] == features(order, absolute)[None, :]).astype(BF)

        canon = features(order_a)
        perm = spread(order_a)
        perm_m = spread(order_m, order_m[0])
        left = me % 2 == 0

        def pick_x(a, b):
            return jnp.where(left, a, b)

        def by_x(a, b, axis=0):
            return pick_x(jnp.concatenate([a, b], axis=axis), jnp.concatenate([b, a], axis=axis))

        flag_cols = rows // owned
        own_blocks = block_table[0]
        mine_q, theirs_q, mine_f, theirs_f = prepare(
            core_arr, block_table, w_query, key_weight, value_weight, w_out, w_gate, w_up, w_down,
            gain_attn[None, :], gain_mlp[None, :], doc_flags,
        )
        first_piece = by_core(mine_q, core_swap(theirs_q))
        acts = jnp.stack([tokens[0], cotangent[0]])
        acts_other = core_swap(acts)
        other_f = core_swap(theirs_f)
        x_two = dot(by_core(acts[0], acts_other[0]), perm).astype(BF)
        x_m = dot(by_core(acts[0], acts_other[0]), perm_m).astype(BF)
        c_m = dot(by_core(acts[1], acts_other[1]), perm_m).astype(BF)
        head_cols = width // 2
        out_cols = width // 4
        out_at = width + LANES

        def cut(value):
            first_cols = [value[:, :head_cols], value[:, width:out_at], value[:, out_at : out_at + out_cols]]
            second_cols = [value[:, head_cols:width], value[:, out_at + out_cols :]]
            return [jnp.concatenate(first_cols, axis=1)], [jnp.concatenate(second_cols, axis=1)]

        if n == 16:
            shared = cut(join(gather_rows([first_piece], "qp")))
            qkv_parts = [gather_rows(shared[0], "x"), gather_rows(shared[1], "y")]
            first_swap = qkv_parts[0][-1]
            qkv_parts = [gather_rows(hold(qkv_parts[0], x_two), "y"), gather_rows(qkv_parts[1], "x")]
        else:
            shared = cut(first_piece)
            qkv_parts = [gather_rows(shared[0], order_a), gather_rows(shared[1], order_b)]
            first_swap = first_piece
        chunk = LANES
        per = chunk // chip_rows
        chunk_orders = [[e // per for e in np.argsort(place_in(o)).tolist()[::per]] for o in (order_a, order_b)]
        extras = assemble([p[:, head_cols : head_cols + LANES] for p in qkv_parts[0]], order_a).astype(F32)
        wo_half = jnp.concatenate(
            [
                assemble([p[:, head_cols + LANES :] for p in qkv_parts[0]], order_a),
                assemble([p[:, head_cols:] for p in qkv_parts[1]], order_b),
            ],
            axis=1,
        )

        hidden = x_two.astype(F32)

        quarter = w_gate.shape[1] // 4
        feed_half = by_core(mine_f, other_f)
        feed_x = feed_half[:, : 3 * quarter], feed_half[:, 3 * quarter :]
        feed_near = pick_x(*feed_x)
        feed_far = after(ctx_swap(pick_x(feed_x[1], feed_x[0]), 1), first_swap)
        feed_cut = quarter + down_split(quarter)
        feed_cols = (feed_cut, 3 * quarter - feed_cut)
        feed_orders = (order_m[1:], order_w[1:])
        feed_parts = [
            gather_rows([by_x(feed_near[:, lo:hi], feed_far[:, lo:hi])], feed_orders[e][:1])
            for e, (lo, hi) in enumerate(((0, feed_cut), (feed_cut, 3 * quarter)))
        ]

        gain_a, gain_m = extras[:, 0][None, :], extras[:, 1][None, :]
        per_chip = extras.reshape(n, 2, owned, LANES)
        block_of = per_chip[:, 0, :2, 2].reshape(-1).astype(I32)
        seq = me % 2
        flags = jnp.where(seq == 0, per_chip[:, 0], per_chip[:, 1])[:, :, 3 : 3 + flag_cols].reshape(slots_n, BLOCK)
        slot_of = (chip_of[:, None] * 2 + jnp.arange(2, dtype=I32)[None, :]).reshape(-1)
        ids = jnp.arange(slots_n, dtype=I32)
        hit = ids[:, None] == block_of[None, :]
        flags_pos = dot(hit.astype(BF), flags.astype(BF))
        kslot = jnp.sum(jnp.where(hit, slot_of[None, :], 0), axis=1)
        pos = jnp.arange(slots_n * BLOCK, dtype=I32).reshape(slots_n, BLOCK)
        begins = jnp.where(flags_pos > 0.5, pos, -1)
        lane = jnp.arange(BLOCK, dtype=I32)
        inside = jnp.max(jnp.where(lane[None, None, :] <= lane[None, :, None], begins[:, None, :], -1), axis=2)
        carried = jnp.max(jnp.where(ids[None, :] < ids[:, None], jnp.max(begins, axis=1)[None, :], -1), axis=1)
        doc_start = jnp.maximum(inside, carried[:, None])
        here = (slot_of // 32) == (me // 16)
        rank = jnp.sum((here[None, :] & (block_of[None, :] < block_of[:, None])).astype(I32), axis=1)
        hit_q = here[None, :] & (rank[None, :] == jnp.arange(32, dtype=I32)[:, None])
        q_block = jnp.sum(jnp.where(hit_q, block_of[None, :], 0), axis=1)
        qslot = jnp.sum(jnp.where(hit_q, slot_of[None, :] - (me // 16) * 32, 0), axis=1)
        q_pos = q_block[:, None] * BLOCK + lane[None, :]
        q_start = jnp.sum(jnp.where((q_block[:, None] == ids[None, :])[:, :, None], doc_start[None], 0), axis=1)
        n_q = 32 * BLOCK
        tile_start = q_start.reshape(n_q // QT, QT)
        tile_pos = q_pos.reshape(n_q // QT, QT)
        low, high = jnp.min(tile_start, axis=1) // KT, jnp.max(tile_pos, axis=1) // KT + 1
        full_low = jnp.minimum((jnp.max(tile_start, axis=1) + KT - 1) // KT, high)
        full_high = jnp.maximum(jnp.minimum((jnp.min(tile_pos, axis=1) + 1) // KT, high), full_low)
        lims = jnp.stack([low, full_low, full_high, high])
        tables = (kslot, qslot, lims, q_pos.reshape(1, n_q), q_start.reshape(1, n_q))

        own_pos = (own_blocks[:, None] * BLOCK + lane[None, :]).reshape(-1)
        cosine, sine = rope_tables(own_pos)
        gain_qk = jnp.concatenate([gain_q, key_norm_gain])[None, :]

        normed_ab, raw, packed = project(
            core_arr, x_two, gain_a, gain_qk, cosine, sine, qkv_parts, chunk, chunk_orders
        )
        feed_parts = [gather_rows(hold(feed_parts[e], packed), feed_orders[e][1:]) for e in range(2)]
        queries = swap_heads(packed.reshape(16, rows, LANES)).reshape(n_q, LANES)
        own_kv = queries
        gain_mm = dot(dot(jnp.broadcast_to(gain_m, (8, width)).astype(BF), perm, NT).astype(BF), perm_m)[:1]

        def from_pair(half):
            far = ctx_swap(half, 1)
            return by_core(far, core_swap(far))

        def mine(value):
            return pick(value[:rows], value[rows:])

        def not_mine(value):
            return pick(value[rows:], value[:rows])

        c_far = from_pair(after(mine(c_m), packed))
        if groups > 1:
            own_kv = lax.all_gather(queries, "ctx", axis=0, tiled=True, axis_index_groups=kv_groups)
        other_kv = core_swap(own_kv)
        wo_other = core_swap(wo_half)
        wo_full = by_core(wo_half, wo_other, axis=1)
        head_ids = jnp.arange(width, dtype=I32)
        place = (head_ids // 512).astype(I32)
        head_row = (((head_ids % 512) // HEAD) * 2 + jnp.bitwise_xor(core.astype(I32), place)) * HEAD + head_ids % HEAD
        select = (head_row[:, None] == canon[None, :]).astype(BF)
        wo_sel = dot(select, dot(wo_full, perm_m).astype(BF)).astype(BF)

        other_kv = after(other_kv, wo_sel)
        mixed_packed, mixed, lse = attend(core_arr, tables, queries, own_kv, other_kv)

        attn_own = swap_heads(mixed_packed.reshape(16, BLOCK, LANES)).reshape(16 * BLOCK, LANES)
        residual, normed_m, n_t, attn, n_half = leave(core_arr, attn_own, core_swap(attn_own), x_m, wo_sel, gain_mm)

        n_far = from_pair(n_half)
        per_chunk = LANES // chip_rows
        feed_chunks = [
            [e // per_chunk for e in np.argsort(place_in(o, order_m)).tolist()[::per_chunk]] for o in (order_m, order_w)
        ]
        *acts_near, out_near, back_near = feed(normed_m, c_m, feed_parts, LANES, feed_chunks, quarter)
        *acts_far, out_far, back_far = feed(n_far, c_far, feed_parts, LANES, feed_chunks, quarter)
        chip_far = (mine(back_far).astype(F32) + core_swap(not_mine(back_far)).astype(F32)).astype(BF)
        back_pair = ctx_swap(chip_far, 1)
        keep_a, send_a, keep_b, send_b = feed_back(
            (n_t, c_m.T, n_far.T, c_far.T), (*acts_near, *acts_far), LANES, feed_chunks, feed_cols
        )
        feed_sums = [
            scatter_begin(keep_a, send_a, feed_orders[0][-1]),
            scatter_begin(keep_b, send_b, feed_orders[1][-1]),
        ]
        grad_h, grad_hb, grad_gm, do_packed = enter(
            core_arr, back_near, core_swap(back_near), back_pair, core_swap(back_pair), residual, c_m, gain_mm, wo_sel
        )
        grads_in = swap_heads(do_packed.reshape(16, BLOCK, LANES)).reshape(n_q // 2, LANES)
        attn = after(attn, do_packed)

        out_other = core_swap(jnp.concatenate([not_mine(out_near), not_mine(out_far)]).astype(BF)).astype(F32)
        out_pair = ctx_swap((mine(out_far) + out_other[rows:]).astype(BF), 1).astype(F32)
        layer_rel = mine(residual) + (mine(out_near) + out_other[:rows] + out_pair)
        layer_out = dot(layer_rel.astype(BF), perm_m, NT).astype(BF)[None]

        attn_rel = dot(attn, select).astype(BF)
        grad_hc = dot(grad_hb, pick(perm_m[: width // 2], perm_m[width // 2 :]), NT).astype(BF)
        out_first = dot(attn_rel, grad_hc[:, :out_cols], TN).astype(BF)
        out_second = dot(columns_in(attn_rel, order_b), grad_hc[:, out_cols:], TN).astype(BF)

        dq, keep, send = attend_back(core_arr, tables, queries, own_kv, other_kv, grads_in, mixed, lse)
        feed_sums = [scatter_next(hold(list(feed_sums[e]), send), feed_orders[e][-2]) for e in range(2)]
        grad_kv = keep + core_swap(send).astype(F32)
        if groups > 1:
            grad_kv = lax.psum_scatter(grad_kv, "ctx", scatter_dimension=0, tiled=True, axis_index_groups=kv_groups)
        back = swap_heads((dq + grad_kv).astype(BF).reshape(16, rows, LANES))
        grad_qkv_in, gain_parts = unproject(core_arr, back.reshape(KV_HEADS, 2, rows, LANES), raw, gain_qk, cosine, sine)
        g_first, g_second = grad_qkv_in[:, : width // 2], grad_qkv_in[:, width // 2 :]

        def halves(value):
            half = value.shape[0] // 2
            return value[:half], value[half:]

        sum_first = jnp.concatenate([dot(normed_ab, g_first, TN).astype(BF), out_first], axis=1)
        sum_second = jnp.concatenate([dot(columns_in(normed_ab, order_b), g_second, TN).astype(BF), out_second], axis=1)
        level_holds = {}
        if n == 16:
            sum_first = scatter_begin(*halves(sum_first), "y")
            sum_second = scatter_begin(*halves(sum_second), "x")
            level_holds[3] = sum_first[1], sum_second[1]
            sum_first = scatter_next(sum_first, "x")
            sum_second = scatter_next(sum_second, "y")
            level_holds[4] = sum_first[1], sum_second[1]
            sums = jnp.concatenate([scatter_end(sum_first), scatter_end(sum_second)], axis=1)
            sums = scatter_whole(sums, "qp")
        else:
            sums = jnp.concatenate([scatter_whole(sum_first, order_a), scatter_whole(sum_second, order_b)], axis=1)
        cut_cols = head_cols + out_cols
        part_qkv = jnp.concatenate([sums[:, :head_cols], sums[:, cut_cols : cut_cols + head_cols]], axis=1)
        part_out = jnp.concatenate([sums[:, head_cols:cut_cols], sums[:, cut_cols + head_cols :]], axis=1)
        w_first = assemble([p[:, : width // 2] for p in qkv_parts[0]], order_a)
        w_second = assemble([p[:, : width // 2] for p in qkv_parts[1]], order_b)
        n1_part = dot(g_first, w_first, NT) + dot(g_second, w_second, NT)
        n1_other = core_swap(pick(n1_part[rows:], n1_part[:rows]))
        grad_n1 = pick(n1_part[:rows], n1_part[rows:]) + n1_other

        x_mine = mine(hidden)
        _, inv_a = rms(x_mine, gain_a)
        moved_a, grad_ga = rms_back(x_mine, inv_a, gain_a, grad_n1)

        def unspread(value, matrix):
            high = value.astype(BF)
            low = (value - high.astype(F32)).astype(BF)
            return dot(high, matrix, NT) + dot(low, matrix, NT)

        grad_input = (unspread(mine(grad_h), perm_m) + unspread(moved_a, perm))[None]

        def exact(vector, matrix):
            return lax.dot_general(
                vector, matrix.astype(F32), NT, precision=lax.Precision.HIGHEST, preferred_element_type=F32
            )

        vectors = jnp.concatenate([exact(grad_ga[None], perm), exact(jnp.where(first, grad_gm, 0.0), perm_m)])
        feed_levels = len(order_m)
        for level in range(3, feed_levels):
            feed_sums = [hold(list(v), *level_holds.get(level, ())) for v in feed_sums]
            feed_sums = [scatter_next(feed_sums[e], feed_orders[e][-level]) for e in range(2)]
        feed_sums = [scatter_end(hold(list(v), vectors)) for v in feed_sums]
        feed_near = jnp.concatenate([pick_x(v[:chip_rows], v[chip_rows:]) for v in feed_sums], axis=1)
        feed_far = jnp.concatenate([pick_x(v[chip_rows:], v[:chip_rows]) for v in feed_sums], axis=1)
        feed_far = ctx_swap(feed_far.astype(BF), 1).astype(F32)
        feed_zero, feed_one = pick_x(feed_near, feed_far), pick_x(feed_far, feed_near)
        heads_gain = jnp.sum(gain_parts[:, 0], axis=0)
        small = jnp.concatenate([vectors.reshape(-1, LANES), heads_gain[None], jnp.zeros((7, LANES), F32)])
        for bit in range(n.bit_length() - 1):
            small = small + ctx_swap(small, 1 << bit)
        small = small + core_swap(small)
        my_row = (me * 2 + core) * owned
        gains = small[: 2 * width // LANES].reshape(2, width)
        gains = lax.dynamic_slice_in_dim(gains, my_row, owned, axis=1)

        def theirs(parts):
            return jnp.concatenate([pick(p[owned:], p[:owned]) for p in parts], axis=1)

        grad_gate, grad_up, grad_down = deliver(
            core_arr, feed_zero, feed_one, core_swap(theirs([feed_zero, feed_one]))
        )
        grad_wout, grad_query, grad_key, grad_value = deliver_heads(
            core_arr, part_qkv, part_out, core_swap(theirs([part_qkv, part_out]))
        )
        return (
            layer_out,
            grad_input,
            grad_query,
            grad_key,
            grad_value,
            grad_wout,
            grad_gate,
            grad_up,
            grad_down,
            gains[0],
            gains[1],
            small[2 * width // LANES, :HEAD],
            small[2 * width // LANES, HEAD:],
        )

    return shards


def solution(mesh):
    seq = P("wt", "ctx", None)
    weight = P(("ctx", "wt"), None)
    vector = P(("ctx", "wt"))
    return jax.shard_map(
        make_shards(mesh.shape["ctx"]),
        mesh=mesh,
        in_specs=(seq, P("ctx", None), P("wt", "ctx")) + (weight,) * 7 + (vector, vector, P(), P(), seq),
        out_specs=(seq, seq) + (weight,) * 7 + (vector, vector, P(), P()),
        check_vma=False,
    )
```

```python
import functools

import jax
import jax.numpy as jnp
import numpy as np
from jax import lax
from jax.experimental import pallas as pl
from jax.experimental.pallas import tpu as pltpu
from jax.sharding import PartitionSpec as P

HEADS = 16
KV_HEADS = 8
HEAD = 64
LANES = 2 * HEAD
BLOCK = 128
EPS = 1e-05
SCALE = HEAD**-0.5
BF = jnp.bfloat16
F32 = jnp.float32
I32 = jnp.int32
QT = 512
KT = 512
VMEM_BYTES = 56 * 1024 * 1024

NN = (((1,), (0,)), ((), ()))
NT = (((1,), (1,)), ((), ()))
TN = (((0,), (0,)), ((), ()))


def dot(a, b, dims=NN):
    return lax.dot_general(a, b, dims, preferred_element_type=F32)


def params(**kw):
    return pltpu.CompilerParams(vmem_limit_bytes=VMEM_BYTES, **kw)


def in_vmem():
    return pl.BlockSpec(memory_space=pltpu.VMEM)


def in_smem():
    return pl.BlockSpec(memory_space=pltpu.SMEM)


def low_lanes(shape):
    return lax.broadcasted_iota(I32, shape, 1) < HEAD


def half_sums(value, low):
    total = jnp.sum(value, axis=-1, keepdims=True)
    first = jnp.sum(jnp.where(low, value, 0.0), axis=-1, keepdims=True)
    return jnp.where(low, first, total - first)


def half_turn(value):
    lane = lax.broadcasted_iota(I32, value.shape, 1)
    first = (lane % HEAD) < HEAD // 2
    return jnp.where(
        first,
        pltpu.roll(value, LANES - HEAD // 2, 1),
        pltpu.roll(value, HEAD // 2, 1),
    )


def project_kernel(n_parts, swaps, core_ref, x_ref, norm_gain_ref, gain_ref, cos_ref, sin_ref, *refs):
    weights, (n_ref, raw_ref, out_ref) = refs[: 2 * n_parts], refs[2 * n_parts :]
    rows = cos_ref.shape[0]
    is_value = core_ref[0] == 1
    x = x_ref[...].astype(F32)
    inverse = lax.rsqrt(jnp.mean(x * x, axis=-1, keepdims=True) + EPS)
    n_ref[...] = (x * inverse * norm_gain_ref[...]).astype(BF)
    groups = KV_HEADS // 2
    for half in range(2):
        total, at = None, 0
        for part in weights[half * n_parts : (half + 1) * n_parts]:
            length = part.shape[0]
            pieces = [n_ref[:, e : e + swaps[2]] for e in swaps[half][at // swaps[2] : (at + length) // swaps[2]]]
            left = pieces[0] if len(pieces) == 1 else jnp.concatenate(pieces, axis=1)
            term = dot(left, part[:, : groups * LANES])
            total = term if total is None else total + term
            at += length
        raw_ref[:, half * groups * LANES : (half + 1) * groups * LANES] = total
    low = low_lanes((rows, LANES))
    turns = jnp.logical_or(low, jnp.logical_not(is_value))
    for g in range(KV_HEADS):
        for s in range(2):
            raw = raw_ref[s * rows : (s + 1) * rows, g * LANES : (g + 1) * LANES]
            inverse = lax.rsqrt(half_sums(raw * raw, low) * (1.0 / HEAD) + EPS)
            normed = raw * inverse * gain_ref[...]
            turned = normed * cos_ref[...] + half_turn(normed) * sin_ref[...]
            out_ref[g, s] = jnp.where(turns, turned, raw).astype(BF)


def project(core, x, norm_gain, gain, cosine, sine, parts, chunk, chunk_orders):
    rows = cosine.shape[0]
    n_parts = len(parts[0])
    swaps = ([c * chunk for c in chunk_orders[0]], [c * chunk for c in chunk_orders[1]], chunk)
    return pl.pallas_call(
        functools.partial(project_kernel, n_parts, swaps),
        in_specs=[in_smem()] + [in_vmem()] * (5 + 2 * n_parts),
        out_specs=[in_vmem()] * 3,
        out_shape=[
            jax.ShapeDtypeStruct(x.shape, BF),
            jax.ShapeDtypeStruct((2 * rows, KV_HEADS * LANES), F32),
            jax.ShapeDtypeStruct((KV_HEADS, 2, rows, LANES), BF),
        ],
        compiler_params=params(),
        cost_estimate=pl.CostEstimate(flops=2 * x.shape[0] * x.shape[1] * KV_HEADS * LANES, bytes_accessed=8 << 20, transcendentals=0),
    )(core, x, norm_gain, gain, cosine, sine, *parts[0], *parts[1])


def unproject_kernel(core_ref, grad_ref, raw_ref, gain_ref, cos_ref, sin_ref, out_ref, gain_out_ref):
    rows = cos_ref.shape[0]
    is_value = core_ref[0] == 1
    for s in range(2):
        raw = raw_ref[s * rows : (s + 1) * rows]
        grad = grad_ref[0, s].astype(F32)
        low = low_lanes(raw.shape)
        inverse = lax.rsqrt(half_sums(raw * raw, low) * (1.0 / HEAD) + EPS)
        back = grad * cos_ref[...] + half_turn(grad * sin_ref[...])
        is_q_or_k = jnp.logical_or(low, jnp.logical_not(is_value))
        gain_rows = jnp.sum(back * raw * inverse, axis=0, keepdims=True)
        scaled = back * gain_ref[...]
        mean = half_sums(scaled * raw, low) * (1.0 / HEAD)
        moved = inverse * scaled - raw * (inverse * inverse * inverse) * mean
        out_ref[s * rows : (s + 1) * rows, :] = jnp.where(is_q_or_k, moved, grad).astype(BF)
        gain_rows = jnp.where(is_q_or_k[:1], gain_rows, 0.0)
        if s == 0:
            total = gain_rows
        else:
            total = total + gain_rows
    gain_out_ref[0] = jnp.broadcast_to(total, (8, LANES))


def unproject(core, grads, raw, gain, cosine, sine):
    rows = cosine.shape[0]
    return pl.pallas_call(
        unproject_kernel,
        grid=(KV_HEADS,),
        in_specs=[
            in_smem(),
            pl.BlockSpec((1, 2, rows, LANES), lambda g: (g, 0, 0, 0)),
            pl.BlockSpec((2 * rows, LANES), lambda g: (0, g)),
            pl.BlockSpec((1, LANES), lambda g: (0, 0)),
            pl.BlockSpec((rows, LANES), lambda g: (0, 0)),
            pl.BlockSpec((rows, LANES), lambda g: (0, 0)),
        ],
        out_specs=[
            pl.BlockSpec((2 * rows, LANES), lambda g: (0, g)),
            pl.BlockSpec((1, 8, LANES), lambda g: (g, 0, 0)),
        ],
        out_shape=[
            jax.ShapeDtypeStruct((2 * rows, KV_HEADS * LANES), BF),
            jax.ShapeDtypeStruct((KV_HEADS, 8, LANES), F32),
        ],
        compiler_params=params(),
        cost_estimate=pl.CostEstimate(flops=1 << 24, bytes_accessed=8 << 20, transcendentals=0),
    )(core, grads, raw, gain, cosine, sine)


def block_rows(ref, slot):
    return ref[pl.ds(pl.multiple_of(slot * BLOCK, BLOCK), BLOCK), :]


def sum_of_parts(value):
    first = value.astype(BF)
    rest = value - first.astype(F32)
    second = rest.astype(BF)
    third = (rest - second.astype(F32)).astype(BF)
    return first, second, third


def allowed_pairs(j, pos_row, start_row):
    key_pos = j * KT + lax.broadcasted_iota(I32, (KT, 1), 0)
    return jnp.logical_and(key_pos <= pos_row, key_pos >= start_row)


def walk_keys(lims_ref, i, step, carry):
    lo, full_lo, full_hi, hi = (lims_ref[e, i] for e in range(4))
    carry = lax.fori_loop(lo, full_lo, functools.partial(step, True), carry)
    carry = lax.fori_loop(full_lo, full_hi, functools.partial(step, False), carry)
    return lax.fori_loop(full_hi, hi, functools.partial(step, True), carry)


def attend_kernel(
    core_ref, kslot_ref, qslot_ref, lims_ref, q_ref, own_ref, other_ref, pos_ref, start_ref,
    out_ref, keep_ref, lse_ref, keys, values_t, placed,
):
    q_tiles = q_ref.shape[0] // QT
    k_tiles = own_ref.shape[0] // KT
    per = KT // BLOCK
    is_first = core_ref[0] == 0
    values_t[HEAD:, :] = jnp.ones((values_t.shape[0] - HEAD, values_t.shape[1]), BF)

    def load(t, carry):
        for b in range(per):
            slot = kslot_ref[t * per + b]
            own = block_rows(own_ref, slot)[:, HEAD:]
            other = block_rows(other_ref, slot)[:, HEAD:]
            at = pl.ds(pl.multiple_of((t * per + b) * BLOCK, BLOCK), BLOCK)
            keys[at, :] = jnp.where(is_first, own, other)
            value = jnp.where(is_first, other, own).astype(F32)
            values_t[:HEAD, at] = value.T.astype(BF)
        return carry

    lax.fori_loop(0, k_tiles, load, 0)

    def tile(i, carry):
        cols = pl.ds(pl.multiple_of(i * QT, QT), QT)
        parts = [block_rows(q_ref, qslot_ref[i * (QT // BLOCK) + b])[:, :HEAD] for b in range(QT // BLOCK)]
        query_t = (jnp.concatenate(parts, axis=0).astype(F32) * SCALE).T.astype(BF)
        pos_row = pos_ref[:, cols]
        start_row = start_ref[:, cols]

        def step(masked, j, acc):
            at = pl.ds(pl.multiple_of(j * KT, KT), KT)
            p = jnp.exp(dot(keys[at, :], query_t))
            if masked:
                p = jnp.where(allowed_pairs(j, pos_row, start_row), p, 0.0)
            return acc + dot(values_t[:, at], p.astype(BF))

        acc = walk_keys(lims_ref, i, step, jnp.zeros((values_t.shape[0], QT), F32))
        total = acc[HEAD : HEAD + 1]
        mixed = acc[:HEAD] / total
        keep_ref[:, cols] = mixed
        lse_ref[:, cols] = jnp.log(total)
        rows = mixed.T
        for b in range(QT // BLOCK):
            slot = qslot_ref[i * (QT // BLOCK) + b]
            placed[pl.ds(pl.multiple_of(slot * BLOCK, BLOCK), BLOCK), :] = rows[b * BLOCK : (b + 1) * BLOCK]
        return carry

    lax.fori_loop(0, q_tiles, tile, 0)

    def pack(c, carry):
        first = placed[pl.ds(pl.multiple_of(c * 2 * BLOCK, BLOCK), BLOCK), :]
        second = placed[pl.ds(pl.multiple_of((c * 2 + 1) * BLOCK, BLOCK), BLOCK), :]
        out_ref[pl.ds(pl.multiple_of(c * BLOCK, BLOCK), BLOCK), :] = jnp.concatenate([first, second], axis=1).astype(BF)
        return carry

    lax.fori_loop(0, q_ref.shape[0] // (2 * BLOCK), pack, 0)


def attend(core, tables, queries, own, other):
    kslot, qslot, lims, pos, start = tables
    n_q, n_k = queries.shape[0], own.shape[0]
    return pl.pallas_call(
        attend_kernel,
        in_specs=[in_smem()] * 4 + [in_vmem()] * 5,
        out_specs=[in_vmem()] * 3,
        out_shape=[
            jax.ShapeDtypeStruct((n_q // 2, LANES), BF),
            jax.ShapeDtypeStruct((HEAD, n_q), F32),
            jax.ShapeDtypeStruct((1, n_q), F32),
        ],
        scratch_shapes=[
            pltpu.VMEM((n_k, HEAD), BF),
            pltpu.VMEM((HEAD + 16, n_k), BF),
            pltpu.VMEM((n_q, HEAD), F32),
        ],
        compiler_params=params(),
        cost_estimate=pl.CostEstimate(flops=8 * n_q * n_k * HEAD, bytes_accessed=8 << 20, transcendentals=n_q * n_k),
    )(core, kslot, qslot, lims, queries, own, other, pos, start)


def attend_back_kernel(
    core_ref, kslot_ref, qslot_ref, lims_ref, q_ref, own_ref, other_ref, pos_ref, start_ref,
    grad_ref, mixed_ref, lse_ref,
    dq_ref, keep_ref, send_ref,
    keys, values, keys_t, grad_keys, grad_values, grad_placed,
):
    q_tiles = q_ref.shape[0] // QT
    k_tiles = own_ref.shape[0] // KT
    per = KT // BLOCK
    is_first = core_ref[0] == 0
    ones = jnp.ones((BLOCK, HEAD), BF)

    def load(t, carry):
        for b in range(per):
            slot = kslot_ref[t * per + b]
            own = block_rows(own_ref, slot)[:, HEAD:]
            other = block_rows(other_ref, slot)[:, HEAD:]
            at = pl.ds(pl.multiple_of((t * per + b) * BLOCK, BLOCK), BLOCK)
            key = jnp.where(is_first, own, other)
            value = jnp.where(is_first, other, own)
            keys[at, :] = jnp.concatenate([key, ones], axis=1)
            values[at, :] = jnp.concatenate([value, ones], axis=1)
            keys_t[:, at] = key.astype(F32).T.astype(BF)
            grad_keys[at, :] = jnp.zeros((BLOCK, HEAD), F32)
            grad_values[at, :] = jnp.zeros((BLOCK, HEAD), F32)
        return carry

    lax.fori_loop(0, k_tiles, load, 0)

    def unpack(c, carry):
        pair = grad_ref[pl.ds(pl.multiple_of(c * BLOCK, BLOCK), BLOCK), :]
        grad_placed[pl.ds(pl.multiple_of(c * 2 * BLOCK, BLOCK), BLOCK), :] = pair[:, :HEAD]
        grad_placed[pl.ds(pl.multiple_of((c * 2 + 1) * BLOCK, BLOCK), BLOCK), :] = pair[:, HEAD:]
        return carry

    lax.fori_loop(0, q_ref.shape[0] // (2 * BLOCK), unpack, 0)

    def tile(i, carry):
        cols = pl.ds(pl.multiple_of(i * QT, QT), QT)
        slots = [qslot_ref[i * (QT // BLOCK) + b] for b in range(QT // BLOCK)]
        query_f = jnp.concatenate([block_rows(q_ref, s)[:, :HEAD] for s in slots], axis=0).astype(F32) * SCALE
        grad = jnp.concatenate([block_rows(grad_placed, s) for s in slots], axis=0)
        query = query_f.astype(BF)
        grad_t = grad.astype(F32).T
        delta = jnp.sum(grad_t * mixed_ref[:, cols], axis=0, keepdims=True)
        pad = jnp.zeros((HEAD - 3, QT), F32)
        query_t = jnp.concatenate(
            [query_f.T] + [e.astype(F32) for e in sum_of_parts(-lse_ref[:, cols])] + [pad], axis=0
        ).astype(BF)
        grad_t = jnp.concatenate([grad_t] + [e.astype(F32) for e in sum_of_parts(-delta)] + [pad], axis=0).astype(BF)
        pos_row = pos_ref[:, cols]
        start_row = start_ref[:, cols]

        def step(masked, j, acc):
            at = pl.ds(pl.multiple_of(j * KT, KT), KT)
            p = jnp.exp(dot(keys[at, :], query_t))
            if masked:
                p = jnp.where(allowed_pairs(j, pos_row, start_row), p, 0.0)
            grad_s = (p * dot(values[at, :], grad_t)).astype(BF)
            grad_values[at, :] += dot(p.astype(BF), grad)
            grad_keys[at, :] += dot(grad_s, query)
            return acc + dot(keys_t[:, at], grad_s)

        acc = walk_keys(lims_ref, i, step, jnp.zeros((HEAD, QT), F32))
        rows = (acc * SCALE).T
        rows = jnp.concatenate([rows, jnp.zeros((QT, HEAD), F32)], axis=1)
        for b in range(QT // BLOCK):
            dq_ref[pl.ds(pl.multiple_of(slots[b] * BLOCK, BLOCK), BLOCK), :] = rows[b * BLOCK : (b + 1) * BLOCK]
        return carry

    lax.fori_loop(0, q_tiles, tile, 0)

    def place(t, carry):
        zeros = jnp.zeros((BLOCK, HEAD), F32)
        for b in range(per):
            slot = kslot_ref[t * per + b]
            at = pl.ds(pl.multiple_of((t * per + b) * BLOCK, BLOCK), BLOCK)
            to = pl.ds(pl.multiple_of(slot * BLOCK, BLOCK), BLOCK)
            key, value = grad_keys[at, :], grad_values[at, :]
            mine = jnp.where(is_first, key, value)
            theirs = jnp.where(is_first, value, key)
            keep_ref[to, :] = jnp.concatenate([zeros, mine], axis=1)
            send_ref[to, :] = jnp.concatenate([zeros, theirs], axis=1).astype(BF)
        return carry

    lax.fori_loop(0, k_tiles, place, 0)


def attend_back(core, tables, queries, own, other, grads, mixed, lse):
    kslot, qslot, lims, pos, start = tables
    n_q, n_k = queries.shape[0], own.shape[0]
    return pl.pallas_call(
        attend_back_kernel,
        in_specs=[in_smem()] * 4 + [in_vmem()] * 8,
        out_specs=[in_vmem()] * 3,
        out_shape=[
            jax.ShapeDtypeStruct((n_q, LANES), F32),
            jax.ShapeDtypeStruct((n_k, LANES), F32),
            jax.ShapeDtypeStruct((n_k, LANES), BF),
        ],
        scratch_shapes=[
            pltpu.VMEM((n_k, LANES), BF),
            pltpu.VMEM((n_k, LANES), BF),
            pltpu.VMEM((HEAD, n_k), BF),
            pltpu.VMEM((n_k, HEAD), F32),
            pltpu.VMEM((n_k, HEAD), F32),
            pltpu.VMEM((n_q, HEAD), BF),
        ],
        compiler_params=params(),
        cost_estimate=pl.CostEstimate(flops=16 * n_q * n_k * HEAD, bytes_accessed=8 << 20, transcendentals=n_q * n_k),
    )(core, kslot, qslot, lims, queries, own, other, pos, start, grads, mixed, lse)


def columns_of(value, chunk, order, part, parts):
    count = len(order) // parts
    pieces = [value[:, e * chunk : (e + 1) * chunk] for e in order[part * count : (part + 1) * count]]
    return jnp.concatenate(pieces, axis=1)


def in_order(values, chunk, order):
    joined = jnp.concatenate(values, axis=1)
    places = sorted(range(len(order)), key=lambda e: order[e])
    return jnp.concatenate([joined[:, e * chunk : (e + 1) * chunk] for e in places], axis=1)


def feed_kernel(n_parts, chunk, orders, n_ref, c_ref, *refs):
    first, second = refs[:n_parts], refs[n_parts : 2 * n_parts]
    mid_ref, gate_ref, up_ref, out_ref, back_ref, nt_ref = refs[2 * n_parts :]
    quarter = mid_ref.shape[1]
    split = first[0].shape[1] - quarter
    normed, upstream = n_ref[...], c_ref[...]

    def over_parts(value, order, parts, lo, hi):
        total = None
        for p, part in enumerate(parts):
            term = dot(columns_of(value, chunk, order, p, n_parts), part[:, lo:hi])
            total = term if total is None else total + term
        return total

    gate = over_parts(normed, orders[0], first, 0, quarter)
    up = over_parts(normed, orders[1], second, 0, quarter)
    down = jnp.concatenate(
        [
            over_parts(upstream, orders[0], first, quarter, quarter + split),
            over_parts(upstream, orders[1], second, quarter, 2 * quarter - split),
        ],
        axis=1,
    )
    sig = 1.0 / (1.0 + jnp.exp(-gate))
    silu = gate * sig
    mid_ref[...] = (silu * up).astype(BF)
    gate_ref[...] = (down * up * (sig * (1.0 + gate * (1.0 - sig)))).astype(BF)
    up_ref[...] = (down * silu).astype(BF)
    out_ref[...] = in_order(
        [dot(mid_ref[:, :split], part[:, quarter:], NT) for part in first], chunk, orders[0]
    ) + in_order([dot(mid_ref[:, split:], part[:, quarter:], NT) for part in second], chunk, orders[1])
    back = in_order([dot(gate_ref[...], part[:, :quarter], NT) for part in first], chunk, orders[0]) + in_order(
        [dot(up_ref[...], part[:, :quarter], NT) for part in second], chunk, orders[1]
    )
    back_ref[...] = back.astype(BF)
    nt_ref[...] = normed.T


def feed(n, c, parts, chunk, orders, quarter):
    rows, width = n.shape
    step = rows // 2
    tall = lambda cols: pl.BlockSpec((step, cols), lambda i: (i, 0))
    whole = [p for piece in parts for p in piece]
    return pl.pallas_call(
        functools.partial(feed_kernel, len(parts[0]), chunk, orders),
        grid=(2,),
        in_specs=[tall(width)] * 2 + [pl.BlockSpec(p.shape, lambda i: (0, 0)) for p in whole],
        out_specs=[tall(quarter)] * 3 + [tall(width)] * 2 + [pl.BlockSpec((width, step), lambda i: (0, i))],
        out_shape=[jax.ShapeDtypeStruct((rows, quarter), BF)] * 3
        + [jax.ShapeDtypeStruct(e, t) for e, t in (((rows, width), F32), ((rows, width), BF), ((width, rows), BF))],
        compiler_params=params(),
        cost_estimate=pl.CostEstimate(flops=12 * rows * width * quarter, bytes_accessed=16 << 20, transcendentals=0),
    )(n, c, *whole)


def turn_kernel(a_ref, b_ref, a_out_ref, b_out_ref):
    a_out_ref[...] = a_ref[...].T
    b_out_ref[...] = b_ref[...].T


def turn(a, b):
    return pl.pallas_call(
        turn_kernel,
        in_specs=[in_vmem()] * 2,
        out_specs=[in_vmem()] * 2,
        out_shape=[jax.ShapeDtypeStruct(v.shape[::-1], v.dtype) for v in (a, b)],
        compiler_params=params(),
        cost_estimate=pl.CostEstimate(flops=1 << 20, bytes_accessed=4 << 20, transcendentals=0),
    )(a, b)


def out_grad_kernel(core_ref, attn_ref, grad_ref, select_ref, unperm_ref, out_ref):
    half = unperm_ref.shape[1] // 2
    rel = dot(attn_ref[...], select_ref[...]).astype(BF).T
    cols = jnp.where(core_ref[0] == 0, unperm_ref[:, :half], unperm_ref[:, half:])
    out_ref[...] = dot(rel, dot(grad_ref[...], cols).astype(BF)).astype(BF)


def out_grad(core, attn, grad, select, unperm):
    width = select.shape[0]
    return pl.pallas_call(
        out_grad_kernel,
        in_specs=[in_smem()] + [in_vmem()] * 4,
        out_specs=in_vmem(),
        out_shape=jax.ShapeDtypeStruct((width, width // 2), BF),
        compiler_params=params(),
        cost_estimate=pl.CostEstimate(flops=4 << 30, bytes_accessed=8 << 20, transcendentals=0),
    )(core, attn, grad, select, unperm)


def feed_back_kernel(chunk, orders, *refs):
    (nt_a, ct_a, nt_b, ct_b, mid_a, gate_a, up_a, mid_b, gate_b, up_b), outs = refs[:10], refs[10:]
    quarter = mid_a.shape[1]
    split = outs[0].shape[1] - quarter
    height = outs[0].shape[0]
    per = height // chunk

    def rows_of(ref, order, place):
        return jnp.concatenate([ref[e * chunk : (e + 1) * chunk, :] for e in order[place * per : (place + 1) * per]], axis=0)

    def total(order, place, left_a, right_a, left_b, right_b):
        return (dot(rows_of(left_a, order, place), right_a) + dot(rows_of(left_b, order, place), right_b)).astype(BF)

    for i in range(2):

        @pl.when(pl.program_id(0) == i)
        def _():
            for side in range(2):
                place = side * 2 + i
                one, two = outs[side], outs[2 + side]
                one[:, :quarter] = total(orders[0], place, nt_a, gate_a[...], nt_b, gate_b[...])
                one[:, quarter:] = total(orders[0], place, ct_a, mid_a[:, :split], ct_b, mid_b[:, :split])
                two[:, :quarter] = total(orders[1], place, nt_a, up_a[...], nt_b, up_b[...])
                two[:, quarter:] = total(orders[1], place, ct_a, mid_a[:, split:], ct_b, mid_b[:, split:])


def feed_back(transposed, acts, chunk, orders, cols):
    width, rows = transposed[0].shape
    quarter = acts[0].shape[1]
    whole = lambda v: pl.BlockSpec(v.shape, lambda i: (0, 0))
    out = lambda c: pl.BlockSpec((width // 4, c), lambda i: (i, 0))
    return pl.pallas_call(
        functools.partial(feed_back_kernel, chunk, orders),
        grid=(2,),
        in_specs=[whole(v) for v in transposed] + [whole(v) for v in acts],
        out_specs=[out(cols[0])] * 2 + [out(cols[1])] * 2,
        out_shape=[jax.ShapeDtypeStruct((width // 2, c), BF) for c in (cols[0], cols[0], cols[1], cols[1])],
        compiler_params=params(),
        cost_estimate=pl.CostEstimate(flops=12 * rows * width * quarter, bytes_accessed=16 << 20, transcendentals=0),
    )(*transposed, *acts)


def down_split(quarter):
    return (quarter // 2 + LANES // 2) // LANES * LANES


def prepare_kernel(
    core_ref, table_ref, q_ref, k_ref, v_ref, o_ref, g_ref, u_ref, d_ref, ga_ref, gm_ref, flags_ref,
    mine_q_ref, theirs_q_ref, mine_f_ref, theirs_f_ref,
):
    first = core_ref[0] == 0
    owned, width = q_ref.shape

    def put(mine_ref, theirs_ref, at, zero, one):
        size = zero.shape[1]
        mine_ref[:, at : at + size] = jnp.where(first, zero, one).astype(BF)
        theirs_ref[:, at : at + size] = jnp.where(first, one, zero).astype(BF)

    for g in range(KV_HEADS):
        at = g * LANES
        kv = slice(g * HEAD, (g + 1) * HEAD)
        zero = jnp.concatenate([q_ref[:, at : at + HEAD], k_ref[:, kv]], axis=1)
        one = jnp.concatenate([q_ref[:, at + HEAD : at + LANES], v_ref[:, kv]], axis=1)
        put(mine_q_ref, theirs_q_ref, at, zero, one)
    shape = (owned, owned)
    diagonal = lax.broadcasted_iota(I32, shape, 0) == lax.broadcasted_iota(I32, shape, 1)
    gain_a = jnp.sum(jnp.where(diagonal, ga_ref[...], 0.0), axis=1, keepdims=True)
    gain_m = jnp.sum(jnp.where(diagonal, gm_ref[...], 0.0), axis=1, keepdims=True)
    count = flags_ref.shape[1]
    cols = count // owned
    row = lax.broadcasted_iota(I32, (owned, count), 0)
    col = lax.broadcasted_iota(I32, (owned, count), 1)
    spread = jnp.where(col // cols == row, flags_ref[...].astype(F32), 0.0).astype(BF)
    row = lax.broadcasted_iota(I32, (count, LANES), 0)
    col = lax.broadcasted_iota(I32, (count, LANES), 1)
    extra = dot(spread, jnp.where(row % cols == col - 3, 1.0, 0.0).astype(BF))
    row = lax.broadcasted_iota(I32, (owned, LANES), 0)
    col = lax.broadcasted_iota(I32, (owned, LANES), 1)
    blocks = jnp.where(row == 0, table_ref[0, 0], jnp.where(row == 1, table_ref[0, 1], 0)).astype(F32)
    extra = jnp.where(col == 0, gain_a, jnp.where(col == 1, gain_m, jnp.where(col == 2, blocks, extra)))
    put(mine_q_ref, theirs_q_ref, width, extra, extra)
    half = g_ref.shape[1] // 2
    quarter = half // 2
    split = down_split(quarter)
    for x in range(2):
        at = 2 * x * quarter * 3 // 2
        for ref, lo, hi in ((g_ref, 0, quarter), (d_ref, 0, split), (u_ref, 0, quarter), (d_ref, split, quarter)):
            zero = ref[:, x * quarter + lo : x * quarter + hi]
            one = ref[:, half + x * quarter + lo : half + x * quarter + hi]
            put(mine_f_ref, theirs_f_ref, at, zero, one)
            at += hi - lo
    put(mine_q_ref, theirs_q_ref, width + LANES, o_ref[:, : width // 2], o_ref[:, width // 2 :])


def prepare(core, table, *arrays):
    owned, width = arrays[0].shape
    cols = 3 * arrays[4].shape[1] // 2
    return pl.pallas_call(
        prepare_kernel,
        in_specs=[in_smem()] * 2 + [in_vmem()] * len(arrays),
        out_specs=[in_vmem()] * 4,
        out_shape=[jax.ShapeDtypeStruct((owned, width + LANES + width // 2), BF)] * 2 + [jax.ShapeDtypeStruct((owned, cols), BF)] * 2,
        compiler_params=params(),
    )(core, table, *arrays)


def deliver_kernel(core_ref, zero_ref, one_ref, other_ref, gate_ref, up_ref, down_ref):
    first = core_ref[0] == 0
    owned, half = gate_ref.shape[0], gate_ref.shape[1] // 2
    quarter = half // 2
    split = down_split(quarter)
    for x, ref in enumerate((zero_ref, one_ref)):
        at = 0
        for out, lo, hi in ((gate_ref, 0, quarter), (down_ref, 0, split), (up_ref, 0, quarter), (down_ref, split, quarter)):
            size = hi - lo
            kept = jnp.where(first, ref[:owned, at : at + size], ref[owned:, at : at + size])
            arrived = other_ref[:, x * 3 * quarter + at : x * 3 * quarter + at + size]
            out[:, x * quarter + lo : x * quarter + hi] = jnp.where(first, kept, arrived)
            out[:, half + x * quarter + lo : half + x * quarter + hi] = jnp.where(first, arrived, kept)
            at += size


def deliver(core, zero, one, other):
    owned, cols = other.shape
    return pl.pallas_call(
        deliver_kernel,
        in_specs=[in_smem()] + [in_vmem()] * 3,
        out_specs=[in_vmem()] * 3,
        out_shape=[jax.ShapeDtypeStruct((owned, 2 * cols // 3), F32)] * 3,
        compiler_params=params(),
    )(core, zero, one, other)


def deliver_heads_kernel(core_ref, qkv_ref, out_ref, other_ref, wo_ref, q_ref, k_ref, v_ref):
    first = core_ref[0] == 0
    owned, width = q_ref.shape
    half = width // 2

    def sides(ref, at, size, shift):
        kept = jnp.where(first, ref[:owned, at : at + size], ref[owned:, at : at + size])
        arrived = other_ref[:, shift + at : shift + at + size]
        return jnp.where(first, kept, arrived), jnp.where(first, arrived, kept)

    wo_ref[:, :half], wo_ref[:, half:] = sides(out_ref, 0, half, width)
    for g in range(0, KV_HEADS, 2):
        zero, one = sides(qkv_ref, g * LANES, LANES, 0)
        zero_next, one_next = sides(qkv_ref, (g + 1) * LANES, LANES, 0)
        q_ref[:, g * LANES : (g + 1) * LANES] = jnp.concatenate([zero[:, :HEAD], one[:, :HEAD]], axis=1)
        q_ref[:, (g + 1) * LANES : (g + 2) * LANES] = jnp.concatenate([zero_next[:, :HEAD], one_next[:, :HEAD]], axis=1)
        k_ref[:, g * HEAD : (g + 2) * HEAD] = jnp.concatenate([zero[:, HEAD:], zero_next[:, HEAD:]], axis=1)
        v_ref[:, g * HEAD : (g + 2) * HEAD] = jnp.concatenate([one[:, HEAD:], one_next[:, HEAD:]], axis=1)


def deliver_heads(core, qkv, out, other):
    owned, width = other.shape[0], qkv.shape[1]
    shapes = [(owned, width), (owned, width), (owned, width // 2), (owned, width // 2)]
    return pl.pallas_call(
        deliver_heads_kernel,
        in_specs=[in_smem()] + [in_vmem()] * 3,
        out_specs=[in_vmem()] * 4,
        out_shape=[jax.ShapeDtypeStruct(e, F32) for e in shapes],
        compiler_params=params(),
    )(core, qkv, out, other)


def leave_kernel(core_ref, own_ref, other_ref, x_ref, wo_ref, gain_ref, res_ref, n_ref, attn_ref, half_ref):
    half = KV_HEADS * HEAD
    for which, ref in enumerate((own_ref, other_ref)):
        for g in range(0, KV_HEADS, 2):
            for s in range(2):
                for j in range(2):
                    lanes = slice(j * HEAD, (j + 1) * HEAD)
                    a = ref[(g * 2 + s) * BLOCK : (g * 2 + s + 1) * BLOCK, lanes]
                    b = ref[((g + 1) * 2 + s) * BLOCK : ((g + 1) * 2 + s + 1) * BLOCK, lanes]
                    row, col = (s * 2 + j) * BLOCK, which * half + g * HEAD
                    attn_ref[row : row + BLOCK, col : col + LANES] = jnp.concatenate([a, b], axis=1)
    value = x_ref[...].astype(F32) + dot(attn_ref[...], wo_ref[...])
    res_ref[...] = value
    inverse = lax.rsqrt(jnp.mean(value * value, axis=-1, keepdims=True) + EPS)
    normed = (value * inverse * gain_ref[...]).astype(BF)
    n_ref[...] = normed
    rows = half_ref.shape[0]
    half_ref[...] = jnp.where(core_ref[0] == 0, normed[:rows], normed[rows:])


def leave(core, own, other, x, wo, gain):
    rows, width = x.shape
    return pl.pallas_call(
        leave_kernel,
        in_specs=[in_smem()] + [in_vmem()] * 5,
        out_specs=[in_vmem()] * 4,
        out_shape=[
            jax.ShapeDtypeStruct((rows, width), F32),
            jax.ShapeDtypeStruct((rows, width), BF),
            jax.ShapeDtypeStruct((rows, width), BF),
            jax.ShapeDtypeStruct((rows // 2, width), BF),
        ],
        compiler_params=params(),
        cost_estimate=pl.CostEstimate(flops=2 * rows * width * width, bytes_accessed=10 << 20, transcendentals=0),
    )(core, own, other, x, wo, gain)


def enter_kernel(
    core_ref, back_ref, other_ref, far_ref, far_other_ref, res_ref, c_ref, gain_ref, wo_ref,
    grad_ref, grad_b_ref, gain_out_ref, out_ref,
):
    value = res_ref[...]
    inverse = lax.rsqrt(jnp.mean(value * value, axis=-1, keepdims=True) + EPS)
    first = core_ref[0] == 0
    far, far_other = far_ref[...].astype(F32), far_other_ref[...].astype(F32)
    far_all = jnp.concatenate([jnp.where(first, far, far_other), jnp.where(first, far_other, far)], axis=0)
    grad = back_ref[...].astype(F32) + other_ref[...].astype(F32) + far_all
    gain_out_ref[...] = jnp.sum(grad * value * inverse, axis=0, keepdims=True)
    scaled = grad * gain_ref[...]
    mean = jnp.mean(scaled * value, axis=-1, keepdims=True)
    total = c_ref[...].astype(F32) + (inverse * scaled - value * (inverse * inverse * inverse) * mean)
    grad_ref[...] = total
    grad_b_ref[...] = total.astype(BF)
    heads = dot(grad_b_ref[...], wo_ref[: KV_HEADS * HEAD, :], NT).astype(BF)
    for g in range(KV_HEADS):
        for s in range(2):
            row = s * 2 * BLOCK
            lanes = slice(g * HEAD, (g + 1) * HEAD)
            out_ref[(g * 2 + s) * BLOCK : (g * 2 + s + 1) * BLOCK, :] = jnp.concatenate(
                [heads[row : row + BLOCK, lanes], heads[row + BLOCK : row + 2 * BLOCK, lanes]], axis=1
            )


def enter(core, back, other, far, far_other, residual, c, gain, wo):
    rows, width = residual.shape
    return pl.pallas_call(
        enter_kernel,
        in_specs=[in_smem()] + [in_vmem()] * 8,
        out_specs=[in_vmem()] * 4,
        out_shape=[
            jax.ShapeDtypeStruct((rows, width), F32),
            jax.ShapeDtypeStruct((rows, width), BF),
            jax.ShapeDtypeStruct((1, width), F32),
            jax.ShapeDtypeStruct((2 * KV_HEADS * BLOCK, LANES), BF),
        ],
        compiler_params=params(),
        cost_estimate=pl.CostEstimate(flops=rows * width * width, bytes_accessed=10 << 20, transcendentals=0),
    )(core, back, other, far, far_other, residual, c, gain, wo)


def rms(value, gain):
    inverse = lax.rsqrt(jnp.mean(value * value, axis=-1, keepdims=True) + EPS)
    return value * inverse * gain, inverse


def rms_back(value, inverse, gain, grad):
    scaled = grad * gain
    mean = jnp.mean(scaled * value, axis=-1, keepdims=True)
    moved = inverse * scaled - value * (inverse * inverse * inverse) * mean
    return moved, jnp.sum(grad * value * inverse, axis=0)


def rope_tables(positions):
    inv_freq = jnp.power(F32(1000000.0), -(2.0 * jnp.arange(HEAD // 2, dtype=F32)) / HEAD)
    angles = positions.astype(F32)[:, None] * inv_freq[None, :]
    cosine, sine = jnp.cos(angles), jnp.sin(angles)
    return (
        jnp.concatenate([cosine] * 4, axis=1),
        jnp.concatenate([-sine, sine, -sine, sine], axis=1),
    )


class Dim:
    def __init__(self, stride, size):
        self.stride, self.size = stride, size


def make_shards(n):
    if n == 16:
        dims = {"x": Dim(1, 2), "y": Dim(2, 2), "p": Dim(4, 2), "q": Dim(8, 2)}
        order_a, order_b, order_m, order_w = "qpxy", "qpyx", "xqpy", "xqyp"
    else:
        names = "abcdefghijkl"[: n.bit_length() - 1]
        dims = {name: Dim(1 << b, 2) for b, name in enumerate(names)}
        order_a = order_b = order_m = order_w = names
    groups = n // 16
    a2a_groups = None if groups == 1 else [[t * 16 + d for d in range(16)] for t in range(groups)]
    kv_groups = None if groups == 1 else [[t * 16 + d for t in range(groups)] for d in range(16)]

    def digits(order):
        places = []
        for r in range(n):
            place = {}
            for name in order:
                place[name] = r % dims[name].size
                r //= dims[name].size
            places.append(place)
        return places

    def place_in(order, base=order_a):
        found = {tuple(sorted(p.items())): r for r, p in enumerate(digits(order))}
        return [found[tuple(sorted(p.items()))] for p in digits(base)]

    def chips(me, order, absolute=None):
        out = []
        for place in digits(order):
            chip = me
            for name, digit in place.items():
                d = dims[name]
                at = (me // d.stride) % d.size
                to = digit if name == absolute else jnp.bitwise_xor(at, digit)
                chip = chip + (to - at) * d.stride
            out.append(chip)
        return jnp.stack(out).astype(I32)

    def ctx_send(value, pairs):
        return lax.ppermute(value, "ctx", pairs)

    def ctx_swap(value, stride):
        return ctx_send(value, [(i, i ^ stride) for i in range(n)])

    def core_swap(value):
        return lax.ppermute(value, "wt", [(0, 1), (1, 0)])

    def gather_dim(value, name):
        return [value, ctx_swap(value, dims[name].stride)]

    def join(parts):
        return parts[0] if len(parts) == 1 else jnp.concatenate(parts, axis=0)

    def gather_rows(parts, names):
        for name in names:
            parts = gather_dim(join(parts), name)
        return parts

    def hold(parts, *others):
        return parts[:-1] + [after(parts[-1], *others)]

    def scatter_begin(keep, send, name):
        return keep, ctx_swap(send.astype(BF), dims[name].stride)

    def scatter_next(state, name):
        keep, arrived = state
        half = keep.shape[0] // 2
        send = (keep[half:].astype(F32) + arrived[half:].astype(F32)).astype(BF)
        return keep[:half].astype(F32) + arrived[:half].astype(F32), ctx_swap(send, dims[name].stride)

    def scatter_end(state):
        keep, arrived = state
        return keep.astype(F32) + arrived.astype(F32)

    def scatter_rows(keep, send, names):
        state = scatter_begin(keep, send, names[-1])
        for name in reversed(names[:-1]):
            state = scatter_next(state, name)
        return scatter_end(state)

    def scatter_whole(value, names):
        half = value.shape[0] // 2
        return scatter_rows(value[:half], value[half:], names)

    def runs(places):
        out = []
        for p in places:
            if out and out[-1][1] == p:
                out[-1][1] = p + 1
            else:
                out.append([p, p + 1])
        return out

    def assemble(parts, order):
        total = sum(p.shape[0] for p in parts)
        unit, each = total // n, parts[0].shape[0] // (total // n)
        out = []
        for lo, hi in runs(place_in(order)):
            while lo < hi:
                part, at = lo // each, lo % each
                stop = min(hi, (part + 1) * each)
                out.append(parts[part][at * unit : (at + stop - lo) * unit])
                lo = stop
        return join(out)

    def columns_in(value, order):
        unit = value.shape[1] // n
        inverse = np.argsort(place_in(order)).tolist()
        pieces = [value[:, lo * unit : hi * unit] for lo, hi in runs(inverse)]
        return pieces[0] if len(pieces) == 1 else jnp.concatenate(pieces, axis=1)

    def after(value, *others):
        return lax.optimization_barrier((value,) + others)[0]

    def swap_heads(value):
        return lax.all_to_all(value, "ctx", 0, 0, axis_index_groups=a2a_groups, tiled=True)

    def shards(
        tokens, block_table, doc_flags, w_query, key_weight, value_weight, w_out, w_gate, w_up, w_down,
        gain_attn, gain_mlp, gain_q, key_norm_gain, cotangent,
    ):
        width = tokens.shape[-1]
        rows = tokens.shape[1]
        owned = w_query.shape[0]
        chip_rows = 2 * owned
        me = lax.axis_index("ctx")
        core = lax.axis_index("wt")
        first = core == 0
        core_arr = core.astype(I32).reshape(1)
        slots_n = 2 * n

        def by_core(a, b, axis=0):
            return jnp.where(first, jnp.concatenate([a, b], axis=axis), jnp.concatenate([b, a], axis=axis))

        def pick(a, b):
            return jnp.where(first, a, b)

        chip_of = chips(me, order_a)

        def features(order, absolute=None):
            chip = chips(me, order, absolute)
            return (chip[:, None] * chip_rows + jnp.arange(chip_rows, dtype=I32)[None, :]).reshape(-1)

        def spread(order, absolute=None):
            return (jnp.arange(width, dtype=I32)[:, None] == features(order, absolute)[None, :]).astype(BF)

        def collect(order, absolute=None):
            return (features(order, absolute)[:, None] == jnp.arange(width, dtype=I32)[None, :]).astype(BF)

        canon = features(order_a)
        perm, perm_m, unperm, unperm_m = lax.optimization_barrier(
            (spread(order_a), spread(order_m, order_m[0]), collect(order_a), collect(order_m, order_m[0]))
        )
        left = me % 2 == 0

        def pick_x(a, b):
            return jnp.where(left, a, b)

        def by_x(a, b, axis=0):
            return pick_x(jnp.concatenate([a, b], axis=axis), jnp.concatenate([b, a], axis=axis))

        flag_cols = rows // owned
        own_blocks = block_table[0]
        mine_q, theirs_q, mine_f, theirs_f = prepare(
            core_arr, block_table, w_query, key_weight, value_weight, w_out, w_gate, w_up, w_down,
            gain_attn[None, :], gain_mlp[None, :], doc_flags,
        )
        first_piece = by_core(mine_q, core_swap(theirs_q))
        acts = jnp.stack([tokens[0], cotangent[0]])
        acts_other = core_swap(acts)
        other_f = core_swap(theirs_f)
        x_two = dot(by_core(acts[0], acts_other[0]), perm).astype(BF)
        x_m = dot(by_core(acts[0], acts_other[0]), perm_m).astype(BF)
        c_m = dot(by_core(acts[1], acts_other[1]), perm_m).astype(BF)
        head_cols = width // 2
        out_cols = width // 4
        out_at = width + LANES

        def cut(value):
            first_cols = [value[:, :head_cols], value[:, width:out_at], value[:, out_at : out_at + out_cols]]
            second_cols = [value[:, head_cols:width], value[:, out_at + out_cols :]]
            return [jnp.concatenate(first_cols, axis=1)], [jnp.concatenate(second_cols, axis=1)]

        if n == 16:
            shared = cut(join(gather_rows([first_piece], "qp")))
            qkv_parts = [gather_rows(shared[0], "x"), gather_rows(shared[1], "y")]
            first_swap = qkv_parts[0][-1]
            qkv_parts = [gather_rows(hold(qkv_parts[0], x_two), "y"), gather_rows(qkv_parts[1], "x")]
        else:
            shared = cut(first_piece)
            qkv_parts = [gather_rows(shared[0], order_a), gather_rows(shared[1], order_b)]
            first_swap = first_piece
        chunk = LANES
        per = chunk // chip_rows
        chunk_orders = [[e // per for e in np.argsort(place_in(o)).tolist()[::per]] for o in (order_a, order_b)]
        extras = assemble([p[:, head_cols : head_cols + LANES] for p in qkv_parts[0]], order_a).astype(F32)
        wo_half = jnp.concatenate(
            [
                assemble([p[:, head_cols + LANES :] for p in qkv_parts[0]], order_a),
                assemble([p[:, head_cols:] for p in qkv_parts[1]], order_b),
            ],
            axis=1,
        )

        hidden = x_two.astype(F32)

        quarter = w_gate.shape[1] // 4
        feed_half = by_core(mine_f, other_f)
        feed_x = feed_half[:, : 3 * quarter], feed_half[:, 3 * quarter :]
        feed_near = pick_x(*feed_x)
        feed_far = after(ctx_swap(pick_x(feed_x[1], feed_x[0]), 1), *shared[0], *shared[1])
        feed_cut = quarter + down_split(quarter)
        feed_cols = (feed_cut, 3 * quarter - feed_cut)
        feed_orders = (order_m[1:], order_w[1:])
        feed_parts = [
            gather_rows([by_x(feed_near[:, lo:hi], feed_far[:, lo:hi])], feed_orders[e][:1])
            for e, (lo, hi) in enumerate(((0, feed_cut), (feed_cut, 3 * quarter)))
        ]

        gain_a, gain_m = extras[:, 0][None, :], extras[:, 1][None, :]
        lane = jnp.arange(BLOCK, dtype=I32)
        n_q = 32 * BLOCK
        own_pos = (own_blocks[:, None] * BLOCK + lane[None, :]).reshape(-1)
        cosine, sine = rope_tables(own_pos)
        gain_qk = jnp.concatenate([gain_q, key_norm_gain])[None, :]

        normed_ab, raw, packed = project(
            core_arr, x_two, gain_a, gain_qk, cosine, sine, qkv_parts, chunk, chunk_orders
        )
        feed_parts = [gather_rows(hold(feed_parts[e], packed), feed_orders[e][1:]) for e in range(2)]
        queries = swap_heads(packed.reshape(16, rows, LANES)).reshape(n_q, LANES)
        own_kv = queries
        gain_mm = dot(dot(jnp.broadcast_to(gain_m, (8, width)).astype(BF), unperm).astype(BF), perm_m)[:1]

        def from_pair(half):
            far = ctx_swap(half, 1)
            return by_core(far, core_swap(far))

        def mine(value):
            return pick(value[:rows], value[rows:])

        def not_mine(value):
            return pick(value[rows:], value[:rows])

        c_far = from_pair(after(mine(c_m), packed))
        if groups > 1:
            own_kv = lax.all_gather(queries, "ctx", axis=0, tiled=True, axis_index_groups=kv_groups)
        other_kv = core_swap(own_kv)
        wo_other = core_swap(wo_half)
        wo_full = by_core(wo_half, wo_other, axis=1)
        head_ids = jnp.arange(width, dtype=I32)
        place = (head_ids // 512).astype(I32)
        head_row = (((head_ids % 512) // HEAD) * 2 + jnp.bitwise_xor(core.astype(I32), place)) * HEAD + head_ids % HEAD
        select = (head_row[:, None] == canon[None, :]).astype(BF)
        wo_sel = dot(select, dot(wo_full, perm_m).astype(BF)).astype(BF)

        extras = after(extras, packed, wo_sel)
        per_chip = extras.reshape(n, 2, owned, LANES)
        block_of = per_chip[:, 0, :2, 2].reshape(-1).astype(I32)
        seq = me % 2
        flags = jnp.where(seq == 0, per_chip[:, 0], per_chip[:, 1])[:, :, 3 : 3 + flag_cols].reshape(slots_n, BLOCK)
        slot_of = (chip_of[:, None] * 2 + jnp.arange(2, dtype=I32)[None, :]).reshape(-1)
        ids = jnp.arange(slots_n, dtype=I32)
        hit = ids[:, None] == block_of[None, :]
        flags_pos = dot(hit.astype(BF), flags.astype(BF))
        kslot = jnp.sum(jnp.where(hit, slot_of[None, :], 0), axis=1)
        pos = jnp.arange(slots_n * BLOCK, dtype=I32).reshape(slots_n, BLOCK)
        begins = jnp.where(flags_pos > 0.5, pos, -1)
        lane = jnp.arange(BLOCK, dtype=I32)
        inside = jnp.max(jnp.where(lane[None, None, :] <= lane[None, :, None], begins[:, None, :], -1), axis=2)
        carried = jnp.max(jnp.where(ids[None, :] < ids[:, None], jnp.max(begins, axis=1)[None, :], -1), axis=1)
        doc_start = jnp.maximum(inside, carried[:, None])
        here = (slot_of // 32) == (me // 16)
        rank = jnp.sum((here[None, :] & (block_of[None, :] < block_of[:, None])).astype(I32), axis=1)
        hit_q = here[None, :] & (rank[None, :] == jnp.arange(32, dtype=I32)[:, None])
        q_block = jnp.sum(jnp.where(hit_q, block_of[None, :], 0), axis=1)
        qslot = jnp.sum(jnp.where(hit_q, slot_of[None, :] - (me // 16) * 32, 0), axis=1)
        q_pos = q_block[:, None] * BLOCK + lane[None, :]
        q_start = jnp.sum(jnp.where((q_block[:, None] == ids[None, :])[:, :, None], doc_start[None], 0), axis=1)
        n_q = 32 * BLOCK
        tile_start = q_start.reshape(n_q // QT, QT)
        tile_pos = q_pos.reshape(n_q // QT, QT)
        low, high = jnp.min(tile_start, axis=1) // KT, jnp.max(tile_pos, axis=1) // KT + 1
        full_low = jnp.minimum((jnp.max(tile_start, axis=1) + KT - 1) // KT, high)
        full_high = jnp.maximum(jnp.minimum((jnp.min(tile_pos, axis=1) + 1) // KT, high), full_low)
        lims = jnp.stack([low, full_low, full_high, high])
        tables = (kslot, qslot, lims, q_pos.reshape(1, n_q), q_start.reshape(1, n_q))

        mixed_packed, mixed, lse = attend(core_arr, tables, queries, own_kv, other_kv)

        attn_own = swap_heads(mixed_packed.reshape(16, BLOCK, LANES)).reshape(16 * BLOCK, LANES)
        residual, normed_m, attn, n_half = leave(core_arr, attn_own, core_swap(attn_own), x_m, wo_sel, gain_mm)

        n_far = from_pair(n_half)
        c_t, c_far_t = turn(c_m, c_far)
        per_chunk = LANES // chip_rows
        feed_chunks = [
            [e // per_chunk for e in np.argsort(place_in(o, order_m)).tolist()[::per_chunk]] for o in (order_m, order_w)
        ]
        *acts_near, out_near, back_near, n_t = feed(normed_m, c_m, feed_parts, LANES, feed_chunks, quarter)
        *acts_far, out_far, back_far, n_far_t = feed(n_far, c_far, feed_parts, LANES, feed_chunks, quarter)
        chip_far = (mine(back_far).astype(F32) + core_swap(not_mine(back_far)).astype(F32)).astype(BF)
        back_pair = ctx_swap(chip_far, 1)
        keep_a, send_a, keep_b, send_b = feed_back(
            (n_t, c_t, n_far_t, c_far_t), (*acts_near, *acts_far), LANES, feed_chunks, feed_cols
        )
        feed_sums = [
            scatter_begin(keep_a, send_a, feed_orders[0][-1]),
            scatter_begin(keep_b, send_b, feed_orders[1][-1]),
        ]
        grad_h, grad_hb, grad_gm, do_packed = enter(
            core_arr, back_near, core_swap(back_near), back_pair, core_swap(back_pair), residual, c_m, gain_mm, wo_sel
        )
        grads_in = swap_heads(do_packed.reshape(16, BLOCK, LANES)).reshape(n_q // 2, LANES)
        attn = after(attn, do_packed)

        out_other = core_swap(jnp.concatenate([not_mine(out_near), not_mine(out_far)]).astype(BF)).astype(F32)
        out_pair = ctx_swap((mine(out_far) + out_other[rows:]).astype(BF), 1).astype(F32)
        layer_rel = mine(residual) + (mine(out_near) + out_other[:rows] + out_pair)
        layer_out = dot(layer_rel.astype(BF), unperm_m).astype(BF)[None]

        grad_wo = out_grad(core_arr, attn, grad_hb, select, unperm_m)
        out_first = grad_wo[:, :out_cols]
        order_rows = np.argsort(place_in(order_b)).tolist()
        out_second = jnp.concatenate(
            [grad_wo[lo * chip_rows : hi * chip_rows, out_cols:] for lo, hi in runs(order_rows)], axis=0
        )

        dq, keep, send = attend_back(core_arr, tables, queries, own_kv, other_kv, grads_in, mixed, lse)
        feed_sums = [scatter_next(hold(list(feed_sums[e]), send), feed_orders[e][-2]) for e in range(2)]
        grad_kv = keep + core_swap(send).astype(F32)
        if groups > 1:
            grad_kv = lax.psum_scatter(grad_kv, "ctx", scatter_dimension=0, tiled=True, axis_index_groups=kv_groups)
        back = swap_heads((dq + grad_kv).astype(BF).reshape(16, rows, LANES))
        grad_qkv_in, gain_parts = unproject(core_arr, back.reshape(KV_HEADS, 2, rows, LANES), raw, gain_qk, cosine, sine)
        g_first, g_second = grad_qkv_in[:, : width // 2], grad_qkv_in[:, width // 2 :]

        def halves(value):
            half = value.shape[0] // 2
            return value[:half], value[half:]

        sum_first = jnp.concatenate([dot(normed_ab, g_first, TN).astype(BF), out_first], axis=1)
        sum_second = jnp.concatenate([dot(columns_in(normed_ab, order_b), g_second, TN).astype(BF), out_second], axis=1)
        level_holds = {}
        if n == 16:
            sum_first = scatter_begin(*halves(sum_first), "y")
            sum_second = scatter_begin(*halves(sum_second), "x")
            level_holds[3] = sum_first[1], sum_second[1]
            sum_first = scatter_next(sum_first, "x")
            sum_second = scatter_next(sum_second, "y")
            level_holds[4] = sum_first[1], sum_second[1]
            sums = jnp.concatenate([scatter_end(sum_first), scatter_end(sum_second)], axis=1)
            sums = scatter_whole(sums, "qp")
        else:
            sums = jnp.concatenate([scatter_whole(sum_first, order_a), scatter_whole(sum_second, order_b)], axis=1)
        cut_cols = head_cols + out_cols
        part_qkv = jnp.concatenate([sums[:, :head_cols], sums[:, cut_cols : cut_cols + head_cols]], axis=1)
        part_out = jnp.concatenate([sums[:, head_cols:cut_cols], sums[:, cut_cols + head_cols :]], axis=1)
        w_first = assemble([p[:, : width // 2] for p in qkv_parts[0]], order_a)
        w_second = assemble([p[:, : width // 2] for p in qkv_parts[1]], order_b)
        n1_part = dot(g_first, w_first, NT) + dot(g_second, w_second, NT)
        n1_other = core_swap(pick(n1_part[rows:], n1_part[:rows]))
        grad_n1 = pick(n1_part[:rows], n1_part[rows:]) + n1_other

        x_mine = mine(hidden)
        _, inv_a = rms(x_mine, gain_a)
        moved_a, grad_ga = rms_back(x_mine, inv_a, gain_a, grad_n1)

        def unspread(value, matrix):
            high = value.astype(BF)
            low = (value - high.astype(F32)).astype(BF)
            return dot(high, matrix) + dot(low, matrix)

        grad_input = (unspread(mine(grad_h), unperm_m) + unspread(moved_a, unperm))[None]

        def exact(vector, matrix):
            return lax.dot_general(
                vector, matrix.astype(F32), NN, precision=lax.Precision.HIGHEST, preferred_element_type=F32
            )

        vectors = jnp.concatenate([exact(grad_ga[None], unperm), exact(jnp.where(first, grad_gm, 0.0), unperm_m)])
        feed_levels = len(order_m)
        for level in range(3, feed_levels):
            feed_sums = [hold(list(v), *level_holds.get(level, ())) for v in feed_sums]
            feed_sums = [scatter_next(feed_sums[e], feed_orders[e][-level]) for e in range(2)]
        feed_sums = [scatter_end(hold(list(v), vectors)) for v in feed_sums]
        feed_near = jnp.concatenate([pick_x(v[:chip_rows], v[chip_rows:]) for v in feed_sums], axis=1)
        feed_far = jnp.concatenate([pick_x(v[chip_rows:], v[:chip_rows]) for v in feed_sums], axis=1)
        feed_far = ctx_swap(feed_far.astype(BF), 1).astype(F32)
        feed_zero, feed_one = pick_x(feed_near, feed_far), pick_x(feed_far, feed_near)
        heads_gain = jnp.sum(gain_parts[:, 0], axis=0)
        chip_gains = jnp.transpose(vectors.reshape(2, n, chip_rows), (1, 0, 2)).reshape(n, 2 * chip_rows)
        small = jnp.concatenate([chip_gains, jnp.broadcast_to(heads_gain[None], (n, LANES))], axis=1)
        small = jnp.pad(small, ((0, 0), (0, 2 * LANES - small.shape[1]))).reshape(n, 1, 2 * LANES)
        small = lax.all_to_all(jnp.broadcast_to(small, (n, 8, 2 * LANES)), "ctx", 0, 0, tiled=True)
        small = jnp.sum(small[:, 0], axis=0)
        small = small + core_swap(small)
        gains = small[: 2 * chip_rows].reshape(2, chip_rows)
        gains = pick(gains[:, :owned], gains[:, owned:])
        head_gains = small[2 * chip_rows : 2 * chip_rows + LANES]

        def theirs(parts):
            return jnp.concatenate([pick(p[owned:], p[:owned]) for p in parts], axis=1)

        grad_gate, grad_up, grad_down = deliver(
            core_arr, feed_zero, feed_one, core_swap(theirs([feed_zero, feed_one]))
        )
        grad_wout, grad_query, grad_key, grad_value = deliver_heads(
            core_arr, part_qkv, part_out, core_swap(theirs([part_qkv, part_out]))
        )
        return (
            layer_out,
            grad_input,
            grad_query,
            grad_key,
            grad_value,
            grad_wout,
            grad_gate,
            grad_up,
            grad_down,
            gains[0],
            gains[1],
            head_gains[:HEAD],
            head_gains[HEAD:],
        )

    return shards


def solution(mesh):
    seq = P("wt", "ctx", None)
    weight = P(("ctx", "wt"), None)
    vector = P(("ctx", "wt"))
    return jax.shard_map(
        make_shards(mesh.shape["ctx"]),
        mesh=mesh,
        in_specs=(seq, P("ctx", None), P("wt", "ctx")) + (weight,) * 7 + (vector, vector, P(), P(), seq),
        out_specs=(seq, seq) + (weight,) * 7 + (vector, vector, P(), P()),
        check_vma=False,
    )
```

```python
import functools

import jax
import jax.numpy as jnp
import numpy as np
from jax import lax
from jax.experimental import pallas as pl
from jax.experimental.pallas import tpu as pltpu
from jax.sharding import PartitionSpec as P

HEADS = 16
KV_HEADS = 8
HEAD = 64
LANES = 2 * HEAD
BLOCK = 128
EPS = 1e-05
SCALE = HEAD**-0.5
BF = jnp.bfloat16
F32 = jnp.float32
I32 = jnp.int32
QT = 512
KT = 512
VMEM_BYTES = 56 * 1024 * 1024

NN = (((1,), (0,)), ((), ()))
NT = (((1,), (1,)), ((), ()))
TN = (((0,), (0,)), ((), ()))


def dot(a, b, dims=NN):
    return lax.dot_general(a, b, dims, preferred_element_type=F32)


def params(**kw):
    return pltpu.CompilerParams(vmem_limit_bytes=VMEM_BYTES, **kw)


def in_vmem():
    return pl.BlockSpec(memory_space=pltpu.VMEM)


def in_smem():
    return pl.BlockSpec(memory_space=pltpu.SMEM)


def low_lanes(shape):
    return lax.broadcasted_iota(I32, shape, 1) < HEAD


def half_sums(value, low):
    total = jnp.sum(value, axis=-1, keepdims=True)
    first = jnp.sum(jnp.where(low, value, 0.0), axis=-1, keepdims=True)
    return jnp.where(low, first, total - first)


def half_turn(value):
    lane = lax.broadcasted_iota(I32, value.shape, 1)
    first = (lane % HEAD) < HEAD // 2
    return jnp.where(
        first,
        pltpu.roll(value, LANES - HEAD // 2, 1),
        pltpu.roll(value, HEAD // 2, 1),
    )


def project_kernel(n_parts, swaps, core_ref, x_ref, norm_gain_ref, gain_ref, cos_ref, sin_ref, *refs):
    weights, (n_ref, raw_ref, out_ref) = refs[: 2 * n_parts], refs[2 * n_parts :]
    rows = cos_ref.shape[0]
    is_value = core_ref[0] == 1
    x = x_ref[...].astype(F32)
    inverse = lax.rsqrt(jnp.mean(x * x, axis=-1, keepdims=True) + EPS)
    n_ref[...] = (x * inverse * norm_gain_ref[...]).astype(BF)
    groups = KV_HEADS // 2
    for half in range(2):
        total, at = None, 0
        for part in weights[half * n_parts : (half + 1) * n_parts]:
            length = part.shape[0]
            pieces = [n_ref[:, e : e + swaps[2]] for e in swaps[half][at // swaps[2] : (at + length) // swaps[2]]]
            left = pieces[0] if len(pieces) == 1 else jnp.concatenate(pieces, axis=1)
            term = dot(left, part[:, : groups * LANES])
            total = term if total is None else total + term
            at += length
        raw_ref[:, half * groups * LANES : (half + 1) * groups * LANES] = total
    low = low_lanes((rows, LANES))
    turns = jnp.logical_or(low, jnp.logical_not(is_value))
    for g in range(KV_HEADS):
        for s in range(2):
            raw = raw_ref[s * rows : (s + 1) * rows, g * LANES : (g + 1) * LANES]
            inverse = lax.rsqrt(half_sums(raw * raw, low) * (1.0 / HEAD) + EPS)
            normed = raw * inverse * gain_ref[...]
            turned = normed * cos_ref[...] + half_turn(normed) * sin_ref[...]
            out_ref[g, s] = jnp.where(turns, turned, raw).astype(BF)


def project(core, x, norm_gain, gain, cosine, sine, parts, chunk, chunk_orders):
    rows = cosine.shape[0]
    n_parts = len(parts[0])
    swaps = ([c * chunk for c in chunk_orders[0]], [c * chunk for c in chunk_orders[1]], chunk)
    return pl.pallas_call(
        functools.partial(project_kernel, n_parts, swaps),
        in_specs=[in_smem()] + [in_vmem()] * (5 + 2 * n_parts),
        out_specs=[in_vmem()] * 3,
        out_shape=[
            jax.ShapeDtypeStruct(x.shape, BF),
            jax.ShapeDtypeStruct((2 * rows, KV_HEADS * LANES), F32),
            jax.ShapeDtypeStruct((KV_HEADS, 2, rows, LANES), BF),
        ],
        compiler_params=params(),
        cost_estimate=pl.CostEstimate(flops=2 * x.shape[0] * x.shape[1] * KV_HEADS * LANES, bytes_accessed=8 << 20, transcendentals=0),
    )(core, x, norm_gain, gain, cosine, sine, *parts[0], *parts[1])


def unproject_kernel(core_ref, grad_ref, raw_ref, gain_ref, cos_ref, sin_ref, out_ref, gain_out_ref):
    rows = cos_ref.shape[0]
    is_value = core_ref[0] == 1
    for s in range(2):
        raw = raw_ref[s * rows : (s + 1) * rows]
        grad = grad_ref[0, s].astype(F32)
        low = low_lanes(raw.shape)
        inverse = lax.rsqrt(half_sums(raw * raw, low) * (1.0 / HEAD) + EPS)
        back = grad * cos_ref[...] + half_turn(grad * sin_ref[...])
        is_q_or_k = jnp.logical_or(low, jnp.logical_not(is_value))
        gain_rows = jnp.sum(back * raw * inverse, axis=0, keepdims=True)
        scaled = back * gain_ref[...]
        mean = half_sums(scaled * raw, low) * (1.0 / HEAD)
        moved = inverse * scaled - raw * (inverse * inverse * inverse) * mean
        out_ref[s * rows : (s + 1) * rows, :] = jnp.where(is_q_or_k, moved, grad).astype(BF)
        gain_rows = jnp.where(is_q_or_k[:1], gain_rows, 0.0)
        if s == 0:
            total = gain_rows
        else:
            total = total + gain_rows
    gain_out_ref[0] = jnp.broadcast_to(total, (8, LANES))


def unproject(core, grads, raw, gain, cosine, sine):
    rows = cosine.shape[0]
    return pl.pallas_call(
        unproject_kernel,
        grid=(KV_HEADS,),
        in_specs=[
            in_smem(),
            pl.BlockSpec((1, 2, rows, LANES), lambda g: (g, 0, 0, 0)),
            pl.BlockSpec((2 * rows, LANES), lambda g: (0, g)),
            pl.BlockSpec((1, LANES), lambda g: (0, 0)),
            pl.BlockSpec((rows, LANES), lambda g: (0, 0)),
            pl.BlockSpec((rows, LANES), lambda g: (0, 0)),
        ],
        out_specs=[
            pl.BlockSpec((2 * rows, LANES), lambda g: (0, g)),
            pl.BlockSpec((1, 8, LANES), lambda g: (g, 0, 0)),
        ],
        out_shape=[
            jax.ShapeDtypeStruct((2 * rows, KV_HEADS * LANES), BF),
            jax.ShapeDtypeStruct((KV_HEADS, 8, LANES), F32),
        ],
        compiler_params=params(),
        cost_estimate=pl.CostEstimate(flops=1 << 24, bytes_accessed=8 << 20, transcendentals=0),
    )(core, grads, raw, gain, cosine, sine)


def block_rows(ref, slot):
    return ref[pl.ds(pl.multiple_of(slot * BLOCK, BLOCK), BLOCK), :]


def sum_of_parts(value):
    first = value.astype(BF)
    rest = value - first.astype(F32)
    second = rest.astype(BF)
    third = (rest - second.astype(F32)).astype(BF)
    return first, second, third


def allowed_pairs(j, pos_row, start_row):
    key_pos = j * KT + lax.broadcasted_iota(I32, (KT, 1), 0)
    return jnp.logical_and(key_pos <= pos_row, key_pos >= start_row)


def walk_keys(lims_ref, i, step, carry):
    lo, full_lo, full_hi, hi = (lims_ref[e, i] for e in range(4))
    carry = lax.fori_loop(lo, full_lo, functools.partial(step, True), carry)
    carry = lax.fori_loop(full_lo, full_hi, functools.partial(step, False), carry)
    return lax.fori_loop(full_hi, hi, functools.partial(step, True), carry)


def attend_kernel(
    core_ref, kslot_ref, qslot_ref, lims_ref, q_ref, own_ref, other_ref, pos_ref, start_ref,
    out_ref, keep_ref, lse_ref, keys, values_t, placed,
):
    q_tiles = q_ref.shape[0] // QT
    k_tiles = own_ref.shape[0] // KT
    per = KT // BLOCK
    is_first = core_ref[0] == 0
    values_t[HEAD:, :] = jnp.ones((values_t.shape[0] - HEAD, values_t.shape[1]), BF)

    def load(t, carry):
        for b in range(per):
            slot = kslot_ref[t * per + b]
            own = block_rows(own_ref, slot)[:, HEAD:]
            other = block_rows(other_ref, slot)[:, HEAD:]
            at = pl.ds(pl.multiple_of((t * per + b) * BLOCK, BLOCK), BLOCK)
            keys[at, :] = jnp.where(is_first, own, other)
            value = jnp.where(is_first, other, own).astype(F32)
            values_t[:HEAD, at] = value.T.astype(BF)
        return carry

    lax.fori_loop(0, k_tiles, load, 0)

    def tile(i, carry):
        cols = pl.ds(pl.multiple_of(i * QT, QT), QT)
        parts = [block_rows(q_ref, qslot_ref[i * (QT // BLOCK) + b])[:, :HEAD] for b in range(QT // BLOCK)]
        query_t = (jnp.concatenate(parts, axis=0).astype(F32) * SCALE).T.astype(BF)
        pos_row = pos_ref[:, cols]
        start_row = start_ref[:, cols]

        def step(masked, j, acc):
            at = pl.ds(pl.multiple_of(j * KT, KT), KT)
            p = jnp.exp(dot(keys[at, :], query_t))
            if masked:
                p = jnp.where(allowed_pairs(j, pos_row, start_row), p, 0.0)
            return acc + dot(values_t[:, at], p.astype(BF))

        acc = walk_keys(lims_ref, i, step, jnp.zeros((values_t.shape[0], QT), F32))
        total = acc[HEAD : HEAD + 1]
        mixed = acc[:HEAD] / total
        keep_ref[:, cols] = mixed
        lse_ref[:, cols] = jnp.log(total)
        rows = mixed.T
        for b in range(QT // BLOCK):
            slot = qslot_ref[i * (QT // BLOCK) + b]
            placed[pl.ds(pl.multiple_of(slot * BLOCK, BLOCK), BLOCK), :] = rows[b * BLOCK : (b + 1) * BLOCK]
        return carry

    lax.fori_loop(0, q_tiles, tile, 0)

    def pack(c, carry):
        first = placed[pl.ds(pl.multiple_of(c * 2 * BLOCK, BLOCK), BLOCK), :]
        second = placed[pl.ds(pl.multiple_of((c * 2 + 1) * BLOCK, BLOCK), BLOCK), :]
        out_ref[pl.ds(pl.multiple_of(c * BLOCK, BLOCK), BLOCK), :] = jnp.concatenate([first, second], axis=1).astype(BF)
        return carry

    lax.fori_loop(0, q_ref.shape[0] // (2 * BLOCK), pack, 0)


def attend(core, tables, queries, own, other):
    kslot, qslot, lims, pos, start = tables
    n_q, n_k = queries.shape[0], own.shape[0]
    return pl.pallas_call(
        attend_kernel,
        in_specs=[in_smem()] * 4 + [in_vmem()] * 5,
        out_specs=[in_vmem()] * 3,
        out_shape=[
            jax.ShapeDtypeStruct((n_q // 2, LANES), BF),
            jax.ShapeDtypeStruct((HEAD, n_q), F32),
            jax.ShapeDtypeStruct((1, n_q), F32),
        ],
        scratch_shapes=[
            pltpu.VMEM((n_k, HEAD), BF),
            pltpu.VMEM((HEAD + 16, n_k), BF),
            pltpu.VMEM((n_q, HEAD), F32),
        ],
        compiler_params=params(),
        cost_estimate=pl.CostEstimate(flops=8 * n_q * n_k * HEAD, bytes_accessed=8 << 20, transcendentals=n_q * n_k),
    )(core, kslot, qslot, lims, queries, own, other, pos, start)


def attend_back_kernel(
    core_ref, kslot_ref, qslot_ref, lims_ref, q_ref, own_ref, other_ref, pos_ref, start_ref,
    grad_ref, mixed_ref, lse_ref,
    dq_ref, keep_ref, send_ref,
    keys, values, keys_t, grad_keys, grad_values, grad_placed,
):
    q_tiles = q_ref.shape[0] // QT
    k_tiles = own_ref.shape[0] // KT
    per = KT // BLOCK
    is_first = core_ref[0] == 0
    ones = jnp.ones((BLOCK, HEAD), BF)

    def load(t, carry):
        for b in range(per):
            slot = kslot_ref[t * per + b]
            own = block_rows(own_ref, slot)[:, HEAD:]
            other = block_rows(other_ref, slot)[:, HEAD:]
            at = pl.ds(pl.multiple_of((t * per + b) * BLOCK, BLOCK), BLOCK)
            key = jnp.where(is_first, own, other)
            value = jnp.where(is_first, other, own)
            keys[at, :] = jnp.concatenate([key, ones], axis=1)
            values[at, :] = jnp.concatenate([value, ones], axis=1)
            keys_t[:, at] = key.astype(F32).T.astype(BF)
            grad_keys[at, :] = jnp.zeros((BLOCK, HEAD), F32)
            grad_values[at, :] = jnp.zeros((BLOCK, HEAD), F32)
        return carry

    lax.fori_loop(0, k_tiles, load, 0)

    def unpack(c, carry):
        pair = grad_ref[pl.ds(pl.multiple_of(c * BLOCK, BLOCK), BLOCK), :]
        grad_placed[pl.ds(pl.multiple_of(c * 2 * BLOCK, BLOCK), BLOCK), :] = pair[:, :HEAD]
        grad_placed[pl.ds(pl.multiple_of((c * 2 + 1) * BLOCK, BLOCK), BLOCK), :] = pair[:, HEAD:]
        return carry

    lax.fori_loop(0, q_ref.shape[0] // (2 * BLOCK), unpack, 0)

    def tile(i, carry):
        cols = pl.ds(pl.multiple_of(i * QT, QT), QT)
        slots = [qslot_ref[i * (QT // BLOCK) + b] for b in range(QT // BLOCK)]
        query_f = jnp.concatenate([block_rows(q_ref, s)[:, :HEAD] for s in slots], axis=0).astype(F32) * SCALE
        grad = jnp.concatenate([block_rows(grad_placed, s) for s in slots], axis=0)
        query = query_f.astype(BF)
        grad_t = grad.astype(F32).T
        delta = jnp.sum(grad_t * mixed_ref[:, cols], axis=0, keepdims=True)
        pad = jnp.zeros((HEAD - 3, QT), F32)
        query_t = jnp.concatenate(
            [query_f.T] + [e.astype(F32) for e in sum_of_parts(-lse_ref[:, cols])] + [pad], axis=0
        ).astype(BF)
        grad_t = jnp.concatenate([grad_t] + [e.astype(F32) for e in sum_of_parts(-delta)] + [pad], axis=0).astype(BF)
        pos_row = pos_ref[:, cols]
        start_row = start_ref[:, cols]

        def step(masked, j, acc):
            at = pl.ds(pl.multiple_of(j * KT, KT), KT)
            p = jnp.exp(dot(keys[at, :], query_t))
            if masked:
                p = jnp.where(allowed_pairs(j, pos_row, start_row), p, 0.0)
            grad_s = (p * dot(values[at, :], grad_t)).astype(BF)
            grad_values[at, :] += dot(p.astype(BF), grad)
            grad_keys[at, :] += dot(grad_s, query)
            return acc + dot(keys_t[:, at], grad_s)

        acc = walk_keys(lims_ref, i, step, jnp.zeros((HEAD, QT), F32))
        rows = (acc * SCALE).T
        rows = jnp.concatenate([rows, jnp.zeros((QT, HEAD), F32)], axis=1)
        for b in range(QT // BLOCK):
            dq_ref[pl.ds(pl.multiple_of(slots[b] * BLOCK, BLOCK), BLOCK), :] = rows[b * BLOCK : (b + 1) * BLOCK]
        return carry

    lax.fori_loop(0, q_tiles, tile, 0)

    def place(t, carry):
        zeros = jnp.zeros((BLOCK, HEAD), F32)
        for b in range(per):
            slot = kslot_ref[t * per + b]
            at = pl.ds(pl.multiple_of((t * per + b) * BLOCK, BLOCK), BLOCK)
            to = pl.ds(pl.multiple_of(slot * BLOCK, BLOCK), BLOCK)
            key, value = grad_keys[at, :], grad_values[at, :]
            mine = jnp.where(is_first, key, value)
            theirs = jnp.where(is_first, value, key)
            keep_ref[to, :] = jnp.concatenate([zeros, mine], axis=1)
            send_ref[to, :] = jnp.concatenate([zeros, theirs], axis=1).astype(BF)
        return carry

    lax.fori_loop(0, k_tiles, place, 0)


def attend_back(core, tables, queries, own, other, grads, mixed, lse):
    kslot, qslot, lims, pos, start = tables
    n_q, n_k = queries.shape[0], own.shape[0]
    return pl.pallas_call(
        attend_back_kernel,
        in_specs=[in_smem()] * 4 + [in_vmem()] * 8,
        out_specs=[in_vmem()] * 3,
        out_shape=[
            jax.ShapeDtypeStruct((n_q, LANES), F32),
            jax.ShapeDtypeStruct((n_k, LANES), F32),
            jax.ShapeDtypeStruct((n_k, LANES), BF),
        ],
        scratch_shapes=[
            pltpu.VMEM((n_k, LANES), BF),
            pltpu.VMEM((n_k, LANES), BF),
            pltpu.VMEM((HEAD, n_k), BF),
            pltpu.VMEM((n_k, HEAD), F32),
            pltpu.VMEM((n_k, HEAD), F32),
            pltpu.VMEM((n_q, HEAD), BF),
        ],
        compiler_params=params(),
        cost_estimate=pl.CostEstimate(flops=16 * n_q * n_k * HEAD, bytes_accessed=8 << 20, transcendentals=n_q * n_k),
    )(core, kslot, qslot, lims, queries, own, other, pos, start, grads, mixed, lse)


def columns_of(value, chunk, order, part, parts):
    count = len(order) // parts
    pieces = [value[:, e * chunk : (e + 1) * chunk] for e in order[part * count : (part + 1) * count]]
    return jnp.concatenate(pieces, axis=1)


def in_order(values, chunk, order):
    joined = jnp.concatenate(values, axis=1)
    places = sorted(range(len(order)), key=lambda e: order[e])
    return jnp.concatenate([joined[:, e * chunk : (e + 1) * chunk] for e in places], axis=1)


def feed_kernel(n_parts, chunk, orders, n_ref, c_ref, *refs):
    first, second = refs[:n_parts], refs[n_parts : 2 * n_parts]
    mid_ref, gate_ref, up_ref, out_ref, back_ref, nt_ref = refs[2 * n_parts :]
    quarter = mid_ref.shape[1]
    split = first[0].shape[1] - quarter
    normed, upstream = n_ref[...], c_ref[...]

    def over_parts(value, order, parts, lo, hi):
        total = None
        for p, part in enumerate(parts):
            term = dot(columns_of(value, chunk, order, p, n_parts), part[:, lo:hi])
            total = term if total is None else total + term
        return total

    gate = over_parts(normed, orders[0], first, 0, quarter)
    up = over_parts(normed, orders[1], second, 0, quarter)
    down = jnp.concatenate(
        [
            over_parts(upstream, orders[0], first, quarter, quarter + split),
            over_parts(upstream, orders[1], second, quarter, 2 * quarter - split),
        ],
        axis=1,
    )
    sig = 1.0 / (1.0 + jnp.exp(-gate))
    silu = gate * sig
    mid_ref[...] = (silu * up).astype(BF)
    gate_ref[...] = (down * up * (sig * (1.0 + gate * (1.0 - sig)))).astype(BF)
    up_ref[...] = (down * silu).astype(BF)
    out_ref[...] = in_order(
        [dot(mid_ref[:, :split], part[:, quarter:], NT) for part in first], chunk, orders[0]
    ) + in_order([dot(mid_ref[:, split:], part[:, quarter:], NT) for part in second], chunk, orders[1])
    back = in_order([dot(gate_ref[...], part[:, :quarter], NT) for part in first], chunk, orders[0]) + in_order(
        [dot(up_ref[...], part[:, :quarter], NT) for part in second], chunk, orders[1]
    )
    back_ref[...] = back.astype(BF)
    nt_ref[...] = normed.T


def feed(n, c, parts, chunk, orders, quarter):
    rows, width = n.shape
    step = rows // 2
    tall = lambda cols: pl.BlockSpec((step, cols), lambda i: (i, 0))
    whole = [p for piece in parts for p in piece]
    return pl.pallas_call(
        functools.partial(feed_kernel, len(parts[0]), chunk, orders),
        grid=(2,),
        in_specs=[tall(width)] * 2 + [pl.BlockSpec(p.shape, lambda i: (0, 0)) for p in whole],
        out_specs=[tall(quarter)] * 3 + [tall(width)] * 2 + [pl.BlockSpec((width, step), lambda i: (0, i))],
        out_shape=[jax.ShapeDtypeStruct((rows, quarter), BF)] * 3
        + [jax.ShapeDtypeStruct(e, t) for e, t in (((rows, width), F32), ((rows, width), BF), ((width, rows), BF))],
        compiler_params=params(),
        cost_estimate=pl.CostEstimate(flops=12 * rows * width * quarter, bytes_accessed=16 << 20, transcendentals=0),
    )(n, c, *whole)


def turn_kernel(a_ref, b_ref, a_out_ref, b_out_ref):
    a_out_ref[...] = a_ref[...].T
    b_out_ref[...] = b_ref[...].T


def turn(a, b):
    return pl.pallas_call(
        turn_kernel,
        in_specs=[in_vmem()] * 2,
        out_specs=[in_vmem()] * 2,
        out_shape=[jax.ShapeDtypeStruct(v.shape[::-1], v.dtype) for v in (a, b)],
        compiler_params=params(),
        cost_estimate=pl.CostEstimate(flops=1 << 20, bytes_accessed=4 << 20, transcendentals=0),
    )(a, b)


def out_grad_kernel(core_ref, attn_ref, grad_ref, select_ref, unperm_ref, out_ref):
    half = unperm_ref.shape[1] // 2
    rel = dot(attn_ref[...], select_ref[...]).astype(BF).T
    cols = jnp.where(core_ref[0] == 0, unperm_ref[:, :half], unperm_ref[:, half:])
    out_ref[...] = dot(rel, dot(grad_ref[...], cols).astype(BF)).astype(BF)


def out_grad(core, attn, grad, select, unperm):
    width = select.shape[0]
    return pl.pallas_call(
        out_grad_kernel,
        in_specs=[in_smem()] + [in_vmem()] * 4,
        out_specs=in_vmem(),
        out_shape=jax.ShapeDtypeStruct((width, width // 2), BF),
        compiler_params=params(),
        cost_estimate=pl.CostEstimate(flops=4 << 30, bytes_accessed=8 << 20, transcendentals=0),
    )(core, attn, grad, select, unperm)


def feed_back_kernel(chunk, orders, *refs):
    (nt_a, ct_a, nt_b, ct_b, mid_a, gate_a, up_a, mid_b, gate_b, up_b), outs = refs[:10], refs[10:]
    quarter = mid_a.shape[1]
    split = outs[0].shape[1] - quarter
    height = outs[0].shape[0]
    per = height // chunk

    def rows_of(ref, order, place):
        return jnp.concatenate([ref[e * chunk : (e + 1) * chunk, :] for e in order[place * per : (place + 1) * per]], axis=0)

    def total(order, place, left_a, right_a, left_b, right_b):
        return (dot(rows_of(left_a, order, place), right_a) + dot(rows_of(left_b, order, place), right_b)).astype(BF)

    for i in range(2):

        @pl.when(pl.program_id(0) == i)
        def _():
            for side in range(2):
                place = side * 2 + i
                one, two = outs[side], outs[2 + side]
                one[:, :quarter] = total(orders[0], place, nt_a, gate_a[...], nt_b, gate_b[...])
                one[:, quarter:] = total(orders[0], place, ct_a, mid_a[:, :split], ct_b, mid_b[:, :split])
                two[:, :quarter] = total(orders[1], place, nt_a, up_a[...], nt_b, up_b[...])
                two[:, quarter:] = total(orders[1], place, ct_a, mid_a[:, split:], ct_b, mid_b[:, split:])


def feed_back(transposed, acts, chunk, orders, cols):
    width, rows = transposed[0].shape
    quarter = acts[0].shape[1]
    whole = lambda v: pl.BlockSpec(v.shape, lambda i: (0, 0))
    out = lambda c: pl.BlockSpec((width // 4, c), lambda i: (i, 0))
    return pl.pallas_call(
        functools.partial(feed_back_kernel, chunk, orders),
        grid=(2,),
        in_specs=[whole(v) for v in transposed] + [whole(v) for v in acts],
        out_specs=[out(cols[0])] * 2 + [out(cols[1])] * 2,
        out_shape=[jax.ShapeDtypeStruct((width // 2, c), BF) for c in (cols[0], cols[0], cols[1], cols[1])],
        compiler_params=params(),
        cost_estimate=pl.CostEstimate(flops=12 * rows * width * quarter, bytes_accessed=16 << 20, transcendentals=0),
    )(*transposed, *acts)


def down_split(quarter):
    return (quarter // 2 + LANES // 2) // LANES * LANES


def prepare_kernel(
    core_ref, table_ref, q_ref, k_ref, v_ref, o_ref, g_ref, u_ref, d_ref, ga_ref, gm_ref, flags_ref,
    mine_q_ref, theirs_q_ref, mine_f_ref, theirs_f_ref,
):
    first = core_ref[0] == 0
    owned, width = q_ref.shape

    def put(mine_ref, theirs_ref, at, zero, one):
        size = zero.shape[1]
        mine_ref[:, at : at + size] = jnp.where(first, zero, one).astype(BF)
        theirs_ref[:, at : at + size] = jnp.where(first, one, zero).astype(BF)

    for g in range(KV_HEADS):
        at = g * LANES
        kv = slice(g * HEAD, (g + 1) * HEAD)
        zero = jnp.concatenate([q_ref[:, at : at + HEAD], k_ref[:, kv]], axis=1)
        one = jnp.concatenate([q_ref[:, at + HEAD : at + LANES], v_ref[:, kv]], axis=1)
        put(mine_q_ref, theirs_q_ref, at, zero, one)
    shape = (owned, owned)
    diagonal = lax.broadcasted_iota(I32, shape, 0) == lax.broadcasted_iota(I32, shape, 1)
    gain_a = jnp.sum(jnp.where(diagonal, ga_ref[...], 0.0), axis=1, keepdims=True)
    gain_m = jnp.sum(jnp.where(diagonal, gm_ref[...], 0.0), axis=1, keepdims=True)
    count = flags_ref.shape[1]
    cols = count // owned
    row = lax.broadcasted_iota(I32, (owned, count), 0)
    col = lax.broadcasted_iota(I32, (owned, count), 1)
    spread = jnp.where(col // cols == row, flags_ref[...].astype(F32), 0.0).astype(BF)
    row = lax.broadcasted_iota(I32, (count, LANES), 0)
    col = lax.broadcasted_iota(I32, (count, LANES), 1)
    extra = dot(spread, jnp.where(row % cols == col - 3, 1.0, 0.0).astype(BF))
    row = lax.broadcasted_iota(I32, (owned, LANES), 0)
    col = lax.broadcasted_iota(I32, (owned, LANES), 1)
    blocks = jnp.where(row == 0, table_ref[0, 0], jnp.where(row == 1, table_ref[0, 1], 0)).astype(F32)
    extra = jnp.where(col == 0, gain_a, jnp.where(col == 1, gain_m, jnp.where(col == 2, blocks, extra)))
    put(mine_q_ref, theirs_q_ref, width, extra, extra)
    half = g_ref.shape[1] // 2
    quarter = half // 2
    split = down_split(quarter)
    for x in range(2):
        at = 2 * x * quarter * 3 // 2
        for ref, lo, hi in ((g_ref, 0, quarter), (d_ref, 0, split), (u_ref, 0, quarter), (d_ref, split, quarter)):
            zero = ref[:, x * quarter + lo : x * quarter + hi]
            one = ref[:, half + x * quarter + lo : half + x * quarter + hi]
            put(mine_f_ref, theirs_f_ref, at, zero, one)
            at += hi - lo
    put(mine_q_ref, theirs_q_ref, width + LANES, o_ref[:, : width // 2], o_ref[:, width // 2 :])


def prepare(core, table, *arrays):
    owned, width = arrays[0].shape
    cols = 3 * arrays[4].shape[1] // 2
    return pl.pallas_call(
        prepare_kernel,
        in_specs=[in_smem()] * 2 + [in_vmem()] * len(arrays),
        out_specs=[in_vmem()] * 4,
        out_shape=[jax.ShapeDtypeStruct((owned, width + LANES + width // 2), BF)] * 2 + [jax.ShapeDtypeStruct((owned, cols), BF)] * 2,
        compiler_params=params(),
    )(core, table, *arrays)


def deliver_kernel(core_ref, zero_ref, one_ref, other_ref, gate_ref, up_ref, down_ref):
    first = core_ref[0] == 0
    owned, half = gate_ref.shape[0], gate_ref.shape[1] // 2
    quarter = half // 2
    split = down_split(quarter)
    for x, ref in enumerate((zero_ref, one_ref)):
        at = 0
        for out, lo, hi in ((gate_ref, 0, quarter), (down_ref, 0, split), (up_ref, 0, quarter), (down_ref, split, quarter)):
            size = hi - lo
            kept = jnp.where(first, ref[:owned, at : at + size], ref[owned:, at : at + size])
            arrived = other_ref[:, x * 3 * quarter + at : x * 3 * quarter + at + size]
            out[:, x * quarter + lo : x * quarter + hi] = jnp.where(first, kept, arrived)
            out[:, half + x * quarter + lo : half + x * quarter + hi] = jnp.where(first, arrived, kept)
            at += size


def deliver(core, zero, one, other):
    owned, cols = other.shape
    return pl.pallas_call(
        deliver_kernel,
        in_specs=[in_smem()] + [in_vmem()] * 3,
        out_specs=[in_vmem()] * 3,
        out_shape=[jax.ShapeDtypeStruct((owned, 2 * cols // 3), F32)] * 3,
        compiler_params=params(),
    )(core, zero, one, other)


def deliver_heads_kernel(core_ref, qkv_ref, out_ref, other_ref, wo_ref, q_ref, k_ref, v_ref):
    first = core_ref[0] == 0
    owned, width = q_ref.shape
    half = width // 2

    def sides(ref, at, size, shift):
        kept = jnp.where(first, ref[:owned, at : at + size], ref[owned:, at : at + size])
        arrived = other_ref[:, shift + at : shift + at + size]
        return jnp.where(first, kept, arrived), jnp.where(first, arrived, kept)

    wo_ref[:, :half], wo_ref[:, half:] = sides(out_ref, 0, half, width)
    for g in range(0, KV_HEADS, 2):
        zero, one = sides(qkv_ref, g * LANES, LANES, 0)
        zero_next, one_next = sides(qkv_ref, (g + 1) * LANES, LANES, 0)
        q_ref[:, g * LANES : (g + 1) * LANES] = jnp.concatenate([zero[:, :HEAD], one[:, :HEAD]], axis=1)
        q_ref[:, (g + 1) * LANES : (g + 2) * LANES] = jnp.concatenate([zero_next[:, :HEAD], one_next[:, :HEAD]], axis=1)
        k_ref[:, g * HEAD : (g + 2) * HEAD] = jnp.concatenate([zero[:, HEAD:], zero_next[:, HEAD:]], axis=1)
        v_ref[:, g * HEAD : (g + 2) * HEAD] = jnp.concatenate([one[:, HEAD:], one_next[:, HEAD:]], axis=1)


def deliver_heads(core, qkv, out, other):
    owned, width = other.shape[0], qkv.shape[1]
    shapes = [(owned, width), (owned, width), (owned, width // 2), (owned, width // 2)]
    return pl.pallas_call(
        deliver_heads_kernel,
        in_specs=[in_smem()] + [in_vmem()] * 3,
        out_specs=[in_vmem()] * 4,
        out_shape=[jax.ShapeDtypeStruct(e, F32) for e in shapes],
        compiler_params=params(),
    )(core, qkv, out, other)


def leave_kernel(core_ref, own_ref, other_ref, x_ref, wo_ref, gain_ref, res_ref, n_ref, attn_ref, half_ref):
    half = KV_HEADS * HEAD
    for which, ref in enumerate((own_ref, other_ref)):
        for g in range(0, KV_HEADS, 2):
            for s in range(2):
                for j in range(2):
                    lanes = slice(j * HEAD, (j + 1) * HEAD)
                    a = ref[(g * 2 + s) * BLOCK : (g * 2 + s + 1) * BLOCK, lanes]
                    b = ref[((g + 1) * 2 + s) * BLOCK : ((g + 1) * 2 + s + 1) * BLOCK, lanes]
                    row, col = (s * 2 + j) * BLOCK, which * half + g * HEAD
                    attn_ref[row : row + BLOCK, col : col + LANES] = jnp.concatenate([a, b], axis=1)
    value = x_ref[...].astype(F32) + dot(attn_ref[...], wo_ref[...])
    res_ref[...] = value
    inverse = lax.rsqrt(jnp.mean(value * value, axis=-1, keepdims=True) + EPS)
    normed = (value * inverse * gain_ref[...]).astype(BF)
    n_ref[...] = normed
    rows = half_ref.shape[0]
    half_ref[...] = jnp.where(core_ref[0] == 0, normed[:rows], normed[rows:])


def leave(core, own, other, x, wo, gain):
    rows, width = x.shape
    return pl.pallas_call(
        leave_kernel,
        in_specs=[in_smem()] + [in_vmem()] * 5,
        out_specs=[in_vmem()] * 4,
        out_shape=[
            jax.ShapeDtypeStruct((rows, width), F32),
            jax.ShapeDtypeStruct((rows, width), BF),
            jax.ShapeDtypeStruct((rows, width), BF),
            jax.ShapeDtypeStruct((rows // 2, width), BF),
        ],
        compiler_params=params(),
        cost_estimate=pl.CostEstimate(flops=2 * rows * width * width, bytes_accessed=10 << 20, transcendentals=0),
    )(core, own, other, x, wo, gain)


def enter_kernel(
    core_ref, back_ref, other_ref, far_ref, far_other_ref, res_ref, c_ref, gain_ref, wo_ref,
    grad_ref, grad_b_ref, gain_out_ref, out_ref,
):
    value = res_ref[...]
    inverse = lax.rsqrt(jnp.mean(value * value, axis=-1, keepdims=True) + EPS)
    first = core_ref[0] == 0
    far, far_other = far_ref[...].astype(F32), far_other_ref[...].astype(F32)
    far_all = jnp.concatenate([jnp.where(first, far, far_other), jnp.where(first, far_other, far)], axis=0)
    grad = back_ref[...].astype(F32) + other_ref[...].astype(F32) + far_all
    gain_out_ref[...] = jnp.sum(grad * value * inverse, axis=0, keepdims=True)
    scaled = grad * gain_ref[...]
    mean = jnp.mean(scaled * value, axis=-1, keepdims=True)
    total = c_ref[...].astype(F32) + (inverse * scaled - value * (inverse * inverse * inverse) * mean)
    grad_ref[...] = total
    grad_b_ref[...] = total.astype(BF)
    heads = dot(grad_b_ref[...], wo_ref[: KV_HEADS * HEAD, :], NT).astype(BF)
    for g in range(KV_HEADS):
        for s in range(2):
            row = s * 2 * BLOCK
            lanes = slice(g * HEAD, (g + 1) * HEAD)
            out_ref[(g * 2 + s) * BLOCK : (g * 2 + s + 1) * BLOCK, :] = jnp.concatenate(
                [heads[row : row + BLOCK, lanes], heads[row + BLOCK : row + 2 * BLOCK, lanes]], axis=1
            )


def enter(core, back, other, far, far_other, residual, c, gain, wo):
    rows, width = residual.shape
    return pl.pallas_call(
        enter_kernel,
        in_specs=[in_smem()] + [in_vmem()] * 8,
        out_specs=[in_vmem()] * 4,
        out_shape=[
            jax.ShapeDtypeStruct((rows, width), F32),
            jax.ShapeDtypeStruct((rows, width), BF),
            jax.ShapeDtypeStruct((1, width), F32),
            jax.ShapeDtypeStruct((2 * KV_HEADS * BLOCK, LANES), BF),
        ],
        compiler_params=params(),
        cost_estimate=pl.CostEstimate(flops=rows * width * width, bytes_accessed=10 << 20, transcendentals=0),
    )(core, back, other, far, far_other, residual, c, gain, wo)


def rms(value, gain):
    inverse = lax.rsqrt(jnp.mean(value * value, axis=-1, keepdims=True) + EPS)
    return value * inverse * gain, inverse


def rms_back(value, inverse, gain, grad):
    scaled = grad * gain
    mean = jnp.mean(scaled * value, axis=-1, keepdims=True)
    moved = inverse * scaled - value * (inverse * inverse * inverse) * mean
    return moved, jnp.sum(grad * value * inverse, axis=0)


def rope_tables(positions):
    inv_freq = jnp.power(F32(1000000.0), -(2.0 * jnp.arange(HEAD // 2, dtype=F32)) / HEAD)
    angles = positions.astype(F32)[:, None] * inv_freq[None, :]
    cosine, sine = jnp.cos(angles), jnp.sin(angles)
    return (
        jnp.concatenate([cosine] * 4, axis=1),
        jnp.concatenate([-sine, sine, -sine, sine], axis=1),
    )


class Dim:
    def __init__(self, stride, size):
        self.stride, self.size = stride, size


def make_shards(n):
    if n == 16:
        dims = {"x": Dim(1, 2), "y": Dim(2, 2), "p": Dim(4, 2), "q": Dim(8, 2)}
        order_a, order_b, order_m, order_w = "qpxy", "qpyx", "xqpy", "xqyp"
    else:
        names = "abcdefghijkl"[: n.bit_length() - 1]
        dims = {name: Dim(1 << b, 2) for b, name in enumerate(names)}
        order_a = order_b = order_m = order_w = names
    groups = n // 16
    a2a_groups = None if groups == 1 else [[t * 16 + d for d in range(16)] for t in range(groups)]
    kv_groups = None if groups == 1 else [[t * 16 + d for t in range(groups)] for d in range(16)]

    def digits(order):
        places = []
        for r in range(n):
            place = {}
            for name in order:
                place[name] = r % dims[name].size
                r //= dims[name].size
            places.append(place)
        return places

    def place_in(order, base=order_a):
        found = {tuple(sorted(p.items())): r for r, p in enumerate(digits(order))}
        return [found[tuple(sorted(p.items()))] for p in digits(base)]

    def chips(me, order, absolute=None):
        out = []
        for place in digits(order):
            chip = me
            for name, digit in place.items():
                d = dims[name]
                at = (me // d.stride) % d.size
                to = digit if name == absolute else jnp.bitwise_xor(at, digit)
                chip = chip + (to - at) * d.stride
            out.append(chip)
        return jnp.stack(out).astype(I32)

    def ctx_send(value, pairs):
        return lax.ppermute(value, "ctx", pairs)

    def ctx_swap(value, stride):
        return ctx_send(value, [(i, i ^ stride) for i in range(n)])

    def core_swap(value):
        return lax.ppermute(value, "wt", [(0, 1), (1, 0)])

    def gather_dim(value, name):
        return [value, ctx_swap(value, dims[name].stride)]

    def join(parts):
        return parts[0] if len(parts) == 1 else jnp.concatenate(parts, axis=0)

    def gather_rows(parts, names):
        for name in names:
            parts = gather_dim(join(parts), name)
        return parts

    def hold(parts, *others):
        return parts[:-1] + [after(parts[-1], *others)]

    def scatter_begin(keep, send, name):
        return keep, ctx_swap(send.astype(BF), dims[name].stride)

    def scatter_next(state, name):
        keep, arrived = state
        half = keep.shape[0] // 2
        send = (keep[half:].astype(F32) + arrived[half:].astype(F32)).astype(BF)
        keep = (keep[:half].astype(F32) + arrived[:half].astype(F32)).astype(BF)
        return keep, ctx_swap(send, dims[name].stride)

    def scatter_end(state):
        keep, arrived = state
        return keep.astype(F32) + arrived.astype(F32)

    def scatter_rows(keep, send, names):
        state = scatter_begin(keep, send, names[-1])
        for name in reversed(names[:-1]):
            state = scatter_next(state, name)
        return scatter_end(state)

    def scatter_whole(value, names):
        half = value.shape[0] // 2
        return scatter_rows(value[:half], value[half:], names)

    def runs(places):
        out = []
        for p in places:
            if out and out[-1][1] == p:
                out[-1][1] = p + 1
            else:
                out.append([p, p + 1])
        return out

    def assemble(parts, order):
        total = sum(p.shape[0] for p in parts)
        unit, each = total // n, parts[0].shape[0] // (total // n)
        out = []
        for lo, hi in runs(place_in(order)):
            while lo < hi:
                part, at = lo // each, lo % each
                stop = min(hi, (part + 1) * each)
                out.append(parts[part][at * unit : (at + stop - lo) * unit])
                lo = stop
        return join(out)

    def columns_in(value, order):
        unit = value.shape[1] // n
        inverse = np.argsort(place_in(order)).tolist()
        pieces = [value[:, lo * unit : hi * unit] for lo, hi in runs(inverse)]
        return pieces[0] if len(pieces) == 1 else jnp.concatenate(pieces, axis=1)

    def after(value, *others):
        return lax.optimization_barrier((value,) + others)[0]

    def swap_heads(value):
        return lax.all_to_all(value, "ctx", 0, 0, axis_index_groups=a2a_groups, tiled=True)

    def shards(
        tokens, block_table, doc_flags, w_query, key_weight, value_weight, w_out, w_gate, w_up, w_down,
        gain_attn, gain_mlp, gain_q, key_norm_gain, cotangent,
    ):
        width = tokens.shape[-1]
        rows = tokens.shape[1]
        owned = w_query.shape[0]
        chip_rows = 2 * owned
        me = lax.axis_index("ctx")
        core = lax.axis_index("wt")
        first = core == 0
        core_arr = core.astype(I32).reshape(1)
        slots_n = 2 * n

        def by_core(a, b, axis=0):
            return jnp.where(first, jnp.concatenate([a, b], axis=axis), jnp.concatenate([b, a], axis=axis))

        def pick(a, b):
            return jnp.where(first, a, b)

        chip_of = chips(me, order_a)

        def features(order, me, absolute=None):
            chip = chips(me, order, absolute)
            return (chip[:, None] * chip_rows + jnp.arange(chip_rows, dtype=I32)[None, :]).reshape(-1)

        def spread(order, me, absolute=None):
            return (jnp.arange(width, dtype=I32)[:, None] == features(order, me, absolute)[None, :]).astype(BF)

        def collect(order, me, absolute=None):
            return (features(order, me, absolute)[:, None] == jnp.arange(width, dtype=I32)[None, :]).astype(BF)

        left = me % 2 == 0

        def pick_x(a, b):
            return jnp.where(left, a, b)

        def by_x(a, b, axis=0):
            return pick_x(jnp.concatenate([a, b], axis=axis), jnp.concatenate([b, a], axis=axis))

        flag_cols = rows // owned
        own_blocks = block_table[0]
        mine_q, theirs_q, mine_f, theirs_f = prepare(
            core_arr, block_table, w_query, key_weight, value_weight, w_out, w_gate, w_up, w_down,
            gain_attn[None, :], gain_mlp[None, :], doc_flags,
        )
        first_piece = by_core(mine_q, core_swap(theirs_q))
        acts = jnp.stack([after(tokens[0], mine_q), after(cotangent[0], mine_q)])
        acts_other = core_swap(acts)
        other_f = core_swap(theirs_f)
        me_later = after(me.astype(I32), first_piece)
        canon = features(order_a, me_later)
        perm, perm_m, unperm, unperm_m = lax.optimization_barrier(
            (spread(order_a, me_later), spread(order_m, me_later, order_m[0]), collect(order_a, me_later), collect(order_m, me_later, order_m[0]))
        )
        x_two = dot(by_core(acts[0], acts_other[0]), perm).astype(BF)
        x_m = dot(by_core(acts[0], acts_other[0]), perm_m).astype(BF)
        c_m = dot(by_core(acts[1], acts_other[1]), perm_m).astype(BF)
        head_cols = width // 2
        quarter = w_gate.shape[1] // 4
        feed_half = by_core(mine_f, other_f)
        feed_x = feed_half[:, : 3 * quarter], feed_half[:, 3 * quarter :]
        feed_near = pick_x(*feed_x)
        feed_far = ctx_swap(pick_x(feed_x[1], feed_x[0]), 1)
        out_cols = width // 4
        out_at = width + LANES

        def cut(value):
            first_cols = [value[:, :head_cols], value[:, width:out_at], value[:, out_at : out_at + out_cols]]
            second_cols = [value[:, head_cols:width], value[:, out_at + out_cols :]]
            return [jnp.concatenate(first_cols, axis=1)], [jnp.concatenate(second_cols, axis=1)]

        if n == 16:
            halfway = hold(gather_rows([first_piece], "q"), feed_far)
            feed_far = after(feed_far, halfway[-1])
            shared = cut(join(gather_rows(halfway, "p")))
            qkv_parts = [gather_rows(shared[0], "x"), gather_rows(shared[1], "y")]
            first_swap = qkv_parts[0][-1]
            qkv_parts = [gather_rows(hold(qkv_parts[0], x_two), "y"), gather_rows(qkv_parts[1], "x")]
        else:
            shared = cut(first_piece)
            qkv_parts = [gather_rows(shared[0], order_a), gather_rows(shared[1], order_b)]
            first_swap = first_piece
        chunk = LANES
        per = chunk // chip_rows
        chunk_orders = [[e // per for e in np.argsort(place_in(o)).tolist()[::per]] for o in (order_a, order_b)]
        extras = assemble([p[:, head_cols : head_cols + LANES] for p in qkv_parts[0]], order_a).astype(F32)
        wo_half = jnp.concatenate(
            [
                assemble([p[:, head_cols + LANES :] for p in qkv_parts[0]], order_a),
                assemble([p[:, head_cols:] for p in qkv_parts[1]], order_b),
            ],
            axis=1,
        )

        hidden = x_two.astype(F32)

        feed_cut = quarter + down_split(quarter)
        feed_cols = (feed_cut, 3 * quarter - feed_cut)
        feed_orders = (order_m[1:], order_w[1:])
        feed_parts = [
            gather_rows([by_x(feed_near[:, lo:hi], feed_far[:, lo:hi])], feed_orders[e][:1])
            for e, (lo, hi) in enumerate(((0, feed_cut), (feed_cut, 3 * quarter)))
        ]

        gain_a, gain_m = extras[:, 0][None, :], extras[:, 1][None, :]
        lane = jnp.arange(BLOCK, dtype=I32)
        n_q = 32 * BLOCK
        own_pos = (own_blocks[:, None] * BLOCK + lane[None, :]).reshape(-1)
        cosine, sine = rope_tables(own_pos)
        gain_qk = jnp.concatenate([gain_q, key_norm_gain])[None, :]

        normed_ab, raw, packed = project(
            core_arr, x_two, gain_a, gain_qk, cosine, sine, qkv_parts, chunk, chunk_orders
        )
        feed_parts = [gather_rows(hold(feed_parts[e], packed), feed_orders[e][1:]) for e in range(2)]
        queries = swap_heads(packed.reshape(16, rows, LANES)).reshape(n_q, LANES)
        own_kv = queries
        gain_mm = dot(dot(jnp.broadcast_to(gain_m, (8, width)).astype(BF), unperm).astype(BF), perm_m)[:1]

        def from_pair(half):
            far = ctx_swap(half, 1)
            return jnp.concatenate([far, core_swap(far)])

        def mine(value):
            return pick(value[:rows], value[rows:])

        def not_mine(value):
            return pick(value[rows:], value[:rows])

        c_far = from_pair(after(mine(c_m), packed))
        if groups > 1:
            own_kv = lax.all_gather(queries, "ctx", axis=0, tiled=True, axis_index_groups=kv_groups)
        other_kv = core_swap(own_kv)
        wo_other = core_swap(wo_half)
        wo_full = by_core(wo_half, wo_other, axis=1)
        head_ids = jnp.arange(width, dtype=I32)
        place = (head_ids // 512).astype(I32)
        head_row = (((head_ids % 512) // HEAD) * 2 + jnp.bitwise_xor(core.astype(I32), place)) * HEAD + head_ids % HEAD
        select = (head_row[:, None] == canon[None, :]).astype(BF)
        wo_sel = dot(select, dot(wo_full, perm_m).astype(BF)).astype(BF)

        extras = after(extras, packed, wo_sel)
        per_chip = extras.reshape(n, 2, owned, LANES)
        block_of = per_chip[:, 0, :2, 2].reshape(-1).astype(I32)
        seq = me % 2
        flags = jnp.where(seq == 0, per_chip[:, 0], per_chip[:, 1])[:, :, 3 : 3 + flag_cols].reshape(slots_n, BLOCK)
        slot_of = (chip_of[:, None] * 2 + jnp.arange(2, dtype=I32)[None, :]).reshape(-1)
        ids = jnp.arange(slots_n, dtype=I32)
        hit = ids[:, None] == block_of[None, :]
        flags_pos = dot(hit.astype(BF), flags.astype(BF))
        kslot = jnp.sum(jnp.where(hit, slot_of[None, :], 0), axis=1)
        pos = jnp.arange(slots_n * BLOCK, dtype=I32).reshape(slots_n, BLOCK)
        begins = jnp.where(flags_pos > 0.5, pos, -1)
        lane = jnp.arange(BLOCK, dtype=I32)
        inside = jnp.max(jnp.where(lane[None, None, :] <= lane[None, :, None], begins[:, None, :], -1), axis=2)
        carried = jnp.max(jnp.where(ids[None, :] < ids[:, None], jnp.max(begins, axis=1)[None, :], -1), axis=1)
        doc_start = jnp.maximum(inside, carried[:, None])
        here = (slot_of // 32) == (me // 16)
        rank = jnp.sum((here[None, :] & (block_of[None, :] < block_of[:, None])).astype(I32), axis=1)
        hit_q = here[None, :] & (rank[None, :] == jnp.arange(32, dtype=I32)[:, None])
        q_block = jnp.sum(jnp.where(hit_q, block_of[None, :], 0), axis=1)
        qslot = jnp.sum(jnp.where(hit_q, slot_of[None, :] - (me // 16) * 32, 0), axis=1)
        q_pos = q_block[:, None] * BLOCK + lane[None, :]
        q_start = jnp.sum(jnp.where((q_block[:, None] == ids[None, :])[:, :, None], doc_start[None], 0), axis=1)
        n_q = 32 * BLOCK
        tile_start = q_start.reshape(n_q // QT, QT)
        tile_pos = q_pos.reshape(n_q // QT, QT)
        low, high = jnp.min(tile_start, axis=1) // KT, jnp.max(tile_pos, axis=1) // KT + 1
        full_low = jnp.minimum((jnp.max(tile_start, axis=1) + KT - 1) // KT, high)
        full_high = jnp.maximum(jnp.minimum((jnp.min(tile_pos, axis=1) + 1) // KT, high), full_low)
        lims = jnp.stack([low, full_low, full_high, high])
        tables = (kslot, qslot, lims, q_pos.reshape(1, n_q), q_start.reshape(1, n_q))

        mixed_packed, mixed, lse = attend(core_arr, tables, queries, own_kv, other_kv)

        attn_own = swap_heads(mixed_packed.reshape(16, BLOCK, LANES)).reshape(16 * BLOCK, LANES)
        residual, normed_m, attn, n_half = leave(core_arr, attn_own, core_swap(attn_own), x_m, wo_sel, gain_mm)

        n_far = from_pair(n_half)
        c_t, c_far_t = turn(c_m, c_far)
        per_chunk = LANES // chip_rows
        feed_chunks = [
            [e // per_chunk for e in np.argsort(place_in(o, order_m)).tolist()[::per_chunk]] for o in (order_m, order_w)
        ]
        *acts_near, out_near, back_near, n_t = feed(normed_m, c_m, feed_parts, LANES, feed_chunks, quarter)
        *acts_far, out_far, back_far, n_far_t = feed(after(n_far, c_t, c_far_t), c_far, feed_parts, LANES, feed_chunks, quarter)
        chip_far = (back_far[:rows].astype(F32) + core_swap(back_far[rows:]).astype(F32)).astype(BF)
        back_pair = ctx_swap(chip_far, 1)
        keep_a, send_a, keep_b, send_b = feed_back(
            (n_t, c_t, n_far_t, c_far_t), (*acts_near, *acts_far), LANES, feed_chunks, feed_cols
        )
        feed_sums = [
            scatter_begin(keep_a, send_a, feed_orders[0][-1]),
            scatter_begin(keep_b, send_b, feed_orders[1][-1]),
        ]
        grad_h, grad_hb, grad_gm, do_packed = enter(
            core_arr, back_near, core_swap(back_near), back_pair, core_swap(back_pair), residual, c_m, gain_mm, wo_sel
        )
        grads_in = swap_heads(do_packed.reshape(16, BLOCK, LANES)).reshape(n_q // 2, LANES)
        attn = after(attn, do_packed)

        out_other = core_swap(jnp.concatenate([not_mine(out_near), out_far[rows:]]).astype(BF)).astype(F32)
        out_pair = ctx_swap((out_far[:rows] + out_other[rows:]).astype(BF), 1).astype(F32)
        layer_rel = mine(residual) + (mine(out_near) + out_other[:rows] + out_pair)
        layer_out = dot(layer_rel.astype(BF), unperm_m).astype(BF)[None]

        grad_wo = out_grad(core_arr, attn, grad_hb, select, unperm_m)
        out_first = grad_wo[:, :out_cols]
        order_rows = np.argsort(place_in(order_b)).tolist()
        out_second = jnp.concatenate(
            [grad_wo[lo * chip_rows : hi * chip_rows, out_cols:] for lo, hi in runs(order_rows)], axis=0
        )

        grads_in = after(grads_in, send_a, send_b)
        dq, keep, send = attend_back(core_arr, tables, queries, own_kv, other_kv, grads_in, mixed, lse)
        feed_sums = [scatter_next(hold(list(feed_sums[e]), send), feed_orders[e][-2]) for e in range(2)]
        grad_kv = keep + core_swap(send).astype(F32)
        if groups > 1:
            grad_kv = lax.psum_scatter(grad_kv, "ctx", scatter_dimension=0, tiled=True, axis_index_groups=kv_groups)
        payload = (dq + grad_kv).astype(BF)
        back = swap_heads(payload.reshape(16, rows, LANES))
        grad_qkv_in, gain_parts = unproject(core_arr, back.reshape(KV_HEADS, 2, rows, LANES), raw, gain_qk, cosine, sine)
        g_first, g_second = grad_qkv_in[:, : width // 2], grad_qkv_in[:, width // 2 :]

        def halves(value):
            half = value.shape[0] // 2
            return value[:half], value[half:]

        sum_first = jnp.concatenate([dot(normed_ab, g_first, TN).astype(BF), out_first], axis=1)
        sum_second = jnp.concatenate([dot(columns_in(normed_ab, order_b), g_second, TN).astype(BF), out_second], axis=1)
        level_holds = {}
        if n == 16:
            sum_first = scatter_begin(*halves(sum_first), "y")
            sum_second = scatter_begin(*halves(sum_second), "x")
            level_holds[3] = sum_first[1], sum_second[1]
            sum_first = scatter_next(sum_first, "x")
            sum_second = scatter_next(sum_second, "y")
            level_holds[4] = sum_first[1], sum_second[1]
            sums = jnp.concatenate([scatter_end(sum_first), scatter_end(sum_second)], axis=1)
            sums = scatter_whole(sums, "qp")
        else:
            sums = jnp.concatenate([scatter_whole(sum_first, order_a), scatter_whole(sum_second, order_b)], axis=1)
        cut_cols = head_cols + out_cols
        part_qkv = jnp.concatenate([sums[:, :head_cols], sums[:, cut_cols : cut_cols + head_cols]], axis=1)
        part_out = jnp.concatenate([sums[:, head_cols:cut_cols], sums[:, cut_cols + head_cols :]], axis=1)
        w_first = assemble([p[:, : width // 2] for p in qkv_parts[0]], order_a)
        w_second = assemble([p[:, : width // 2] for p in qkv_parts[1]], order_b)
        n1_part = dot(g_first, w_first, NT) + dot(g_second, w_second, NT)
        n1_other = core_swap(pick(n1_part[rows:], n1_part[:rows]))
        grad_n1 = pick(n1_part[:rows], n1_part[rows:]) + n1_other

        x_mine = mine(hidden)
        _, inv_a = rms(x_mine, gain_a)
        moved_a, grad_ga = rms_back(x_mine, inv_a, gain_a, grad_n1)

        def unspread(value, matrix):
            high = value.astype(BF)
            low = (value - high.astype(F32)).astype(BF)
            return dot(high, matrix) + dot(low, matrix)

        grad_input = (unspread(mine(grad_h), unperm_m) + unspread(moved_a, unperm))[None]

        def exact(vector, matrix):
            return lax.dot_general(
                vector, matrix.astype(F32), NN, precision=lax.Precision.HIGHEST, preferred_element_type=F32
            )

        vectors = jnp.concatenate([exact(grad_ga[None], unperm), exact(jnp.where(first, grad_gm, 0.0), unperm_m)])
        feed_levels = len(order_m)
        for level in range(3, feed_levels):
            feed_sums = [hold(list(v), *level_holds.get(level, ())) for v in feed_sums]
            feed_sums = [scatter_next(feed_sums[e], feed_orders[e][-level]) for e in range(2)]
        feed_sums = [scatter_end(hold(list(v), vectors)) for v in feed_sums]
        feed_near = jnp.concatenate([pick_x(v[:chip_rows], v[chip_rows:]) for v in feed_sums], axis=1)
        feed_far = jnp.concatenate([pick_x(v[chip_rows:], v[:chip_rows]) for v in feed_sums], axis=1)
        feed_far = ctx_swap(feed_far.astype(BF), 1).astype(F32)
        feed_zero, feed_one = pick_x(feed_near, feed_far), pick_x(feed_far, feed_near)
        heads_gain = jnp.sum(gain_parts[:, 0], axis=0)
        chip_gains = jnp.transpose(vectors.reshape(2, n, chip_rows), (1, 0, 2)).reshape(n, 2 * chip_rows)
        small = jnp.concatenate([chip_gains, jnp.broadcast_to(heads_gain[None], (n, LANES))], axis=1)
        small = jnp.pad(small, ((0, 0), (0, 2 * LANES - small.shape[1]))).reshape(n, 1, 2 * LANES)
        small = lax.all_to_all(jnp.broadcast_to(small, (n, 8, 2 * LANES)), "ctx", 0, 0, tiled=True)
        small = jnp.sum(small[:, 0], axis=0)
        small = small + core_swap(small)
        gains = small[: 2 * chip_rows].reshape(2, chip_rows)
        gains = pick(gains[:, :owned], gains[:, owned:])
        head_gains = small[2 * chip_rows : 2 * chip_rows + LANES]

        def theirs(parts):
            return jnp.concatenate([pick(p[owned:], p[:owned]) for p in parts], axis=1)

        grad_gate, grad_up, grad_down = deliver(
            core_arr, feed_zero, feed_one, core_swap(theirs([feed_zero, feed_one]))
        )
        grad_wout, grad_query, grad_key, grad_value = deliver_heads(
            core_arr, part_qkv, part_out, core_swap(theirs([part_qkv, part_out]))
        )
        return (
            layer_out,
            grad_input,
            grad_query,
            grad_key,
            grad_value,
            grad_wout,
            grad_gate,
            grad_up,
            grad_down,
            gains[0],
            gains[1],
            head_gains[:HEAD],
            head_gains[HEAD:],
        )

    return shards


def solution(mesh):
    seq = P("wt", "ctx", None)
    weight = P(("ctx", "wt"), None)
    vector = P(("ctx", "wt"))
    return jax.shard_map(
        make_shards(mesh.shape["ctx"]),
        mesh=mesh,
        in_specs=(seq, P("ctx", None), P("wt", "ctx")) + (weight,) * 7 + (vector, vector, P(), P(), seq),
        out_specs=(seq, seq) + (weight,) * 7 + (vector, vector, P(), P()),
        check_vma=False,
    )
```

```python
import functools

import jax
import jax.numpy as jnp
import numpy as np
from jax import lax
from jax.experimental import pallas as pl
from jax.experimental.pallas import tpu as pltpu
from jax.sharding import PartitionSpec as P

HEADS = 16
KV_HEADS = 8
HEAD = 64
LANES = 2 * HEAD
BLOCK = 128
EPS = 1e-05
SCALE = HEAD**-0.5
BF = jnp.bfloat16
F32 = jnp.float32
I32 = jnp.int32
QT = 512
KT = 512
VMEM_BYTES = 56 * 1024 * 1024

NN = (((1,), (0,)), ((), ()))
NT = (((1,), (1,)), ((), ()))
TN = (((0,), (0,)), ((), ()))


def dot(a, b, dims=NN):
    return lax.dot_general(a, b, dims, preferred_element_type=F32)


def params(**kw):
    return pltpu.CompilerParams(vmem_limit_bytes=VMEM_BYTES, **kw)


def in_vmem():
    return pl.BlockSpec(memory_space=pltpu.VMEM)


def in_smem():
    return pl.BlockSpec(memory_space=pltpu.SMEM)


def low_lanes(shape):
    return lax.broadcasted_iota(I32, shape, 1) < HEAD


def half_sums(value, low):
    shape = (LANES, LANES)
    same = lax.broadcasted_iota(I32, shape, 0) // HEAD == lax.broadcasted_iota(I32, shape, 1) // HEAD
    ones = jnp.where(same, 1.0, 0.0).astype(BF)
    high = value.astype(BF)
    rest = (value - high.astype(F32)).astype(BF)
    return dot(high, ones) + dot(rest, ones)


def half_turn(value):
    lane = lax.broadcasted_iota(I32, value.shape, 1)
    first = (lane % HEAD) < HEAD // 2
    return jnp.where(
        first,
        pltpu.roll(value, LANES - HEAD // 2, 1),
        pltpu.roll(value, HEAD // 2, 1),
    )


def project_kernel(n_parts, swaps, core_ref, x_ref, norm_gain_ref, gain_ref, cos_ref, sin_ref, *refs):
    weights, (n_ref, raw_ref, out_ref) = refs[: 2 * n_parts], refs[2 * n_parts :]
    rows = cos_ref.shape[0]
    is_value = core_ref[0] == 1
    x = x_ref[...].astype(F32)
    inverse = lax.rsqrt(jnp.mean(x * x, axis=-1, keepdims=True) + EPS)
    n_ref[...] = (x * inverse * norm_gain_ref[...]).astype(BF)
    groups = KV_HEADS // 2
    for half in range(2):
        total, at = None, 0
        for part in weights[half * n_parts : (half + 1) * n_parts]:
            length = part.shape[0]
            pieces = [n_ref[:, e : e + swaps[2]] for e in swaps[half][at // swaps[2] : (at + length) // swaps[2]]]
            left = pieces[0] if len(pieces) == 1 else jnp.concatenate(pieces, axis=1)
            term = dot(left, part[:, : groups * LANES])
            total = term if total is None else total + term
            at += length
        raw_ref[:, half * groups * LANES : (half + 1) * groups * LANES] = total
    low = low_lanes((rows, LANES))
    turns = jnp.logical_or(low, jnp.logical_not(is_value))
    for g in range(KV_HEADS):
        for s in range(2):
            raw = raw_ref[s * rows : (s + 1) * rows, g * LANES : (g + 1) * LANES]
            inverse = lax.rsqrt(half_sums(raw * raw, low) * (1.0 / HEAD) + EPS)
            normed = raw * inverse * gain_ref[...]
            turned = normed * cos_ref[...] + half_turn(normed) * sin_ref[...]
            out_ref[g, s] = jnp.where(turns, turned, raw).astype(BF)


def project(core, x, norm_gain, gain, cosine, sine, parts, chunk, chunk_orders):
    rows = cosine.shape[0]
    n_parts = len(parts[0])
    swaps = ([c * chunk for c in chunk_orders[0]], [c * chunk for c in chunk_orders[1]], chunk)
    return pl.pallas_call(
        functools.partial(project_kernel, n_parts, swaps),
        in_specs=[in_smem()] + [in_vmem()] * (5 + 2 * n_parts),
        out_specs=[in_vmem()] * 3,
        out_shape=[
            jax.ShapeDtypeStruct(x.shape, BF),
            jax.ShapeDtypeStruct((2 * rows, KV_HEADS * LANES), F32),
            jax.ShapeDtypeStruct((KV_HEADS, 2, rows, LANES), BF),
        ],
        compiler_params=params(),
        cost_estimate=pl.CostEstimate(flops=2 * x.shape[0] * x.shape[1] * KV_HEADS * LANES, bytes_accessed=8 << 20, transcendentals=0),
    )(core, x, norm_gain, gain, cosine, sine, *parts[0], *parts[1])


def unproject_kernel(core_ref, grad_ref, raw_ref, gain_ref, cos_ref, sin_ref, out_ref, gain_out_ref):
    rows = cos_ref.shape[0]
    is_value = core_ref[0] == 1
    for s in range(2):
        raw = raw_ref[s * rows : (s + 1) * rows]
        grad = grad_ref[0, s].astype(F32)
        low = low_lanes(raw.shape)
        inverse = lax.rsqrt(half_sums(raw * raw, low) * (1.0 / HEAD) + EPS)
        back = grad * cos_ref[...] + half_turn(grad * sin_ref[...])
        is_q_or_k = jnp.logical_or(low, jnp.logical_not(is_value))
        gain_rows = jnp.sum(back * raw * inverse, axis=0, keepdims=True)
        scaled = back * gain_ref[...]
        mean = half_sums(scaled * raw, low) * (1.0 / HEAD)
        moved = inverse * scaled - raw * (inverse * inverse * inverse) * mean
        out_ref[s * rows : (s + 1) * rows, :] = jnp.where(is_q_or_k, moved, grad).astype(BF)
        gain_rows = jnp.where(is_q_or_k[:1], gain_rows, 0.0)
        if s == 0:
            total = gain_rows
        else:
            total = total + gain_rows
    gain_out_ref[0] = jnp.broadcast_to(total, (8, LANES))


def unproject(core, grads, raw, gain, cosine, sine):
    rows = cosine.shape[0]
    return pl.pallas_call(
        unproject_kernel,
        grid=(KV_HEADS,),
        in_specs=[
            in_smem(),
            pl.BlockSpec((1, 2, rows, LANES), lambda g: (g, 0, 0, 0)),
            pl.BlockSpec((2 * rows, LANES), lambda g: (0, g)),
            pl.BlockSpec((1, LANES), lambda g: (0, 0)),
            pl.BlockSpec((rows, LANES), lambda g: (0, 0)),
            pl.BlockSpec((rows, LANES), lambda g: (0, 0)),
        ],
        out_specs=[
            pl.BlockSpec((2 * rows, LANES), lambda g: (0, g)),
            pl.BlockSpec((1, 8, LANES), lambda g: (g, 0, 0)),
        ],
        out_shape=[
            jax.ShapeDtypeStruct((2 * rows, KV_HEADS * LANES), BF),
            jax.ShapeDtypeStruct((KV_HEADS, 8, LANES), F32),
        ],
        compiler_params=params(),
        cost_estimate=pl.CostEstimate(flops=1 << 24, bytes_accessed=8 << 20, transcendentals=0),
    )(core, grads, raw, gain, cosine, sine)


def block_rows(ref, slot):
    return ref[pl.ds(pl.multiple_of(slot * BLOCK, BLOCK), BLOCK), :]


def sum_of_parts(value):
    first = value.astype(BF)
    rest = value - first.astype(F32)
    second = rest.astype(BF)
    third = (rest - second.astype(F32)).astype(BF)
    return first, second, third


def allowed_pairs(j, pos_row, start_row):
    key_pos = j * KT + lax.broadcasted_iota(I32, (KT, 1), 0)
    return jnp.logical_and(key_pos <= pos_row, key_pos >= start_row)


def walk_keys(lims_ref, i, step, carry):
    lo, full_lo, full_hi, hi = (lims_ref[e, i] for e in range(4))
    carry = lax.fori_loop(lo, full_lo, functools.partial(step, True), carry)
    carry = lax.fori_loop(full_lo, full_hi, functools.partial(step, False), carry)
    return lax.fori_loop(full_hi, hi, functools.partial(step, True), carry)


def attend_kernel(
    core_ref, kslot_ref, qslot_ref, lims_ref, q_ref, own_ref, other_ref, pos_ref, start_ref,
    out_ref, keep_ref, lse_ref, keys, values_t, placed,
):
    q_tiles = q_ref.shape[0] // QT
    k_tiles = own_ref.shape[0] // KT
    per = KT // BLOCK
    is_first = core_ref[0] == 0
    values_t[HEAD:, :] = jnp.ones((values_t.shape[0] - HEAD, values_t.shape[1]), BF)

    def load(t, carry):
        for b in range(per):
            slot = kslot_ref[t * per + b]
            own = block_rows(own_ref, slot)[:, HEAD:]
            other = block_rows(other_ref, slot)[:, HEAD:]
            at = pl.ds(pl.multiple_of((t * per + b) * BLOCK, BLOCK), BLOCK)
            keys[at, :] = jnp.where(is_first, own, other)
            value = jnp.where(is_first, other, own).astype(F32)
            values_t[:HEAD, at] = value.T.astype(BF)
        return carry

    lax.fori_loop(0, k_tiles, load, 0)

    def tile(i, carry):
        cols = pl.ds(pl.multiple_of(i * QT, QT), QT)
        parts = [block_rows(q_ref, qslot_ref[i * (QT // BLOCK) + b])[:, :HEAD] for b in range(QT // BLOCK)]
        query_t = (jnp.concatenate(parts, axis=0).astype(F32) * SCALE).T.astype(BF)
        pos_row = pos_ref[:, cols]
        start_row = start_ref[:, cols]

        def step(masked, j, acc):
            at = pl.ds(pl.multiple_of(j * KT, KT), KT)
            p = jnp.exp(dot(keys[at, :], query_t))
            if masked:
                p = jnp.where(allowed_pairs(j, pos_row, start_row), p, 0.0)
            return acc + dot(values_t[:, at], p.astype(BF))

        acc = walk_keys(lims_ref, i, step, jnp.zeros((values_t.shape[0], QT), F32))
        total = acc[HEAD : HEAD + 1]
        mixed = acc[:HEAD] / total
        keep_ref[:, cols] = mixed
        lse_ref[:, cols] = jnp.log(total)
        rows = mixed.T
        for b in range(QT // BLOCK):
            slot = qslot_ref[i * (QT // BLOCK) + b]
            placed[pl.ds(pl.multiple_of(slot * BLOCK, BLOCK), BLOCK), :] = rows[b * BLOCK : (b + 1) * BLOCK]
        return carry

    lax.fori_loop(0, q_tiles, tile, 0)

    def pack(c, carry):
        first = placed[pl.ds(pl.multiple_of(c * 2 * BLOCK, BLOCK), BLOCK), :]
        second = placed[pl.ds(pl.multiple_of((c * 2 + 1) * BLOCK, BLOCK), BLOCK), :]
        out_ref[pl.ds(pl.multiple_of(c * BLOCK, BLOCK), BLOCK), :] = jnp.concatenate([first, second], axis=1).astype(BF)
        return carry

    lax.fori_loop(0, q_ref.shape[0] // (2 * BLOCK), pack, 0)


def attend(core, tables, queries, own, other):
    kslot, qslot, lims, pos, start = tables
    n_q, n_k = queries.shape[0], own.shape[0]
    return pl.pallas_call(
        attend_kernel,
        in_specs=[in_smem()] * 4 + [in_vmem()] * 5,
        out_specs=[in_vmem()] * 3,
        out_shape=[
            jax.ShapeDtypeStruct((n_q // 2, LANES), BF),
            jax.ShapeDtypeStruct((HEAD, n_q), F32),
            jax.ShapeDtypeStruct((1, n_q), F32),
        ],
        scratch_shapes=[
            pltpu.VMEM((n_k, HEAD), BF),
            pltpu.VMEM((HEAD + 16, n_k), BF),
            pltpu.VMEM((n_q, HEAD), F32),
        ],
        compiler_params=params(),
        cost_estimate=pl.CostEstimate(flops=8 * n_q * n_k * HEAD, bytes_accessed=8 << 20, transcendentals=n_q * n_k),
    )(core, kslot, qslot, lims, queries, own, other, pos, start)


def attend_back_kernel(
    core_ref, kslot_ref, qslot_ref, lims_ref, q_ref, own_ref, other_ref, pos_ref, start_ref,
    grad_ref, mixed_ref, lse_ref,
    dq_ref, keep_ref, send_ref,
    keys, values, keys_t, grad_keys, grad_values, grad_placed,
):
    q_tiles = q_ref.shape[0] // QT
    k_tiles = own_ref.shape[0] // KT
    per = KT // BLOCK
    is_first = core_ref[0] == 0
    ones = jnp.ones((BLOCK, HEAD), BF)

    def load(t, carry):
        for b in range(per):
            slot = kslot_ref[t * per + b]
            own = block_rows(own_ref, slot)[:, HEAD:]
            other = block_rows(other_ref, slot)[:, HEAD:]
            at = pl.ds(pl.multiple_of((t * per + b) * BLOCK, BLOCK), BLOCK)
            key = jnp.where(is_first, own, other)
            value = jnp.where(is_first, other, own)
            keys[at, :] = jnp.concatenate([key, ones], axis=1)
            values[at, :] = jnp.concatenate([value, ones], axis=1)
            keys_t[:, at] = key.astype(F32).T.astype(BF)
            grad_keys[at, :] = jnp.zeros((BLOCK, HEAD), F32)
            grad_values[at, :] = jnp.zeros((BLOCK, HEAD), F32)
        return carry

    lax.fori_loop(0, k_tiles, load, 0)

    def unpack(c, carry):
        pair = grad_ref[pl.ds(pl.multiple_of(c * BLOCK, BLOCK), BLOCK), :]
        grad_placed[pl.ds(pl.multiple_of(c * 2 * BLOCK, BLOCK), BLOCK), :] = pair[:, :HEAD]
        grad_placed[pl.ds(pl.multiple_of((c * 2 + 1) * BLOCK, BLOCK), BLOCK), :] = pair[:, HEAD:]
        return carry

    lax.fori_loop(0, q_ref.shape[0] // (2 * BLOCK), unpack, 0)

    def tile(i, carry):
        cols = pl.ds(pl.multiple_of(i * QT, QT), QT)
        slots = [qslot_ref[i * (QT // BLOCK) + b] for b in range(QT // BLOCK)]
        query_f = jnp.concatenate([block_rows(q_ref, s)[:, :HEAD] for s in slots], axis=0).astype(F32) * SCALE
        grad = jnp.concatenate([block_rows(grad_placed, s) for s in slots], axis=0)
        query = query_f.astype(BF)
        grad_t = grad.astype(F32).T
        delta = jnp.sum(grad_t * mixed_ref[:, cols], axis=0, keepdims=True)
        pad = jnp.zeros((HEAD - 3, QT), F32)
        query_t = jnp.concatenate(
            [query_f.T] + [e.astype(F32) for e in sum_of_parts(-lse_ref[:, cols])] + [pad], axis=0
        ).astype(BF)
        grad_t = jnp.concatenate([grad_t] + [e.astype(F32) for e in sum_of_parts(-delta)] + [pad], axis=0).astype(BF)
        pos_row = pos_ref[:, cols]
        start_row = start_ref[:, cols]

        def step(masked, j, acc):
            at = pl.ds(pl.multiple_of(j * KT, KT), KT)
            p = jnp.exp(dot(keys[at, :], query_t))
            if masked:
                p = jnp.where(allowed_pairs(j, pos_row, start_row), p, 0.0)
            grad_s = (p * dot(values[at, :], grad_t)).astype(BF)
            grad_values[at, :] += dot(p.astype(BF), grad)
            grad_keys[at, :] += dot(grad_s, query)
            return acc + dot(keys_t[:, at], grad_s)

        acc = walk_keys(lims_ref, i, step, jnp.zeros((HEAD, QT), F32))
        rows = (acc * SCALE).T
        rows = jnp.concatenate([rows, jnp.zeros((QT, HEAD), F32)], axis=1)
        for b in range(QT // BLOCK):
            dq_ref[pl.ds(pl.multiple_of(slots[b] * BLOCK, BLOCK), BLOCK), :] = rows[b * BLOCK : (b + 1) * BLOCK]
        return carry

    lax.fori_loop(0, q_tiles, tile, 0)

    def place(t, carry):
        zeros = jnp.zeros((BLOCK, HEAD), F32)
        for b in range(per):
            slot = kslot_ref[t * per + b]
            at = pl.ds(pl.multiple_of((t * per + b) * BLOCK, BLOCK), BLOCK)
            to = pl.ds(pl.multiple_of(slot * BLOCK, BLOCK), BLOCK)
            key, value = grad_keys[at, :], grad_values[at, :]
            mine = jnp.where(is_first, key, value)
            theirs = jnp.where(is_first, value, key)
            keep_ref[to, :] = jnp.concatenate([zeros, mine], axis=1)
            send_ref[to, :] = jnp.concatenate([zeros, theirs], axis=1).astype(BF)
        return carry

    lax.fori_loop(0, k_tiles, place, 0)


def attend_back(core, tables, queries, own, other, grads, mixed, lse):
    kslot, qslot, lims, pos, start = tables
    n_q, n_k = queries.shape[0], own.shape[0]
    return pl.pallas_call(
        attend_back_kernel,
        in_specs=[in_smem()] * 4 + [in_vmem()] * 8,
        out_specs=[in_vmem()] * 3,
        out_shape=[
            jax.ShapeDtypeStruct((n_q, LANES), F32),
            jax.ShapeDtypeStruct((n_k, LANES), F32),
            jax.ShapeDtypeStruct((n_k, LANES), BF),
        ],
        scratch_shapes=[
            pltpu.VMEM((n_k, LANES), BF),
            pltpu.VMEM((n_k, LANES), BF),
            pltpu.VMEM((HEAD, n_k), BF),
            pltpu.VMEM((n_k, HEAD), F32),
            pltpu.VMEM((n_k, HEAD), F32),
            pltpu.VMEM((n_q, HEAD), BF),
        ],
        compiler_params=params(),
        cost_estimate=pl.CostEstimate(flops=16 * n_q * n_k * HEAD, bytes_accessed=8 << 20, transcendentals=n_q * n_k),
    )(core, kslot, qslot, lims, queries, own, other, pos, start, grads, mixed, lse)


def columns_of(value, chunk, order, part, parts):
    count = len(order) // parts
    pieces = [value[:, e * chunk : (e + 1) * chunk] for e in order[part * count : (part + 1) * count]]
    return jnp.concatenate(pieces, axis=1)


def in_order(values, chunk, order):
    joined = jnp.concatenate(values, axis=1)
    places = sorted(range(len(order)), key=lambda e: order[e])
    return jnp.concatenate([joined[:, e * chunk : (e + 1) * chunk] for e in places], axis=1)


def feed_kernel(n_parts, chunk, orders, n_ref, c_ref, *refs):
    first, second = refs[:n_parts], refs[n_parts : 2 * n_parts]
    mid_ref, gate_ref, up_ref, out_ref, back_ref, nt_ref = refs[2 * n_parts :]
    quarter = mid_ref.shape[1]
    split = first[0].shape[1] - quarter
    normed, upstream = n_ref[...], c_ref[...]

    def over_parts(value, order, parts, lo, hi):
        total = None
        for p, part in enumerate(parts):
            term = dot(columns_of(value, chunk, order, p, n_parts), part[:, lo:hi])
            total = term if total is None else total + term
        return total

    gate = over_parts(normed, orders[0], first, 0, quarter)
    up = over_parts(normed, orders[1], second, 0, quarter)
    down = jnp.concatenate(
        [
            over_parts(upstream, orders[0], first, quarter, quarter + split),
            over_parts(upstream, orders[1], second, quarter, 2 * quarter - split),
        ],
        axis=1,
    )
    sig = 1.0 / (1.0 + jnp.exp(-gate))
    silu = gate * sig
    mid_ref[...] = (silu * up).astype(BF)
    gate_ref[...] = (down * up * (sig * (1.0 + gate * (1.0 - sig)))).astype(BF)
    up_ref[...] = (down * silu).astype(BF)
    out_ref[...] = in_order(
        [dot(mid_ref[:, :split], part[:, quarter:], NT) for part in first], chunk, orders[0]
    ) + in_order([dot(mid_ref[:, split:], part[:, quarter:], NT) for part in second], chunk, orders[1])
    back = in_order([dot(gate_ref[...], part[:, :quarter], NT) for part in first], chunk, orders[0]) + in_order(
        [dot(up_ref[...], part[:, :quarter], NT) for part in second], chunk, orders[1]
    )
    back_ref[...] = back.astype(BF)
    nt_ref[...] = normed.T


def feed(n, c, parts, chunk, orders, quarter):
    rows, width = n.shape
    step = rows // 2
    tall = lambda cols: pl.BlockSpec((step, cols), lambda i: (i, 0))
    whole = [p for piece in parts for p in piece]
    return pl.pallas_call(
        functools.partial(feed_kernel, len(parts[0]), chunk, orders),
        grid=(2,),
        in_specs=[tall(width)] * 2 + [pl.BlockSpec(p.shape, lambda i: (0, 0)) for p in whole],
        out_specs=[tall(quarter)] * 3 + [tall(width)] * 2 + [pl.BlockSpec((width, step), lambda i: (0, i))],
        out_shape=[jax.ShapeDtypeStruct((rows, quarter), BF)] * 3
        + [jax.ShapeDtypeStruct(e, t) for e, t in (((rows, width), F32), ((rows, width), BF), ((width, rows), BF))],
        compiler_params=params(),
        cost_estimate=pl.CostEstimate(flops=12 * rows * width * quarter, bytes_accessed=16 << 20, transcendentals=0),
    )(n, c, *whole)


def turn_kernel(a_ref, b_ref, a_out_ref, b_out_ref):
    a_out_ref[...] = a_ref[...].T
    b_out_ref[...] = b_ref[...].T


def turn(a, b):
    return pl.pallas_call(
        turn_kernel,
        in_specs=[in_vmem()] * 2,
        out_specs=[in_vmem()] * 2,
        out_shape=[jax.ShapeDtypeStruct(v.shape[::-1], v.dtype) for v in (a, b)],
        compiler_params=params(),
        cost_estimate=pl.CostEstimate(flops=1 << 20, bytes_accessed=4 << 20, transcendentals=0),
    )(a, b)


def out_grad_kernel(core_ref, attn_ref, grad_ref, select_ref, unperm_ref, out_ref):
    half = unperm_ref.shape[1] // 2
    rel = dot(attn_ref[...], select_ref[...]).astype(BF).T
    cols = jnp.where(core_ref[0] == 0, unperm_ref[:, :half], unperm_ref[:, half:])
    out_ref[...] = dot(rel, dot(grad_ref[...], cols).astype(BF)).astype(BF)


def out_grad(core, attn, grad, select, unperm):
    width = select.shape[0]
    return pl.pallas_call(
        out_grad_kernel,
        in_specs=[in_smem()] + [in_vmem()] * 4,
        out_specs=in_vmem(),
        out_shape=jax.ShapeDtypeStruct((width, width // 2), BF),
        compiler_params=params(),
        cost_estimate=pl.CostEstimate(flops=4 << 30, bytes_accessed=8 << 20, transcendentals=0),
    )(core, attn, grad, select, unperm)


def feed_back_kernel(chunk, orders, *refs):
    (nt_a, ct_a, nt_b, ct_b, mid_a, gate_a, up_a, mid_b, gate_b, up_b), outs = refs[:10], refs[10:]
    quarter = mid_a.shape[1]
    split = outs[0].shape[1] - quarter
    height = outs[0].shape[0]
    per = height // chunk

    def rows_of(ref, order, place):
        return jnp.concatenate([ref[e * chunk : (e + 1) * chunk, :] for e in order[place * per : (place + 1) * per]], axis=0)

    def total(order, place, left_a, right_a, left_b, right_b):
        return (dot(rows_of(left_a, order, place), right_a) + dot(rows_of(left_b, order, place), right_b)).astype(BF)

    for i in range(2):

        @pl.when(pl.program_id(0) == i)
        def _():
            for side in range(2):
                place = side * 2 + i
                one, two = outs[side], outs[2 + side]
                one[:, :quarter] = total(orders[0], place, nt_a, gate_a[...], nt_b, gate_b[...])
                one[:, quarter:] = total(orders[0], place, ct_a, mid_a[:, :split], ct_b, mid_b[:, :split])
                two[:, :quarter] = total(orders[1], place, nt_a, up_a[...], nt_b, up_b[...])
                two[:, quarter:] = total(orders[1], place, ct_a, mid_a[:, split:], ct_b, mid_b[:, split:])


def feed_back(transposed, acts, chunk, orders, cols):
    width, rows = transposed[0].shape
    quarter = acts[0].shape[1]
    whole = lambda v: pl.BlockSpec(v.shape, lambda i: (0, 0))
    out = lambda c: pl.BlockSpec((width // 4, c), lambda i: (i, 0))
    return pl.pallas_call(
        functools.partial(feed_back_kernel, chunk, orders),
        grid=(2,),
        in_specs=[whole(v) for v in transposed] + [whole(v) for v in acts],
        out_specs=[out(cols[0])] * 2 + [out(cols[1])] * 2,
        out_shape=[jax.ShapeDtypeStruct((width // 2, c), BF) for c in (cols[0], cols[0], cols[1], cols[1])],
        compiler_params=params(),
        cost_estimate=pl.CostEstimate(flops=12 * rows * width * quarter, bytes_accessed=16 << 20, transcendentals=0),
    )(*transposed, *acts)


def down_split(quarter):
    return (quarter // 2 + LANES // 2) // LANES * LANES


def prepare_kernel(
    core_ref, table_ref, q_ref, k_ref, v_ref, o_ref, g_ref, u_ref, d_ref, ga_ref, gm_ref, flags_ref,
    mine_q_ref, theirs_q_ref, mine_f_ref, theirs_f_ref,
):
    first = core_ref[0] == 0
    owned, width = q_ref.shape

    def put(mine_ref, theirs_ref, at, zero, one):
        size = zero.shape[1]
        mine_ref[:, at : at + size] = jnp.where(first, zero, one).astype(BF)
        theirs_ref[:, at : at + size] = jnp.where(first, one, zero).astype(BF)

    for g in range(KV_HEADS):
        at = g * LANES
        kv = slice(g * HEAD, (g + 1) * HEAD)
        zero = jnp.concatenate([q_ref[:, at : at + HEAD], k_ref[:, kv]], axis=1)
        one = jnp.concatenate([q_ref[:, at + HEAD : at + LANES], v_ref[:, kv]], axis=1)
        put(mine_q_ref, theirs_q_ref, at, zero, one)
    shape = (owned, owned)
    diagonal = lax.broadcasted_iota(I32, shape, 0) == lax.broadcasted_iota(I32, shape, 1)
    gain_a = jnp.sum(jnp.where(diagonal, ga_ref[...], 0.0), axis=1, keepdims=True)
    gain_m = jnp.sum(jnp.where(diagonal, gm_ref[...], 0.0), axis=1, keepdims=True)
    count = flags_ref.shape[1]
    cols = count // owned
    row = lax.broadcasted_iota(I32, (owned, count), 0)
    col = lax.broadcasted_iota(I32, (owned, count), 1)
    spread = jnp.where(col // cols == row, flags_ref[...].astype(F32), 0.0).astype(BF)
    row = lax.broadcasted_iota(I32, (count, LANES), 0)
    col = lax.broadcasted_iota(I32, (count, LANES), 1)
    extra = dot(spread, jnp.where(row % cols == col - 3, 1.0, 0.0).astype(BF))
    row = lax.broadcasted_iota(I32, (owned, LANES), 0)
    col = lax.broadcasted_iota(I32, (owned, LANES), 1)
    blocks = jnp.where(row == 0, table_ref[0, 0], jnp.where(row == 1, table_ref[0, 1], 0)).astype(F32)
    extra = jnp.where(col == 0, gain_a, jnp.where(col == 1, gain_m, jnp.where(col == 2, blocks, extra)))
    put(mine_q_ref, theirs_q_ref, width, extra, extra)
    half = g_ref.shape[1] // 2
    quarter = half // 2
    split = down_split(quarter)
    for x in range(2):
        at = 2 * x * quarter * 3 // 2
        for ref, lo, hi in ((g_ref, 0, quarter), (d_ref, 0, split), (u_ref, 0, quarter), (d_ref, split, quarter)):
            zero = ref[:, x * quarter + lo : x * quarter + hi]
            one = ref[:, half + x * quarter + lo : half + x * quarter + hi]
            put(mine_f_ref, theirs_f_ref, at, zero, one)
            at += hi - lo
    put(mine_q_ref, theirs_q_ref, width + LANES, o_ref[:, : width // 2], o_ref[:, width // 2 :])


def prepare(core, table, *arrays):
    owned, width = arrays[0].shape
    cols = 3 * arrays[4].shape[1] // 2
    return pl.pallas_call(
        prepare_kernel,
        in_specs=[in_smem()] * 2 + [in_vmem()] * len(arrays),
        out_specs=[in_vmem()] * 4,
        out_shape=[jax.ShapeDtypeStruct((owned, width + LANES + width // 2), BF)] * 2 + [jax.ShapeDtypeStruct((owned, cols), BF)] * 2,
        compiler_params=params(),
    )(core, table, *arrays)


def deliver_kernel(core_ref, zero_ref, one_ref, other_ref, gate_ref, up_ref, down_ref):
    first = core_ref[0] == 0
    owned, half = gate_ref.shape[0], gate_ref.shape[1] // 2
    quarter = half // 2
    split = down_split(quarter)
    for x, ref in enumerate((zero_ref, one_ref)):
        at = 0
        for out, lo, hi in ((gate_ref, 0, quarter), (down_ref, 0, split), (up_ref, 0, quarter), (down_ref, split, quarter)):
            size = hi - lo
            kept = jnp.where(first, ref[:owned, at : at + size], ref[owned:, at : at + size])
            arrived = other_ref[:, x * 3 * quarter + at : x * 3 * quarter + at + size]
            out[:, x * quarter + lo : x * quarter + hi] = jnp.where(first, kept, arrived)
            out[:, half + x * quarter + lo : half + x * quarter + hi] = jnp.where(first, arrived, kept)
            at += size


def deliver(core, zero, one, other):
    owned, cols = other.shape
    return pl.pallas_call(
        deliver_kernel,
        in_specs=[in_smem()] + [in_vmem()] * 3,
        out_specs=[in_vmem()] * 3,
        out_shape=[jax.ShapeDtypeStruct((owned, 2 * cols // 3), F32)] * 3,
        compiler_params=params(),
    )(core, zero, one, other)


def deliver_heads_kernel(core_ref, qkv_ref, out_ref, other_ref, wo_ref, q_ref, k_ref, v_ref):
    first = core_ref[0] == 0
    owned, width = q_ref.shape
    half = width // 2

    def sides(ref, at, size, shift):
        kept = jnp.where(first, ref[:owned, at : at + size], ref[owned:, at : at + size])
        arrived = other_ref[:, shift + at : shift + at + size]
        return jnp.where(first, kept, arrived), jnp.where(first, arrived, kept)

    wo_ref[:, :half], wo_ref[:, half:] = sides(out_ref, 0, half, width)
    for g in range(0, KV_HEADS, 2):
        zero, one = sides(qkv_ref, g * LANES, LANES, 0)
        zero_next, one_next = sides(qkv_ref, (g + 1) * LANES, LANES, 0)
        q_ref[:, g * LANES : (g + 1) * LANES] = jnp.concatenate([zero[:, :HEAD], one[:, :HEAD]], axis=1)
        q_ref[:, (g + 1) * LANES : (g + 2) * LANES] = jnp.concatenate([zero_next[:, :HEAD], one_next[:, :HEAD]], axis=1)
        k_ref[:, g * HEAD : (g + 2) * HEAD] = jnp.concatenate([zero[:, HEAD:], zero_next[:, HEAD:]], axis=1)
        v_ref[:, g * HEAD : (g + 2) * HEAD] = jnp.concatenate([one[:, HEAD:], one_next[:, HEAD:]], axis=1)


def deliver_heads(core, qkv, out, other):
    owned, width = other.shape[0], qkv.shape[1]
    shapes = [(owned, width), (owned, width), (owned, width // 2), (owned, width // 2)]
    return pl.pallas_call(
        deliver_heads_kernel,
        in_specs=[in_smem()] + [in_vmem()] * 3,
        out_specs=[in_vmem()] * 4,
        out_shape=[jax.ShapeDtypeStruct(e, F32) for e in shapes],
        compiler_params=params(),
    )(core, qkv, out, other)


def leave_kernel(core_ref, own_ref, other_ref, x_ref, wo_ref, gain_ref, res_ref, n_ref, attn_ref, half_ref):
    half = KV_HEADS * HEAD
    for which, ref in enumerate((own_ref, other_ref)):
        for g in range(0, KV_HEADS, 2):
            for s in range(2):
                for j in range(2):
                    lanes = slice(j * HEAD, (j + 1) * HEAD)
                    a = ref[(g * 2 + s) * BLOCK : (g * 2 + s + 1) * BLOCK, lanes]
                    b = ref[((g + 1) * 2 + s) * BLOCK : ((g + 1) * 2 + s + 1) * BLOCK, lanes]
                    row, col = (s * 2 + j) * BLOCK, which * half + g * HEAD
                    attn_ref[row : row + BLOCK, col : col + LANES] = jnp.concatenate([a, b], axis=1)
    value = x_ref[...].astype(F32) + dot(attn_ref[...], wo_ref[...])
    res_ref[...] = value
    inverse = lax.rsqrt(jnp.mean(value * value, axis=-1, keepdims=True) + EPS)
    normed = (value * inverse * gain_ref[...]).astype(BF)
    n_ref[...] = normed
    rows = half_ref.shape[0]
    half_ref[...] = jnp.where(core_ref[0] == 0, normed[:rows], normed[rows:])


def leave(core, own, other, x, wo, gain):
    rows, width = x.shape
    return pl.pallas_call(
        leave_kernel,
        in_specs=[in_smem()] + [in_vmem()] * 5,
        out_specs=[in_vmem()] * 4,
        out_shape=[
            jax.ShapeDtypeStruct((rows, width), F32),
            jax.ShapeDtypeStruct((rows, width), BF),
            jax.ShapeDtypeStruct((rows, width), BF),
            jax.ShapeDtypeStruct((rows // 2, width), BF),
        ],
        compiler_params=params(),
        cost_estimate=pl.CostEstimate(flops=2 * rows * width * width, bytes_accessed=10 << 20, transcendentals=0),
    )(core, own, other, x, wo, gain)


def enter_kernel(
    core_ref, back_ref, other_ref, far_ref, far_other_ref, res_ref, c_ref, gain_ref, wo_ref,
    grad_ref, grad_b_ref, gain_out_ref, out_ref,
):
    value = res_ref[...]
    inverse = lax.rsqrt(jnp.mean(value * value, axis=-1, keepdims=True) + EPS)
    first = core_ref[0] == 0
    far, far_other = far_ref[...].astype(F32), far_other_ref[...].astype(F32)
    far_all = jnp.concatenate([jnp.where(first, far, far_other), jnp.where(first, far_other, far)], axis=0)
    grad = back_ref[...].astype(F32) + other_ref[...].astype(F32) + far_all
    gain_out_ref[...] = jnp.sum(grad * value * inverse, axis=0, keepdims=True)
    scaled = grad * gain_ref[...]
    mean = jnp.mean(scaled * value, axis=-1, keepdims=True)
    total = c_ref[...].astype(F32) + (inverse * scaled - value * (inverse * inverse * inverse) * mean)
    grad_ref[...] = total
    grad_b_ref[...] = total.astype(BF)
    heads = dot(grad_b_ref[...], wo_ref[: KV_HEADS * HEAD, :], NT).astype(BF)
    for g in range(KV_HEADS):
        for s in range(2):
            row = s * 2 * BLOCK
            lanes = slice(g * HEAD, (g + 1) * HEAD)
            out_ref[(g * 2 + s) * BLOCK : (g * 2 + s + 1) * BLOCK, :] = jnp.concatenate(
                [heads[row : row + BLOCK, lanes], heads[row + BLOCK : row + 2 * BLOCK, lanes]], axis=1
            )


def enter(core, back, other, far, far_other, residual, c, gain, wo):
    rows, width = residual.shape
    return pl.pallas_call(
        enter_kernel,
        in_specs=[in_smem()] + [in_vmem()] * 8,
        out_specs=[in_vmem()] * 4,
        out_shape=[
            jax.ShapeDtypeStruct((rows, width), F32),
            jax.ShapeDtypeStruct((rows, width), BF),
            jax.ShapeDtypeStruct((1, width), F32),
            jax.ShapeDtypeStruct((2 * KV_HEADS * BLOCK, LANES), BF),
        ],
        compiler_params=params(),
        cost_estimate=pl.CostEstimate(flops=rows * width * width, bytes_accessed=10 << 20, transcendentals=0),
    )(core, back, other, far, far_other, residual, c, gain, wo)


def rms(value, gain):
    inverse = lax.rsqrt(jnp.mean(value * value, axis=-1, keepdims=True) + EPS)
    return value * inverse * gain, inverse


def rms_back(value, inverse, gain, grad):
    scaled = grad * gain
    mean = jnp.mean(scaled * value, axis=-1, keepdims=True)
    moved = inverse * scaled - value * (inverse * inverse * inverse) * mean
    return moved, jnp.sum(grad * value * inverse, axis=0)


def rope_tables(positions):
    inv_freq = jnp.power(F32(1000000.0), -(2.0 * jnp.arange(HEAD // 2, dtype=F32)) / HEAD)
    angles = positions.astype(F32)[:, None] * inv_freq[None, :]
    cosine, sine = jnp.cos(angles), jnp.sin(angles)
    return (
        jnp.concatenate([cosine] * 4, axis=1),
        jnp.concatenate([-sine, sine, -sine, sine], axis=1),
    )


class Dim:
    def __init__(self, stride, size):
        self.stride, self.size = stride, size


def make_shards(n):
    if n == 16:
        dims = {"x": Dim(1, 2), "y": Dim(2, 2), "p": Dim(4, 2), "q": Dim(8, 2)}
        order_a, order_b, order_m, order_w = "qpxy", "qpyx", "xqpy", "xqyp"
    else:
        names = "abcdefghijkl"[: n.bit_length() - 1]
        dims = {name: Dim(1 << b, 2) for b, name in enumerate(names)}
        order_a = order_b = order_m = order_w = names
    groups = n // 16
    a2a_groups = None if groups == 1 else [[t * 16 + d for d in range(16)] for t in range(groups)]
    kv_groups = None if groups == 1 else [[t * 16 + d for t in range(groups)] for d in range(16)]

    def digits(order):
        places = []
        for r in range(n):
            place = {}
            for name in order:
                place[name] = r % dims[name].size
                r //= dims[name].size
            places.append(place)
        return places

    def place_in(order, base=order_a):
        found = {tuple(sorted(p.items())): r for r, p in enumerate(digits(order))}
        return [found[tuple(sorted(p.items()))] for p in digits(base)]

    def chips(me, order, absolute=None):
        out = []
        for place in digits(order):
            chip = me
            for name, digit in place.items():
                d = dims[name]
                at = (me // d.stride) % d.size
                to = digit if name == absolute else jnp.bitwise_xor(at, digit)
                chip = chip + (to - at) * d.stride
            out.append(chip)
        return jnp.stack(out).astype(I32)

    def ctx_send(value, pairs):
        return lax.ppermute(value, "ctx", pairs)

    def ctx_swap(value, stride):
        return ctx_send(value, [(i, i ^ stride) for i in range(n)])

    def core_swap(value):
        return lax.ppermute(value, "wt", [(0, 1), (1, 0)])

    def gather_dim(value, name):
        return [value, ctx_swap(value, dims[name].stride)]

    def join(parts):
        return parts[0] if len(parts) == 1 else jnp.concatenate(parts, axis=0)

    def gather_rows(parts, names):
        for name in names:
            parts = gather_dim(join(parts), name)
        return parts

    def hold(parts, *others):
        return parts[:-1] + [after(parts[-1], *others)]

    def scatter_begin(keep, send, name):
        return keep, ctx_swap(send.astype(BF), dims[name].stride)

    def scatter_next(state, name):
        keep, arrived = state
        half = keep.shape[0] // 2
        send = (keep[half:].astype(F32) + arrived[half:].astype(F32)).astype(BF)
        keep = (keep[:half].astype(F32) + arrived[:half].astype(F32)).astype(BF)
        return keep, ctx_swap(send, dims[name].stride)

    def scatter_end(state):
        keep, arrived = state
        return keep.astype(F32) + arrived.astype(F32)

    def scatter_rows(keep, send, names):
        state = scatter_begin(keep, send, names[-1])
        for name in reversed(names[:-1]):
            state = scatter_next(state, name)
        return scatter_end(state)

    def scatter_whole(value, names):
        half = value.shape[0] // 2
        return scatter_rows(value[:half], value[half:], names)

    def runs(places):
        out = []
        for p in places:
            if out and out[-1][1] == p:
                out[-1][1] = p + 1
            else:
                out.append([p, p + 1])
        return out

    def assemble(parts, order):
        total = sum(p.shape[0] for p in parts)
        unit, each = total // n, parts[0].shape[0] // (total // n)
        out = []
        for lo, hi in runs(place_in(order)):
            while lo < hi:
                part, at = lo // each, lo % each
                stop = min(hi, (part + 1) * each)
                out.append(parts[part][at * unit : (at + stop - lo) * unit])
                lo = stop
        return join(out)

    def columns_in(value, order):
        unit = value.shape[1] // n
        inverse = np.argsort(place_in(order)).tolist()
        pieces = [value[:, lo * unit : hi * unit] for lo, hi in runs(inverse)]
        return pieces[0] if len(pieces) == 1 else jnp.concatenate(pieces, axis=1)

    def after(value, *others):
        return lax.optimization_barrier((value,) + others)[0]

    def swap_heads(value):
        return lax.all_to_all(value, "ctx", 0, 0, axis_index_groups=a2a_groups, tiled=True)

    def shards(
        tokens, block_table, doc_flags, w_query, key_weight, value_weight, w_out, w_gate, w_up, w_down,
        gain_attn, gain_mlp, gain_q, key_norm_gain, cotangent,
    ):
        width = tokens.shape[-1]
        rows = tokens.shape[1]
        owned = w_query.shape[0]
        chip_rows = 2 * owned
        me = lax.axis_index("ctx")
        core = lax.axis_index("wt")
        first = core == 0
        core_arr = core.astype(I32).reshape(1)
        slots_n = 2 * n

        def by_core(a, b, axis=0):
            return jnp.where(first, jnp.concatenate([a, b], axis=axis), jnp.concatenate([b, a], axis=axis))

        def pick(a, b):
            return jnp.where(first, a, b)

        chip_of = chips(me, order_a)

        def features(order, me, absolute=None):
            chip = chips(me, order, absolute)
            return (chip[:, None] * chip_rows + jnp.arange(chip_rows, dtype=I32)[None, :]).reshape(-1)

        def spread(order, me, absolute=None):
            return (jnp.arange(width, dtype=I32)[:, None] == features(order, me, absolute)[None, :]).astype(BF)

        def collect(order, me, absolute=None):
            return (features(order, me, absolute)[:, None] == jnp.arange(width, dtype=I32)[None, :]).astype(BF)

        left = me % 2 == 0

        def pick_x(a, b):
            return jnp.where(left, a, b)

        def by_x(a, b, axis=0):
            return pick_x(jnp.concatenate([a, b], axis=axis), jnp.concatenate([b, a], axis=axis))

        flag_cols = rows // owned
        own_blocks = block_table[0]
        mine_q, theirs_q, mine_f, theirs_f = prepare(
            core_arr, block_table, w_query, key_weight, value_weight, w_out, w_gate, w_up, w_down,
            gain_attn[None, :], gain_mlp[None, :], doc_flags,
        )
        first_piece = by_core(mine_q, core_swap(theirs_q))
        acts = jnp.stack([after(tokens[0], mine_q), after(cotangent[0], mine_q)])
        acts_other = core_swap(acts)
        other_f = core_swap(theirs_f)
        me_later = after(me.astype(I32), first_piece)
        canon = features(order_a, me_later)
        perm, perm_m, unperm, unperm_m = lax.optimization_barrier(
            (spread(order_a, me_later), spread(order_m, me_later, order_m[0]), collect(order_a, me_later), collect(order_m, me_later, order_m[0]))
        )
        x_two = dot(by_core(acts[0], acts_other[0]), perm).astype(BF)
        x_m = dot(by_core(acts[0], acts_other[0]), perm_m).astype(BF)
        c_m = dot(by_core(acts[1], acts_other[1]), perm_m).astype(BF)
        head_cols = width // 2
        quarter = w_gate.shape[1] // 4
        feed_half = by_core(mine_f, other_f)
        feed_x = feed_half[:, : 3 * quarter], feed_half[:, 3 * quarter :]
        feed_near = pick_x(*feed_x)
        feed_far = ctx_swap(pick_x(feed_x[1], feed_x[0]), 1)
        out_cols = width // 4
        out_at = width + LANES

        def cut(value):
            first_cols = [value[:, :head_cols], value[:, width:out_at], value[:, out_at : out_at + out_cols]]
            second_cols = [value[:, head_cols:width], value[:, out_at + out_cols :]]
            return [jnp.concatenate(first_cols, axis=1)], [jnp.concatenate(second_cols, axis=1)]

        if n == 16:
            halfway = hold(gather_rows([first_piece], "q"), feed_far)
            feed_far = after(feed_far, halfway[-1])
            shared = cut(join(gather_rows(halfway, "p")))
            qkv_parts = [gather_rows(shared[0], "x"), gather_rows(shared[1], "y")]
            first_swap = qkv_parts[0][-1]
            qkv_parts = [gather_rows(hold(qkv_parts[0], x_two), "y"), gather_rows(qkv_parts[1], "x")]
        else:
            shared = cut(first_piece)
            qkv_parts = [gather_rows(shared[0], order_a), gather_rows(shared[1], order_b)]
            first_swap = first_piece
        chunk = LANES
        per = chunk // chip_rows
        chunk_orders = [[e // per for e in np.argsort(place_in(o)).tolist()[::per]] for o in (order_a, order_b)]
        extras = assemble([p[:, head_cols : head_cols + LANES] for p in qkv_parts[0]], order_a).astype(F32)
        wo_half = jnp.concatenate(
            [
                assemble([p[:, head_cols + LANES :] for p in qkv_parts[0]], order_a),
                assemble([p[:, head_cols:] for p in qkv_parts[1]], order_b),
            ],
            axis=1,
        )

        hidden = x_two.astype(F32)

        feed_cut = quarter + down_split(quarter)
        feed_cols = (feed_cut, 3 * quarter - feed_cut)
        feed_orders = (order_m[1:], order_w[1:])
        feed_parts = [
            gather_rows([by_x(feed_near[:, lo:hi], feed_far[:, lo:hi])], feed_orders[e][:1])
            for e, (lo, hi) in enumerate(((0, feed_cut), (feed_cut, 3 * quarter)))
        ]

        gain_a, gain_m = extras[:, 0][None, :], extras[:, 1][None, :]
        lane = jnp.arange(BLOCK, dtype=I32)
        n_q = 32 * BLOCK
        own_pos = (own_blocks[:, None] * BLOCK + lane[None, :]).reshape(-1)
        cosine, sine = rope_tables(own_pos)
        gain_qk = jnp.concatenate([gain_q, key_norm_gain])[None, :]

        normed_ab, raw, packed = project(
            core_arr, x_two, gain_a, gain_qk, cosine, sine, qkv_parts, chunk, chunk_orders
        )
        feed_parts = [gather_rows(hold(feed_parts[e], packed), feed_orders[e][1:]) for e in range(2)]
        queries = swap_heads(packed.reshape(16, rows, LANES)).reshape(n_q, LANES)
        own_kv = queries
        gain_mm = dot(dot(jnp.broadcast_to(gain_m, (8, width)).astype(BF), unperm).astype(BF), perm_m)[:1]

        def from_pair(half):
            far = ctx_swap(half, 1)
            return jnp.concatenate([far, core_swap(far)])

        def mine(value):
            return pick(value[:rows], value[rows:])

        def not_mine(value):
            return pick(value[rows:], value[:rows])

        c_far = from_pair(after(mine(c_m), packed))
        if groups > 1:
            own_kv = lax.all_gather(queries, "ctx", axis=0, tiled=True, axis_index_groups=kv_groups)
        other_kv = core_swap(own_kv)
        wo_other = core_swap(wo_half)
        wo_full = by_core(wo_half, wo_other, axis=1)
        head_ids = jnp.arange(width, dtype=I32)
        place = (head_ids // 512).astype(I32)
        head_row = (((head_ids % 512) // HEAD) * 2 + jnp.bitwise_xor(core.astype(I32), place)) * HEAD + head_ids % HEAD
        select = (head_row[:, None] == canon[None, :]).astype(BF)
        wo_sel = dot(select, dot(wo_full, perm_m).astype(BF)).astype(BF)

        extras = after(extras, packed, wo_sel)
        per_chip = extras.reshape(n, 2, owned, LANES)
        block_of = per_chip[:, 0, :2, 2].reshape(-1).astype(I32)
        seq = me % 2
        flags = jnp.where(seq == 0, per_chip[:, 0], per_chip[:, 1])[:, :, 3 : 3 + flag_cols].reshape(slots_n, BLOCK)
        slot_of = (chip_of[:, None] * 2 + jnp.arange(2, dtype=I32)[None, :]).reshape(-1)
        ids = jnp.arange(slots_n, dtype=I32)
        hit = ids[:, None] == block_of[None, :]
        flags_pos = dot(hit.astype(BF), flags.astype(BF))
        kslot = jnp.sum(jnp.where(hit, slot_of[None, :], 0), axis=1)
        pos = jnp.arange(slots_n * BLOCK, dtype=I32).reshape(slots_n, BLOCK)
        begins = jnp.where(flags_pos > 0.5, pos, -1)
        lane = jnp.arange(BLOCK, dtype=I32)
        inside = jnp.max(jnp.where(lane[None, None, :] <= lane[None, :, None], begins[:, None, :], -1), axis=2)
        carried = jnp.max(jnp.where(ids[None, :] < ids[:, None], jnp.max(begins, axis=1)[None, :], -1), axis=1)
        doc_start = jnp.maximum(inside, carried[:, None])
        here = (slot_of // 32) == (me // 16)
        rank = jnp.sum((here[None, :] & (block_of[None, :] < block_of[:, None])).astype(I32), axis=1)
        hit_q = here[None, :] & (rank[None, :] == jnp.arange(32, dtype=I32)[:, None])
        q_block = jnp.sum(jnp.where(hit_q, block_of[None, :], 0), axis=1)
        qslot = jnp.sum(jnp.where(hit_q, slot_of[None, :] - (me // 16) * 32, 0), axis=1)
        q_pos = q_block[:, None] * BLOCK + lane[None, :]
        q_start = jnp.sum(jnp.where((q_block[:, None] == ids[None, :])[:, :, None], doc_start[None], 0), axis=1)
        n_q = 32 * BLOCK
        tile_start = q_start.reshape(n_q // QT, QT)
        tile_pos = q_pos.reshape(n_q // QT, QT)
        low, high = jnp.min(tile_start, axis=1) // KT, jnp.max(tile_pos, axis=1) // KT + 1
        full_low = jnp.minimum((jnp.max(tile_start, axis=1) + KT - 1) // KT, high)
        full_high = jnp.maximum(jnp.minimum((jnp.min(tile_pos, axis=1) + 1) // KT, high), full_low)
        lims = jnp.stack([low, full_low, full_high, high])
        tables = (kslot, qslot, lims, q_pos.reshape(1, n_q), q_start.reshape(1, n_q))

        mixed_packed, mixed, lse = attend(core_arr, tables, queries, own_kv, other_kv)

        attn_own = swap_heads(mixed_packed.reshape(16, BLOCK, LANES)).reshape(16 * BLOCK, LANES)
        residual, normed_m, attn, n_half = leave(core_arr, attn_own, core_swap(attn_own), x_m, wo_sel, gain_mm)

        n_far = from_pair(n_half)
        c_t, c_far_t = turn(c_m, c_far)
        per_chunk = LANES // chip_rows
        feed_chunks = [
            [e // per_chunk for e in np.argsort(place_in(o, order_m)).tolist()[::per_chunk]] for o in (order_m, order_w)
        ]
        *acts_near, out_near, back_near, n_t = feed(normed_m, c_m, feed_parts, LANES, feed_chunks, quarter)
        *acts_far, out_far, back_far, n_far_t = feed(after(n_far, c_t, c_far_t), c_far, feed_parts, LANES, feed_chunks, quarter)
        chip_far = (back_far[:rows].astype(F32) + core_swap(back_far[rows:]).astype(F32)).astype(BF)
        back_pair = ctx_swap(chip_far, 1)
        keep_a, send_a, keep_b, send_b = feed_back(
            (n_t, c_t, n_far_t, c_far_t), (*acts_near, *acts_far), LANES, feed_chunks, feed_cols
        )
        feed_sums = [
            scatter_begin(keep_a, send_a, feed_orders[0][-1]),
            scatter_begin(keep_b, send_b, feed_orders[1][-1]),
        ]
        grad_h, grad_hb, grad_gm, do_packed = enter(
            core_arr, back_near, core_swap(back_near), back_pair, core_swap(back_pair), residual, c_m, gain_mm, wo_sel
        )
        grads_in = swap_heads(do_packed.reshape(16, BLOCK, LANES)).reshape(n_q // 2, LANES)
        attn = after(attn, do_packed)

        out_other = core_swap(jnp.concatenate([not_mine(out_near), out_far[rows:]]).astype(BF)).astype(F32)
        out_pair = ctx_swap((out_far[:rows] + out_other[rows:]).astype(BF), 1).astype(F32)
        layer_rel = mine(residual) + (mine(out_near) + out_other[:rows] + out_pair)
        layer_out = dot(layer_rel.astype(BF), unperm_m).astype(BF)[None]

        grad_wo = out_grad(core_arr, attn, grad_hb, select, unperm_m)
        out_first = grad_wo[:, :out_cols]
        order_rows = np.argsort(place_in(order_b)).tolist()
        out_second = jnp.concatenate(
            [grad_wo[lo * chip_rows : hi * chip_rows, out_cols:] for lo, hi in runs(order_rows)], axis=0
        )

        grads_in = after(grads_in, send_a, send_b)
        dq, keep, send = attend_back(core_arr, tables, queries, own_kv, other_kv, grads_in, mixed, lse)
        feed_sums = [scatter_next(hold(list(feed_sums[e]), send), feed_orders[e][-2]) for e in range(2)]
        grad_kv = keep + core_swap(send).astype(F32)
        if groups > 1:
            grad_kv = lax.psum_scatter(grad_kv, "ctx", scatter_dimension=0, tiled=True, axis_index_groups=kv_groups)
        payload = (dq + grad_kv).astype(BF)
        back = swap_heads(payload.reshape(16, rows, LANES))
        grad_qkv_in, gain_parts = unproject(core_arr, back.reshape(KV_HEADS, 2, rows, LANES), raw, gain_qk, cosine, sine)
        g_first, g_second = grad_qkv_in[:, : width // 2], grad_qkv_in[:, width // 2 :]

        def halves(value):
            half = value.shape[0] // 2
            return value[:half], value[half:]

        sum_first = jnp.concatenate([dot(normed_ab, g_first, TN).astype(BF), out_first], axis=1)
        sum_second = jnp.concatenate([dot(columns_in(normed_ab, order_b), g_second, TN).astype(BF), out_second], axis=1)
        level_holds = {}
        if n == 16:
            sum_first = scatter_begin(*halves(sum_first), "y")
            sum_second = scatter_begin(*halves(sum_second), "x")
            level_holds[3] = sum_first[1], sum_second[1]
            sum_first = scatter_next(sum_first, "x")
            sum_second = scatter_next(sum_second, "y")
            level_holds[4] = sum_first[1], sum_second[1]
            sums = jnp.concatenate([scatter_end(sum_first), scatter_end(sum_second)], axis=1)
            sums = scatter_whole(sums, "qp")
        else:
            sums = jnp.concatenate([scatter_whole(sum_first, order_a), scatter_whole(sum_second, order_b)], axis=1)
        cut_cols = head_cols + out_cols
        part_qkv = jnp.concatenate([sums[:, :head_cols], sums[:, cut_cols : cut_cols + head_cols]], axis=1)
        part_out = jnp.concatenate([sums[:, head_cols:cut_cols], sums[:, cut_cols + head_cols :]], axis=1)
        w_first = assemble([p[:, : width // 2] for p in qkv_parts[0]], order_a)
        w_second = assemble([p[:, : width // 2] for p in qkv_parts[1]], order_b)
        n1_part = dot(g_first, w_first, NT) + dot(g_second, w_second, NT)
        n1_other = core_swap(pick(n1_part[rows:], n1_part[:rows]))
        grad_n1 = pick(n1_part[:rows], n1_part[rows:]) + n1_other

        x_mine = mine(hidden)
        _, inv_a = rms(x_mine, gain_a)
        moved_a, grad_ga = rms_back(x_mine, inv_a, gain_a, grad_n1)

        def unspread(value, matrix):
            high = value.astype(BF)
            low = (value - high.astype(F32)).astype(BF)
            return dot(high, matrix) + dot(low, matrix)

        grad_input = (unspread(mine(grad_h), unperm_m) + unspread(moved_a, unperm))[None]

        def exact(vector, matrix):
            return lax.dot_general(
                vector, matrix.astype(F32), NN, precision=lax.Precision.HIGHEST, preferred_element_type=F32
            )

        vectors = jnp.concatenate([exact(grad_ga[None], unperm), exact(jnp.where(first, grad_gm, 0.0), unperm_m)])
        feed_levels = len(order_m)
        for level in range(3, feed_levels):
            feed_sums = [hold(list(v), *level_holds.get(level, ())) for v in feed_sums]
            feed_sums = [scatter_next(feed_sums[e], feed_orders[e][-level]) for e in range(2)]
        feed_sums = [scatter_end(hold(list(v), vectors)) for v in feed_sums]
        feed_near = jnp.concatenate([pick_x(v[:chip_rows], v[chip_rows:]) for v in feed_sums], axis=1)
        feed_far = jnp.concatenate([pick_x(v[chip_rows:], v[:chip_rows]) for v in feed_sums], axis=1)
        feed_far = ctx_swap(feed_far.astype(BF), 1).astype(F32)
        feed_zero, feed_one = pick_x(feed_near, feed_far), pick_x(feed_far, feed_near)
        heads_gain = jnp.sum(gain_parts[:, 0], axis=0)
        chip_gains = jnp.transpose(vectors.reshape(2, n, chip_rows), (1, 0, 2)).reshape(n, 2 * chip_rows)
        small = jnp.concatenate([chip_gains, jnp.broadcast_to(heads_gain[None], (n, LANES))], axis=1)
        small = jnp.pad(small, ((0, 0), (0, 2 * LANES - small.shape[1]))).reshape(n, 1, 2 * LANES)
        small = lax.all_to_all(jnp.broadcast_to(small, (n, 8, 2 * LANES)), "ctx", 0, 0, tiled=True)
        small = jnp.sum(small[:, 0], axis=0)
        small = small + core_swap(small)
        gains = small[: 2 * chip_rows].reshape(2, chip_rows)
        gains = pick(gains[:, :owned], gains[:, owned:])
        head_gains = small[2 * chip_rows : 2 * chip_rows + LANES]

        def theirs(parts):
            return jnp.concatenate([pick(p[owned:], p[:owned]) for p in parts], axis=1)

        grad_gate, grad_up, grad_down = deliver(
            core_arr, feed_zero, feed_one, core_swap(theirs([feed_zero, feed_one]))
        )
        grad_wout, grad_query, grad_key, grad_value = deliver_heads(
            core_arr, part_qkv, part_out, core_swap(theirs([part_qkv, part_out]))
        )
        return (
            layer_out,
            grad_input,
            grad_query,
            grad_key,
            grad_value,
            grad_wout,
            grad_gate,
            grad_up,
            grad_down,
            gains[0],
            gains[1],
            head_gains[:HEAD],
            head_gains[HEAD:],
        )

    return shards


def solution(mesh):
    seq = P("wt", "ctx", None)
    weight = P(("ctx", "wt"), None)
    vector = P(("ctx", "wt"))
    return jax.shard_map(
        make_shards(mesh.shape["ctx"]),
        mesh=mesh,
        in_specs=(seq, P("ctx", None), P("wt", "ctx")) + (weight,) * 7 + (vector, vector, P(), P(), seq),
        out_specs=(seq, seq) + (weight,) * 7 + (vector, vector, P(), P()),
        check_vma=False,
    )
```
